512 devices in a mesh: gx: 32 (over z, core), gy: 16 (over x, y).
Axes of the slice: x: 4, y: 4, z: 16, core: 2. Of those that a mesh axis runs over, the one named last changes fastest.
Arguments:
- source: float32 [128, 512, 128], P('gx', 'gy'), may hold values from -7 to 7
- beta: float32 [128, 512, 128], P('gx', 'gy'), may hold values from 0.5 to 4
- shift_field: float32 [128, 512, 128], P('gx', 'gy'), may hold values from 0.001 to 0.1
Outputs:
- correction: float32 [128, 512, 128], P('gx', 'gy')
The draws below stay inside these ranges and needn't reach their ends.
All inputs are finite; a program needn't handle non-finite values.
Results may differ from the reference program's by a relative error of at most 0.0001.
Values sent between devices are 32-bit elements; how exact they have to be, the bound alone decides.
A program may use at most 64 MiB of HBM per device.

```python
import math
import jax
import jax.numpy as jnp

NZ = 128
ITERS = 6
NX = 128
NY = 512


def positions(count):
    return (jnp.arange(count, dtype=jnp.float32) + 0.5) / count


def smooth_field(key, count, lowest, highest):
    across = positions(NX)
    along = positions(NY)
    depth = positions(NZ)
    total = jnp.zeros((NX, NY, NZ), jnp.float32)
    for index in range(count):
        keys = jax.random.split(jax.random.fold_in(key, index), 4)
        frequency = jax.random.randint(keys[0], (3,), lowest, highest).astype(jnp.float32)
        phase = jax.random.uniform(keys[1], (3,), jnp.float32, -math.pi, math.pi)
        strength = jax.random.uniform(keys[2], (), jnp.float32, 0.5, 1.0)
        strength = jnp.where(jax.random.bernoulli(keys[3]), strength, -strength)
        first = jnp.sin(math.pi * frequency[0] * across + phase[0])
        second = jnp.sin(math.pi * frequency[1] * along + phase[1])
        third = jnp.cos(0.5 * math.pi * frequency[2] * depth + phase[2])
        total = total + strength * first[:, None, None] * second[None, :, None] * third[None, None, :]
    return total / count


def draw_source(key, part):
    key = jax.random.fold_in(key, 11)
    noise_key, smooth_key = jax.random.split(key)
    smooth = smooth_field(smooth_key, 4, 1, 4)
    noise = jax.random.truncated_normal(noise_key, -6.0, 6.0, (NX, NY, NZ), jnp.float32)
    return noise + 0.03 * smooth


def draw_shift_field(key, part):
    key = jax.random.fold_in(key, 23)
    cell_key, region_key = jax.random.split(key)
    level = jax.random.uniform(cell_key, (NX, NY, NZ), jnp.float32, math.log(0.003), math.log(0.03))
    region = smooth_field(region_key, 3, 1, 5)
    return jnp.exp(level + 0.7 * region)


def level_of(rng, dims, cuts, smallest, high):
    def one(position, blocks):
        heights = jax.random.uniform(jax.random.fold_in(jax.random.fold_in(rng, 6), position), (blocks,), jnp.float32, smallest / len(cuts), high / len(cuts))
        return jnp.repeat(jnp.exp(heights), dims[position] // blocks).reshape((-1,) + (1,) * (len(dims) - position - 1))

    loudness = one(*cuts[0])
    for cut in cuts[1:]:
        loudness = loudness * one(*cut)
    return loudness


def setup_inputs(seed: int = 0) -> dict:
    splits = jax.random.split(jax.random.key(seed), 4)
    return {
        "source": draw_source(jax.random.fold_in(splits[3], 71), 0),
        "beta": jnp.clip(jnp.exp(math.log(4.0) - 2.0794415 * jax.random.uniform(splits[1], (NX, NY, NZ), jnp.float32) ** level_of(splits[1], (NX, NY, NZ), ((0, 32), (1, 16)), -0.2, 0.2)), 0.5, 4.0),
        "shift_field": draw_shift_field(jax.random.fold_in(splits[3], 71), 0),
    }


FIRST = 1.0 / 1.2
CARRY = 2.0 / 7.0
SECOND = 0.75 / 0.7
VERTICAL = 1.0 / 16.0
PLANE_SCALES = (1.0, 0.25, 0.0625)


def weights_of(beta_ext, plane_scale):
    centre = beta_ext[1:-1, 1:-1, :]
    z_padded = jnp.pad(centre, ((0, 0), (0, 0), (1, 1)))
    plane = 0.5 * plane_scale
    upright = 0.5 * VERTICAL
    return (plane * (centre + beta_ext[2:, 1:-1, :]), plane * (centre + beta_ext[:-2, 1:-1, :]),
            plane * (centre + beta_ext[1:-1, 2:, :]), plane * (centre + beta_ext[1:-1, :-2, :]),
            upright * (centre + z_padded[:, :, 2:]), upright * (centre + z_padded[:, :, :-2]))


def operate(field_ext, shift_term, weights):
    centre = field_ext[1:-1, 1:-1, :]
    z_padded = jnp.pad(centre, ((0, 0), (0, 0), (1, 1)))
    result = shift_term * centre
    result = result + weights[0] * (centre - field_ext[2:, 1:-1, :])
    result = result + weights[1] * (centre - field_ext[:-2, 1:-1, :])
    result = result + weights[2] * (centre - field_ext[1:-1, 2:, :])
    result = result + weights[3] * (centre - field_ext[1:-1, :-2, :])
    result = result + weights[4] * (centre - z_padded[:, :, 2:])
    result = result + weights[5] * (centre - z_padded[:, :, :-2])
    return result


def diagonal_of(shift_term, weights):
    return shift_term + weights[0] + weights[1] + weights[2] + weights[3] + weights[4] + weights[5]


def coarsen(field):
    height, width, depth = field.shape
    return field.reshape(height // 2, 2, width // 2, 2, depth).mean(axis=(1, 3))


def prolong(field):
    return jnp.repeat(jnp.repeat(field, 2, axis=0), 2, axis=1)


def pad_plane(field):
    return jnp.pad(field, ((1, 1), (1, 1), (0, 0)))


def reference(source, beta, shift_field):
    betas = [beta]
    shifts = [shift_field]
    for level in range(2):
        betas.append(coarsen(betas[-1]))
        shifts.append(coarsen(shifts[-1]))
    weights = [weights_of(pad_plane(betas[k]), PLANE_SCALES[k]) for k in range(3)]
    diagonals = [diagonal_of(shifts[k], weights[k]) for k in range(3)]

    def apply_level(field, level):
        return operate(pad_plane(field), shifts[level], weights[level])

    def presmooth(rhs, level):
        first_step = FIRST * rhs / diagonals[level]
        second_resid = rhs - apply_level(first_step, level)
        return first_step + (CARRY * first_step + SECOND * second_resid / diagonals[level])

    def postsmooth(iterate, rhs, level):
        first_resid = rhs - apply_level(iterate, level)
        first_step = FIRST * first_resid / diagonals[level]
        moved = iterate + first_step
        second_resid = rhs - apply_level(moved, level)
        return moved + (CARRY * first_step + SECOND * second_resid / diagonals[level])

    fine_iter = presmooth(source, 0)
    middle_rhs = coarsen(source - apply_level(fine_iter, 0))
    middle_iter = presmooth(middle_rhs, 1)
    coarse_rhs = coarsen(middle_rhs - apply_level(middle_iter, 1))

    coarse_sol = jnp.zeros_like(coarse_rhs)
    residual = coarse_rhs
    direction = coarse_rhs
    norm_now = jnp.sum(residual * residual)
    for turn_index in range(ITERS):
        image = apply_level(direction, 2)
        alpha = norm_now / jnp.sum(direction * image)
        coarse_sol = coarse_sol + alpha * direction
        residual = residual - alpha * image
        norm_next = jnp.sum(residual * residual)
        direction = residual + (norm_next / norm_now) * direction
        norm_now = norm_next

    middle_iter = postsmooth(middle_iter + prolong(coarse_sol), middle_rhs, 1)
    return postsmooth(fine_iter + prolong(middle_iter), source, 0)
```

```python
import functools

import jax
import jax.numpy as jnp
from jax import lax
from jax.experimental import pallas as pl
from jax.experimental.pallas import tpu as pltpu
from jax.sharding import PartitionSpec as P

MESH = pl.DeviceIdType.MESH
ITERS = 6
FIRST = 1.0 / 1.2
CARRY = 2.0 / 7.0
SECOND = 0.75 / 0.7
KEEP = 1.0 + CARRY + SECOND * (1.0 - FIRST) / FIRST
VERTICAL = 1.0 / 16.0
PLANE_SCALES = (1.0, 0.25, 0.0625)
EDGE = 16
SPLIT = 4097.0

PAIRS = [(i, j) for i in range(ITERS) for j in range(i, ITERS)] + [(ITERS - 1, ITERS)]
SLOT = {pair: n for n, pair in enumerate(PAIRS)}
ROWS = 24


def two_sum(a, b):
    s = a + b
    t = s - a
    return s, (a - (s - t)) + (b - t)


def fast_two_sum(a, b):
    s = a + b
    return s, b - (s - a)


def halves(a):
    t = SPLIT * a
    high = t - (t - a)
    return high, a - high


def two_prod(a, b, a_halves=None, b_halves=None):
    ah, al = halves(a) if a_halves is None else a_halves
    bh, bl = halves(b) if b_halves is None else b_halves
    p = a * b
    return p, ((ah * bh - p) + ah * bl + al * bh) + al * bl


def dd_add(a, b):
    s, t = two_sum(a[0], b[0])
    return fast_two_sum(s, t + (a[1] + b[1]))


def dd_mul(a, b):
    p, t = two_prod(a[0], b[0])
    return fast_two_sum(p, t + (a[0] * b[1] + a[1] * b[0]))


def dd_neg(a):
    return -a[0], -a[1]


def dd_half(a):
    return 0.5 * a[0], 0.5 * a[1]


def dd_div(a, b):
    q = a[0] / b[0]
    p, t = two_prod(q, b[0])
    rest = ((a[0] - p) - t) + (a[1] - q * b[1])
    return fast_two_sum(q, rest / b[0])


def dd_dot(us, ws):
    terms = [dd_mul(u, w) for u, w in zip(us, ws)]
    while len(terms) > 1:
        terms = [dd_add(terms[i], terms[i + 1]) if i + 1 < len(terms) else terms[i] for i in range(0, len(terms), 2)]
    return terms[0]


def gradient_coefficients(gram):
    one = (jnp.ones_like(gram(0, 0)[0]), jnp.zeros_like(gram(0, 0)[0]))
    residual, direction, answer = [one], [one], [None] * ITERS
    norm_now = gram(0, 0)
    for turn in range(ITERS):
        image = []
        for k in range(turn + 2):
            terms = [direction[k]] if k <= turn else []
            if k >= 1:
                terms.append(direction[0] if k == 1 else dd_half(direction[k - 1]))
            if k + 1 <= turn:
                terms.append(dd_half(direction[k + 1]))
            total = terms[0]
            for term in terms[1:]:
                total = dd_add(total, term)
            image.append(total)
        along = dd_mul(direction[turn], dd_dot(image, [gram(i, turn) for i in range(turn + 2)]))
        alpha = dd_div(norm_now, along)
        for k in range(turn + 1):
            step = dd_mul(alpha, direction[k])
            answer[k] = step if answer[k] is None else dd_add(answer[k], step)
        if turn + 1 == ITERS:
            break
        less = dd_neg(alpha)
        steps = [dd_mul(less, value) for value in image]
        residual = [dd_add(residual[k], steps[k]) if k <= turn else steps[k] for k in range(turn + 2)]
        norm_next = dd_mul(residual[turn + 1], dd_dot(residual, [gram(i, turn + 1) for i in range(turn + 2)]))
        beta = dd_div(norm_next, norm_now)
        norm_now = norm_next
        direction = [dd_add(residual[k], dd_mul(beta, direction[k])) if k <= turn else residual[k] for k in range(turn + 2)]
    return [value[0] + value[1] for value in answer]


def loop(low, high, body):
    def step(p, carry):
        body(p)
        return carry

    lax.fori_loop(low, high, step, 0)


def lane_of(shape):
    return lax.broadcasted_iota(jnp.int32, shape, len(shape) - 1)


def box(reach, width):
    return [(i, j) for i in range(-reach, reach + 1) for j in range(-width, width + 1) if (i, j) != (0, 0)]


def ring(count, size):
    far = sorted(range(1, count), key=lambda d: -min(d, count - d))
    return [((d, 0) if size else (0, d)) for d in far]


def windows(offsets, count, rows, first, reach):
    out = []
    for dx, dy in sorted(offsets, key=lambda o: -abs(o[0]) - abs(o[1])):
        if dx == 0:
            start, planes, target = 0, count, first
        elif dx > 0:
            start = max(0, dx * count - reach)
            planes, target = count - start, first - dx * count + start
        else:
            start, planes = 0, min(count, reach + (dx + 1) * count)
            target = first - dx * count
        row, high, to = (EDGE, rows, EDGE) if dy == 0 else (EDGE + rows - 8, 8, EDGE - 8) if dy > 0 else (EDGE, 8, EDGE + rows)
        out.append((dx, dy, first + start, target, planes, row, to, high))
    return out


def tiles_of(geometry, fields):
    return sum(fields * w[4] * w[7] // 8 for w in geometry)


def kernel(
    counts, source, beta, shift, out,
    fields, coarse2, coarse3, rhs2, rhs3,
    masked1, wx1, wy1, wz1, diag1, inv1, step1, near1, iter1, start1,
    masked2, wx2, wy2, wz2, diag2, inv2, step2, near2, iter2, start2, sum2,
    masked3, wx3, wy3, wz3, own3, inside3, basis, sol3,
    pair_high, pair_low, bound_y, bound_x, gram_y, gram_x, scalars, dummy,
    load_sem, send_sem, recv_sem,
):
    nx, ny = counts
    gx, gy = lax.axis_index("gx"), lax.axis_index("gy")

    def device(dx, dy):
        return lax.rem(gx + (dx + nx), nx), lax.rem(gy + (dy + ny), ny)

    near, wide, far = box(1, 1), box(2, 1), box(7, 1)
    over_y, over_x = ring(ny, 0), ring(nx, 1)

    loads = [
        pltpu.make_async_copy(ref, fields.at[n, pl.ds(3, 4), pl.ds(EDGE, 32)], load_sem.at[n])
        for n, ref in enumerate((source, shift, beta))
    ]
    for load in loads:
        load.start()

    partners = sorted({((dx + nx) % nx, (dy + ny) % ny) for dx, dy in far + over_y + over_x})
    barrier = pltpu.get_barrier_semaphore()
    for dx, dy in partners:
        pl.semaphore_signal(barrier, 1, device_id=device(-dx, -dy), device_id_type=MESH)

    def send(phase, ref, geometry, stacked):
        for dx, dy, plane, target, planes, row, to, high in geometry:
            here, there = (pl.ds(plane, planes), pl.ds(row, high)), (pl.ds(target, planes), pl.ds(to, high))
            if stacked:
                here, there = (slice(None), *here), (slice(None), *there)
            pltpu.make_async_remote_copy(
                src_ref=ref.at[here], dst_ref=ref.at[there], send_sem=send_sem.at[phase], recv_sem=recv_sem.at[phase],
                device_id=device(dx, dy), device_id_type=MESH,
            ).start()

    def wait(sems, phase, tiles):
        part = dummy.at[pl.ds(0, tiles)]
        pltpu.make_async_copy(part, part, sems.at[phase]).wait()

    def spread(phase, ref, offsets):
        for dx, dy in offsets:
            pltpu.make_async_remote_copy(
                src_ref=ref.at[0], dst_ref=ref.at[max(dx, dy)], send_sem=send_sem.at[phase], recv_sem=recv_sem.at[phase],
                device_id=device(dx, dy), device_id_type=MESH,
            ).start()

    def wait_spread(sems, phase, ref, count):
        part = ref.at[pl.ds(1, count - 1)]
        pltpu.make_async_copy(part, part, sems.at[phase]).wait()

    def inside(p, rows, low, first, count, own_planes, own_rows):
        plane = gx * own_planes + (p - first)
        row = gy * own_rows + (low - EDGE) + lax.broadcasted_iota(jnp.int32, (rows, 128), 0)
        fits = jnp.logical_and(plane >= 0, plane < nx * own_planes).astype(jnp.int32)
        return jnp.where(jnp.logical_and(row >= 0, row < ny * own_rows), fits, 0) > 0

    def off(v, wx, wy, wz, p, low, rows):
        here = v[p, pl.ds(low, rows), :]
        up = wz[p, pl.ds(low, rows), :]
        total = wx[p, pl.ds(low, rows), :] * v[p + 1, pl.ds(low, rows), :]
        total = total + wx[p - 1, pl.ds(low, rows), :] * v[p - 1, pl.ds(low, rows), :]
        total = total + wy[p, pl.ds(low, rows), :] * v[p, pl.ds(low + 1, rows), :]
        total = total + wy[p, pl.ds(low - 1, rows), :] * v[p, pl.ds(low - 1, rows), :]
        total = total + up * pltpu.roll(here, 127, 1)
        return total + pltpu.roll(up * here, 1, 1)

    def weights(b, p, low, rows, plane, upright):
        here = b[p, pl.ds(low, rows), :]
        lane = lane_of((rows, 128))
        wxp = plane * (here + b[p + 1, pl.ds(low, rows), :])
        wxm = plane * (here + b[p - 1, pl.ds(low, rows), :])
        wyp = plane * (here + b[p, pl.ds(low + 1, rows), :])
        wym = plane * (here + b[p, pl.ds(low - 1, rows), :])
        wzp = upright * (here + jnp.where(lane < 127, pltpu.roll(here, 127, 1), 0.0))
        wzm = upright * (here + jnp.where(lane > 0, pltpu.roll(here, 1, 1), 0.0))
        return wxp, wyp, jnp.where(lane < 127, wzp, 0.0), wxp + wxm + wyp + wym + wzp + wzm

    def prepare(refs, pair, rows, first, own, scale):
        masked, wx, wy, wz, diag, inv = refs
        shift_at, beta_at = pair

        def clean(p):
            ok = inside(p, rows, 8, first, 10, own[0], own[1])
            masked[p, pl.ds(8, rows), :] = jnp.where(ok, beta_at(p), 0.0)

        def fill(p):
            wxp, wyp, wzp, total = weights(masked, p, 8, rows, 0.5 * scale, 0.5 * VERTICAL)
            total = total + shift_at(p)
            wx[p, pl.ds(8, rows), :] = wxp
            wy[p, pl.ds(8, rows), :] = wyp
            wz[p, pl.ds(8, rows), :] = wzp
            diag[p, pl.ds(8, rows), :] = total
            ok = inside(p, rows, 8, first, 10, own[0], own[1])
            inv[p, pl.ds(8, rows), :] = jnp.where(ok, 1.0 / total, 0.0)

        loop(0, 10, clean)
        loop(1, 9, fill)

    def coarsen_rows(ref, at, rows):
        even = ref[at, pl.ds(EDGE, rows // 2, stride=2), :]
        return 0.25 * (even + ref[at, pl.ds(EDGE + 1, rows // 2, stride=2), :])

    for load in loads:
        load.wait()
    for n, level in ((0, 1), (1, 2)):
        for q in range(2):
            both = fields[1 + n, 3 + 2 * q, pl.ds(EDGE, 32), :] + fields[1 + n, 4 + 2 * q, pl.ds(EDGE, 32), :]
            near1[q, pl.ds(EDGE, 32), :] = both
            coarse2[n, 4 + q, pl.ds(EDGE, 16), :] = coarsen_rows(near1, q, 32)
        near2[0, pl.ds(EDGE, 16), :] = coarse2[n, 4, pl.ds(EDGE, 16), :] + coarse2[n, 5, pl.ds(EDGE, 16), :]
        coarse3[n, 7, pl.ds(EDGE, 8), :] = coarsen_rows(near2, 0, 16)
    shift_own, beta_own = coarse3[0, 7, pl.ds(EDGE, 8), :], coarse3[1, 7, pl.ds(EDGE, 8), :]
    around = pltpu.roll(beta_own, 1, 0) + pltpu.roll(beta_own, 7, 0) + pltpu.roll(beta_own, 1, 1) + pltpu.roll(beta_own, 127, 1)
    bound = jnp.max(shift_own + PLANE_SCALES[2] * (6.0 * beta_own + 1.5 * around))
    bound_y[0] = jnp.full((1, 128), bound, jnp.float32)

    pl.semaphore_wait(barrier, len(partners))
    geo_fields = windows(near, 4, 32, 3, 3)
    geo_coarse2 = windows(wide, 2, 16, 4, 4)
    geo_coarse3 = windows(far, 1, 8, 7, 7)
    geo_iter1 = windows(near, 4, 32, 3, 2)
    geo_rhs2 = windows(near, 2, 16, 4, 2)
    send(0, fields, geo_fields, True)
    send(1, coarse2, geo_coarse2, True)
    spread(7, bound_y, over_y)
    send(2, coarse3, geo_coarse3, True)

    wait(recv_sem, 0, tiles_of(geo_fields, 3))
    level1 = (masked1, wx1, wy1, wz1, diag1, inv1)
    prepare(
        level1, (lambda p: fields[1, p, pl.ds(8, 48), :], lambda p: fields[2, p, pl.ds(8, 48), :]), 48, 3, (4, 32), PLANE_SCALES[0]
    )

    def first_step(step, inv, value, rows):
        def body(p):
            step[p, pl.ds(8, rows), :] = FIRST * value(p) * inv[p, pl.ds(8, rows), :]

        return body

    def smooth(step, wx, wy, wz, inv, p, low, rows):
        part = off(step, wx, wy, wz, p, low, rows)
        return KEEP * step[p, pl.ds(low, rows), :] + SECOND * inv[p, pl.ds(low, rows), :] * part

    loop(1, 9, first_step(step1, inv1, lambda p: fields[0, p, pl.ds(8, 48), :], 48))

    def presmooth1(p):
        near1[p, pl.ds(8, 48), :] = smooth(step1, wx1, wy1, wz1, inv1, p, 8, 48)

    loop(2, 8, presmooth1)

    def residual(f, v, level, p, low, rows):
        _, wx, wy, wz, diag, _ = level
        value = f(p, low, rows) - diag[p, pl.ds(low, rows), :] * v[p, pl.ds(low, rows), :]
        return value + off(v, wx, wy, wz, p, low, rows)

    def source_at(p, low, rows):
        return fields[0, p, pl.ds(low, rows), :]

    def rhs2_at(p, low, rows):
        return rhs2[p, pl.ds(low, rows), :]

    def restrict1(q):
        both = residual(source_at, near1, level1, 3 + 2 * q, EDGE, 32) + residual(source_at, near1, level1, 4 + 2 * q, EDGE, 32)
        start1[q, pl.ds(EDGE, 32), :] = both
        rhs2[4 + q, pl.ds(EDGE, 16), :] = coarsen_rows(start1, q, 32)

    loop(0, 2, restrict1)
    send(3, rhs2, geo_rhs2, False)

    def keep1(p):
        iter1[p, pl.ds(EDGE, 32), :] = near1[p, pl.ds(EDGE, 32), :]

    loop(3, 7, keep1)
    send(4, iter1, geo_iter1, False)

    wait(recv_sem, 1, tiles_of(geo_coarse2, 2))
    level2 = (masked2, wx2, wy2, wz2, diag2, inv2)
    prepare(
        level2, (lambda p: coarse2[0, p, pl.ds(8, 32), :], lambda p: coarse2[1, p, pl.ds(8, 32), :]), 32, 4, (2, 16), PLANE_SCALES[1]
    )
    wait_spread(recv_sem, 7, bound_y, ny)
    bound_x[0] = functools.reduce(jnp.maximum, [bound_y[n] for n in range(ny)])
    spread(8, bound_x, over_x)

    wait(recv_sem, 3, tiles_of(geo_rhs2, 1))
    loop(2, 8, first_step(step2, inv2, lambda p: rhs2_at(p, 8, 32), 32))

    def presmooth2(p):
        near2[p, pl.ds(8, 32), :] = smooth(step2, wx2, wy2, wz2, inv2, p, 8, 32)

    loop(3, 7, presmooth2)
    both = residual(rhs2_at, near2, level2, 4, EDGE, 16) + residual(rhs2_at, near2, level2, 5, EDGE, 16)
    start2[0, pl.ds(EDGE, 16), :] = both
    rhs3[7, pl.ds(EDGE, 8), :] = coarsen_rows(start2, 0, 16)
    send(5, rhs3, geo_coarse3, False)
    for p in (4, 5):
        iter2[p, pl.ds(EDGE, 16), :] = near2[p, pl.ds(EDGE, 16), :]
    send(6, iter2, geo_coarse2, False)

    wait(recv_sem, 2, tiles_of(geo_coarse3, 2))
    wait_spread(recv_sem, 8, bound_x, nx)
    scale = 2.0 / functools.reduce(jnp.maximum, [bound_x[n] for n in range(nx)])

    def clean3(p):
        ok = inside(p, 24, 8, 7, 15, 1, 8)
        masked3[p, pl.ds(8, 24), :] = jnp.where(ok, coarse3[1, p, pl.ds(8, 24), :], 0.0)

    loop(0, 15, clean3)
    wx3[0, pl.ds(8, 24), :] = (PLANE_SCALES[2] * scale) * (masked3[0, pl.ds(8, 24), :] + masked3[1, pl.ds(8, 24), :])

    def fill3(p):
        wxp, wyp, wzp, total = weights(masked3, p, 8, 24, PLANE_SCALES[2] * scale, VERTICAL * scale)
        total = total + 2.0 * scale * coarse3[0, p, pl.ds(8, 24), :]
        wx3[p, pl.ds(8, 24), :] = wxp
        wy3[p, pl.ds(8, 24), :] = wyp
        wz3[p, pl.ds(8, 24), :] = wzp
        ok = inside(p, 24, 8, 7, 15, 1, 8)
        own3[p, pl.ds(8, 24), :] = jnp.where(ok, total - 2.0, 0.0)
        inside3[p, pl.ds(8, 24), :] = jnp.where(ok, 1.0, 0.0)

    loop(1, 14, fill3)
    wait(recv_sem, 5, tiles_of(geo_coarse3, 1))

    def begin3(p):
        ok = inside(p, 24, 8, 7, 15, 1, 8)
        basis[0, p, pl.ds(8, 24), :] = jnp.where(ok, rhs3[p, pl.ds(8, 24), :], 0.0)

    loop(0, 15, begin3)

    def doubled(v, p, low, rows):
        value = own3[p, pl.ds(low, rows), :] * v[p, pl.ds(low, rows), :]
        return value - inside3[p, pl.ds(low, rows), :] * off(v, wx3, wy3, wz3, p, low, rows)

    for k in range(ITERS):
        low, rows, reach = (8, 24, 6 - k) if k < ITERS - 1 else (EDGE, 8, 0)

        def advance(p, k=k, low=low, rows=rows):
            value = doubled(basis.at[k], p, low, rows)
            value = 0.5 * value if k == 0 else value - basis[k - 1, p, pl.ds(low, rows), :]
            basis[k + 1, p, pl.ds(low, rows), :] = value

        loop(7 - reach, 8 + reach, advance)

    own = [basis[k, 7, pl.ds(EDGE, 8), :] for k in range(ITERS + 1)]
    parts = [halves(v) for v in own]
    for n, (i, j) in enumerate(PAIRS):
        high, low = two_prod(own[i], own[j], parts[i], parts[j])
        pair_high[pl.ds(8 * n, 8), :] = high
        pair_low[pl.ds(8 * n, 8), :] = low
    for n in range(len(PAIRS), ROWS):
        pair_high[pl.ds(8 * n, 8), :] = jnp.zeros((8, 128), jnp.float32)
        pair_low[pl.ds(8 * n, 8), :] = jnp.zeros((8, 128), jnp.float32)

    def merge(a, b):
        s, t = two_sum(a[0], b[0])
        return s, t + (a[1] + b[1])

    def tree(terms):
        while len(terms) > 1:
            terms = [merge(terms[i], terms[i + 1]) if i + 1 < len(terms) else terms[i] for i in range(0, len(terms), 2)]
        return terms[0]

    sums = tree([(pair_high[pl.ds(s, ROWS, stride=8), :], pair_low[pl.ds(s, ROWS, stride=8), :]) for s in range(8)])
    for d in (64, 32, 16, 8, 4, 2, 1):
        sums = merge(sums, (pltpu.roll(sums[0], d, 1), pltpu.roll(sums[1], d, 1)))
    lane, row = lane_of((ROWS, 128)), lax.broadcasted_iota(jnp.int32, (ROWS, 128), 0)
    line = jnp.where(lane == row, sums[0], jnp.where(lane == row + 64, sums[1], 0.0))
    gram_y[0] = jnp.sum(line, axis=0, keepdims=True)

    def total_of(ref, count):
        zero = jnp.zeros((1, 128), jnp.float32)
        s, t = tree([(ref[n], zero) for n in range(count)])
        return s + jnp.where(lane_of((1, 128)) >= 64, pltpu.roll(t, 64, 1), 0.0)

    spread(9, gram_y, over_y)
    wait_spread(recv_sem, 9, gram_y, ny)
    gram_x[0] = total_of(gram_y, ny)
    spread(10, gram_x, over_x)
    wait(recv_sem, 4, tiles_of(geo_iter1, 1))
    wait(recv_sem, 6, tiles_of(geo_coarse2, 1))
    wait_spread(recv_sem, 10, gram_x, nx)
    entries = jnp.broadcast_to(total_of(gram_x, nx), (2 * ROWS, 128))
    lane, row = lane_of((2 * ROWS, 128)), lax.broadcasted_iota(jnp.int32, (2 * ROWS, 128), 0)
    place = jnp.where(row < ROWS, row, row + (64 - ROWS))
    column = jnp.sum(jnp.where(lane == place, entries, 0.0), axis=1, keepdims=True)
    scalars[...] = jnp.broadcast_to(column, (2 * ROWS, 128))

    def gram(i, j):
        n = SLOT[(min(i, j), max(i, j))]
        return scalars[pl.ds(n, 1), :], scalars[pl.ds(ROWS + n, 1), :]

    answer = [value * scale for value in gradient_coefficients(gram)]

    for n in range(5):
        p = 5 + n
        total = answer[0] * basis[0, p, pl.ds(8, 24), :]
        for k in range(1, ITERS):
            total = total + answer[k] * basis[k, p, pl.ds(8, 24), :]
        sol3[n, pl.ds(8, 24), :] = total

    def prolong2(p):
        value = sol3[p // 2, pl.ds(12, 16), :]
        start2[p, pl.ds(8, 16, stride=2), :] = value
        start2[p, pl.ds(9, 16, stride=2), :] = value
        ok = inside(p, 32, 8, 4, 10, 2, 16)
        start2[p, pl.ds(8, 32), :] = jnp.where(ok, start2[p, pl.ds(8, 32), :] + iter2[p, pl.ds(8, 32), :], 0.0)

    loop(1, 9, prolong2)
    loop(2, 8, first_step(step2, inv2, lambda p: residual(rhs2_at, start2, level2, p, 8, 32), 32))

    def post2(p):
        sum2[p, pl.ds(8, 32), :] = start2[p, pl.ds(8, 32), :] + smooth(step2, wx2, wy2, wz2, inv2, p, 8, 32)

    loop(3, 7, post2)

    def prolong1(p):
        value = sum2[(p + 5) // 2, pl.ds(12, 24), :]
        start1[p, pl.ds(8, 24, stride=2), :] = value
        start1[p, pl.ds(9, 24, stride=2), :] = value
        ok = inside(p, 48, 8, 3, 10, 4, 32)
        start1[p, pl.ds(8, 48), :] = jnp.where(ok, start1[p, pl.ds(8, 48), :] + iter1[p, pl.ds(8, 48), :], 0.0)

    loop(1, 9, prolong1)
    loop(2, 8, first_step(step1, inv1, lambda p: residual(source_at, start1, level1, p, 8, 48), 48))

    def post1(p):
        out[p - 3] = start1[p, pl.ds(EDGE, 32), :] + smooth(step1, wx1, wy1, wz1, inv1, p, EDGE, 32)

    loop(3, 7, post1)

    wait(send_sem, 0, tiles_of(geo_fields, 3))
    wait(send_sem, 1, tiles_of(geo_coarse2, 2))
    wait(send_sem, 2, tiles_of(geo_coarse3, 2))
    wait(send_sem, 3, tiles_of(geo_rhs2, 1))
    wait(send_sem, 4, tiles_of(geo_iter1, 1))
    wait(send_sem, 5, tiles_of(geo_coarse3, 1))
    wait(send_sem, 6, tiles_of(geo_coarse2, 1))
    wait_spread(send_sem, 7, bound_y, ny)
    wait_spread(send_sem, 8, bound_x, nx)
    wait_spread(send_sem, 9, gram_y, ny)
    wait_spread(send_sem, 10, gram_x, nx)


def solution(mesh):
    nx, ny = mesh.shape["gx"], mesh.shape["gy"]

    def vmem(*shape):
        return pltpu.VMEM(shape, jnp.float32)

    one = [vmem(10, 64, 128)] * 10
    two = [vmem(10, 48, 128)] * 11
    three = [vmem(15, 40, 128)] * 6 + [vmem(ITERS + 1, 15, 40, 128), vmem(5, 40, 128)]

    def on_device(source, beta, shift):
        return pl.pallas_call(
            functools.partial(kernel, (nx, ny)),
            out_shape=jax.ShapeDtypeStruct(source.shape, jnp.float32),
            in_specs=[pl.BlockSpec(memory_space=pl.ANY)] * 3,
            out_specs=pl.BlockSpec(memory_space=pltpu.VMEM),
            scratch_shapes=[
                vmem(3, 10, 64, 128), vmem(2, 10, 48, 128), vmem(2, 15, 40, 128), vmem(10, 48, 128), vmem(15, 40, 128),
                *one, *two, *three,
                vmem(8 * ROWS, 128), vmem(8 * ROWS, 128),
                vmem(ny, 1, 128), vmem(nx, 1, 128), vmem(ny, 1, 128), vmem(nx, 1, 128),
                vmem(2 * ROWS, 128), vmem(140, 8, 128),
                pltpu.SemaphoreType.DMA((3,)), pltpu.SemaphoreType.DMA((11,)), pltpu.SemaphoreType.DMA((11,)),
            ],
            compiler_params=pltpu.CompilerParams(collective_id=0, has_side_effects=True, vmem_limit_bytes=40 * 2**20),
        )(source, beta, shift)

    placed = P("gx", "gy", None)
    return jax.shard_map(on_device, mesh=mesh, in_specs=(placed,) * 3, out_specs=placed, check_vma=False)
```

```python
import functools

import jax
import jax.numpy as jnp
from jax import lax
from jax.experimental import pallas as pl
from jax.experimental.pallas import tpu as pltpu
from jax.sharding import PartitionSpec as P

MESH = pl.DeviceIdType.MESH
ITERS = 6
FIRST = 1.0 / 1.2
CARRY = 2.0 / 7.0
SECOND = 0.75 / 0.7
KEEP = 1.0 + CARRY + SECOND * (1.0 - FIRST) / FIRST
VERTICAL = 1.0 / 16.0
PLANE_SCALES = (1.0, 0.25, 0.0625)
EDGE = 16
SPLIT = 4097.0

PAIRS = [(i, j) for i in range(ITERS) for j in range(i, ITERS)] + [(ITERS - 1, ITERS)]
SLOT = {pair: n for n, pair in enumerate(PAIRS)}
ROWS = 24


def two_sum(a, b):
    s = a + b
    t = s - a
    return s, (a - (s - t)) + (b - t)


def fast_two_sum(a, b):
    s = a + b
    return s, b - (s - a)


def halves(a):
    t = SPLIT * a
    high = t - (t - a)
    return high, a - high


def two_prod(a, b, a_halves=None, b_halves=None):
    ah, al = halves(a) if a_halves is None else a_halves
    bh, bl = halves(b) if b_halves is None else b_halves
    p = a * b
    return p, ((ah * bh - p) + ah * bl + al * bh) + al * bl


def dd_add(a, b):
    s, t = two_sum(a[0], b[0])
    return fast_two_sum(s, t + (a[1] + b[1]))


def dd_mul(a, b):
    p, t = two_prod(a[0], b[0])
    return fast_two_sum(p, t + (a[0] * b[1] + a[1] * b[0]))


def dd_neg(a):
    return -a[0], -a[1]


def dd_half(a):
    return 0.5 * a[0], 0.5 * a[1]


def dd_div(a, b):
    q = a[0] / b[0]
    p, t = two_prod(q, b[0])
    rest = ((a[0] - p) - t) + (a[1] - q * b[1])
    return fast_two_sum(q, rest / b[0])


def dd_dot(us, ws):
    terms = [dd_mul(u, w) for u, w in zip(us, ws)]
    while len(terms) > 1:
        terms = [dd_add(terms[i], terms[i + 1]) if i + 1 < len(terms) else terms[i] for i in range(0, len(terms), 2)]
    return terms[0]


def gradient_coefficients(gram):
    one = (jnp.ones_like(gram(0, 0)[0]), jnp.zeros_like(gram(0, 0)[0]))
    residual, direction, answer = [one], [one], [None] * ITERS
    norm_now = gram(0, 0)
    for turn in range(ITERS):
        image = []
        for k in range(turn + 2):
            terms = [direction[k]] if k <= turn else []
            if k >= 1:
                terms.append(direction[0] if k == 1 else dd_half(direction[k - 1]))
            if k + 1 <= turn:
                terms.append(dd_half(direction[k + 1]))
            total = terms[0]
            for term in terms[1:]:
                total = dd_add(total, term)
            image.append(total)
        along = dd_mul(direction[turn], dd_dot(image, [gram(i, turn) for i in range(turn + 2)]))
        alpha = dd_div(norm_now, along)
        for k in range(turn + 1):
            step = dd_mul(alpha, direction[k])
            answer[k] = step if answer[k] is None else dd_add(answer[k], step)
        if turn + 1 == ITERS:
            break
        less = dd_neg(alpha)
        steps = [dd_mul(less, value) for value in image]
        residual = [dd_add(residual[k], steps[k]) if k <= turn else steps[k] for k in range(turn + 2)]
        norm_next = dd_mul(residual[turn + 1], dd_dot(residual, [gram(i, turn + 1) for i in range(turn + 2)]))
        beta = dd_div(norm_next, norm_now)
        norm_now = norm_next
        direction = [dd_add(residual[k], dd_mul(beta, direction[k])) if k <= turn else residual[k] for k in range(turn + 2)]
    return [value[0] + value[1] for value in answer]


def loop(low, high, body):
    def step(p, carry):
        body(p)
        return carry

    for p in range(low, high):
        body(p)


def lane_of(shape):
    return lax.broadcasted_iota(jnp.int32, shape, len(shape) - 1)


def box(reach, width):
    return [(i, j) for i in range(-reach, reach + 1) for j in range(-width, width + 1) if (i, j) != (0, 0)]


def ring(count, size):
    far = sorted(range(1, count), key=lambda d: -min(d, count - d))
    return [((d, 0) if size else (0, d)) for d in far]


def windows(offsets, count, rows, first, reach):
    out = []
    for dx, dy in sorted(offsets, key=lambda o: -abs(o[0]) - abs(o[1])):
        if dx == 0:
            start, planes, target = 0, count, first
        elif dx > 0:
            start = max(0, dx * count - reach)
            planes, target = count - start, first - dx * count + start
        else:
            start, planes = 0, min(count, reach + (dx + 1) * count)
            target = first - dx * count
        row, high, to = (EDGE, rows, EDGE) if dy == 0 else (EDGE + rows - 8, 8, EDGE - 8) if dy > 0 else (EDGE, 8, EDGE + rows)
        out.append((dx, dy, first + start, target, planes, row, to, high))
    return out


def tiles_of(geometry, fields):
    return sum(fields * w[4] * w[7] // 8 for w in geometry)


def kernel(
    counts, source, beta, shift, out,
    fields, coarse2, coarse3, rhs2, rhs3,
    masked1, wx1, wy1, wz1, diag1, inv1, step1, near1, iter1, start1,
    masked2, wx2, wy2, wz2, diag2, inv2, step2, near2, iter2, start2, sum2,
    masked3, wx3, wy3, wz3, own3, inside3, basis, sol3,
    pair_high, pair_low, bound_y, bound_x, gram_y, gram_x, scalars, dummy,
    load_sem, send_sem, recv_sem,
):
    nx, ny = counts
    gx, gy = lax.axis_index("gx"), lax.axis_index("gy")

    def device(dx, dy):
        return lax.rem(gx + (dx + nx), nx), lax.rem(gy + (dy + ny), ny)

    near, wide, far = box(1, 1), box(2, 1), box(7, 1)
    over_y, over_x = ring(ny, 0), ring(nx, 1)

    loads = [
        pltpu.make_async_copy(ref, fields.at[n, pl.ds(3, 4), pl.ds(EDGE, 32)], load_sem.at[n])
        for n, ref in enumerate((source, shift, beta))
    ]
    for load in loads:
        load.start()

    partners = sorted({((dx + nx) % nx, (dy + ny) % ny) for dx, dy in far + over_y + over_x})
    barrier = pltpu.get_barrier_semaphore()
    for dx, dy in partners:
        pl.semaphore_signal(barrier, 1, device_id=device(-dx, -dy), device_id_type=MESH)

    def send(phase, ref, geometry, stacked):
        for dx, dy, plane, target, planes, row, to, high in geometry:
            here, there = (pl.ds(plane, planes), pl.ds(row, high)), (pl.ds(target, planes), pl.ds(to, high))
            if stacked:
                here, there = (slice(None), *here), (slice(None), *there)
            pltpu.make_async_remote_copy(
                src_ref=ref.at[here], dst_ref=ref.at[there], send_sem=send_sem.at[phase], recv_sem=recv_sem.at[phase],
                device_id=device(dx, dy), device_id_type=MESH,
            ).start()

    def wait(sems, phase, tiles):
        part = dummy.at[pl.ds(0, tiles)]
        pltpu.make_async_copy(part, part, sems.at[phase]).wait()

    def spread(phase, ref, offsets):
        for dx, dy in offsets:
            pltpu.make_async_remote_copy(
                src_ref=ref.at[0], dst_ref=ref.at[max(dx, dy)], send_sem=send_sem.at[phase], recv_sem=recv_sem.at[phase],
                device_id=device(dx, dy), device_id_type=MESH,
            ).start()

    def wait_spread(sems, phase, ref, count):
        part = ref.at[pl.ds(1, count - 1)]
        pltpu.make_async_copy(part, part, sems.at[phase]).wait()

    def inside(p, rows, low, first, count, own_planes, own_rows):
        plane = gx * own_planes + (p - first)
        row = gy * own_rows + (low - EDGE) + lax.broadcasted_iota(jnp.int32, (rows, 128), 0)
        fits = jnp.logical_and(plane >= 0, plane < nx * own_planes).astype(jnp.int32)
        return jnp.where(jnp.logical_and(row >= 0, row < ny * own_rows), fits, 0) > 0

    def off(v, wx, wy, wz, p, low, rows):
        here = v[p, pl.ds(low, rows), :]
        up = wz[p, pl.ds(low, rows), :]
        total = wx[p, pl.ds(low, rows), :] * v[p + 1, pl.ds(low, rows), :]
        total = total + wx[p - 1, pl.ds(low, rows), :] * v[p - 1, pl.ds(low, rows), :]
        total = total + wy[p, pl.ds(low, rows), :] * v[p, pl.ds(low + 1, rows), :]
        total = total + wy[p, pl.ds(low - 1, rows), :] * v[p, pl.ds(low - 1, rows), :]
        total = total + up * pltpu.roll(here, 127, 1)
        return total + pltpu.roll(up * here, 1, 1)

    def weights(b, p, low, rows, plane, upright):
        here = b[p, pl.ds(low, rows), :]
        lane = lane_of((rows, 128))
        wxp = plane * (here + b[p + 1, pl.ds(low, rows), :])
        wxm = plane * (here + b[p - 1, pl.ds(low, rows), :])
        wyp = plane * (here + b[p, pl.ds(low + 1, rows), :])
        wym = plane * (here + b[p, pl.ds(low - 1, rows), :])
        wzp = upright * (here + jnp.where(lane < 127, pltpu.roll(here, 127, 1), 0.0))
        wzm = upright * (here + jnp.where(lane > 0, pltpu.roll(here, 1, 1), 0.0))
        return wxp, wyp, jnp.where(lane < 127, wzp, 0.0), wxp + wxm + wyp + wym + wzp + wzm

    def prepare(refs, pair, rows, first, own, scale):
        masked, wx, wy, wz, diag, inv = refs
        shift_at, beta_at = pair

        def clean(p):
            ok = inside(p, rows, 8, first, 10, own[0], own[1])
            masked[p, pl.ds(8, rows), :] = jnp.where(ok, beta_at(p), 0.0)

        def fill(p):
            wxp, wyp, wzp, total = weights(masked, p, 8, rows, 0.5 * scale, 0.5 * VERTICAL)
            total = total + shift_at(p)
            wx[p, pl.ds(8, rows), :] = wxp
            wy[p, pl.ds(8, rows), :] = wyp
            wz[p, pl.ds(8, rows), :] = wzp
            diag[p, pl.ds(8, rows), :] = total
            ok = inside(p, rows, 8, first, 10, own[0], own[1])
            inv[p, pl.ds(8, rows), :] = jnp.where(ok, 1.0 / total, 0.0)

        loop(0, 10, clean)
        loop(1, 9, fill)

    def coarsen_rows(ref, at, rows):
        even = ref[at, pl.ds(EDGE, rows // 2, stride=2), :]
        return 0.25 * (even + ref[at, pl.ds(EDGE + 1, rows // 2, stride=2), :])

    for load in loads:
        load.wait()
    for n, level in ((0, 1), (1, 2)):
        for q in range(2):
            both = fields[1 + n, 3 + 2 * q, pl.ds(EDGE, 32), :] + fields[1 + n, 4 + 2 * q, pl.ds(EDGE, 32), :]
            near1[q, pl.ds(EDGE, 32), :] = both
            coarse2[n, 4 + q, pl.ds(EDGE, 16), :] = coarsen_rows(near1, q, 32)
        near2[0, pl.ds(EDGE, 16), :] = coarse2[n, 4, pl.ds(EDGE, 16), :] + coarse2[n, 5, pl.ds(EDGE, 16), :]
        coarse3[n, 7, pl.ds(EDGE, 8), :] = coarsen_rows(near2, 0, 16)
    shift_own, beta_own = coarse3[0, 7, pl.ds(EDGE, 8), :], coarse3[1, 7, pl.ds(EDGE, 8), :]
    around = pltpu.roll(beta_own, 1, 0) + pltpu.roll(beta_own, 7, 0) + pltpu.roll(beta_own, 1, 1) + pltpu.roll(beta_own, 127, 1)
    bound = jnp.max(shift_own + PLANE_SCALES[2] * (6.0 * beta_own + 1.5 * around))
    bound_y[0] = jnp.full((1, 128), bound, jnp.float32)

    pl.semaphore_wait(barrier, len(partners))
    geo_fields = windows(near, 4, 32, 3, 3)
    geo_coarse2 = windows(wide, 2, 16, 4, 4)
    geo_coarse3 = windows(far, 1, 8, 7, 7)
    geo_iter1 = windows(near, 4, 32, 3, 2)
    geo_rhs2 = windows(near, 2, 16, 4, 2)
    send(0, fields, geo_fields, True)
    send(1, coarse2, geo_coarse2, True)
    spread(7, bound_y, over_y)
    send(2, coarse3, geo_coarse3, True)

    wait(recv_sem, 0, tiles_of(geo_fields, 3))
    level1 = (masked1, wx1, wy1, wz1, diag1, inv1)
    prepare(
        level1, (lambda p: fields[1, p, pl.ds(8, 48), :], lambda p: fields[2, p, pl.ds(8, 48), :]), 48, 3, (4, 32), PLANE_SCALES[0]
    )

    def first_step(step, inv, value, rows):
        def body(p):
            step[p, pl.ds(8, rows), :] = FIRST * value(p) * inv[p, pl.ds(8, rows), :]

        return body

    def smooth(step, wx, wy, wz, inv, p, low, rows):
        part = off(step, wx, wy, wz, p, low, rows)
        return KEEP * step[p, pl.ds(low, rows), :] + SECOND * inv[p, pl.ds(low, rows), :] * part

    loop(1, 9, first_step(step1, inv1, lambda p: fields[0, p, pl.ds(8, 48), :], 48))

    def presmooth1(p):
        near1[p, pl.ds(8, 48), :] = smooth(step1, wx1, wy1, wz1, inv1, p, 8, 48)

    loop(2, 8, presmooth1)

    def residual(f, v, level, p, low, rows):
        _, wx, wy, wz, diag, _ = level
        value = f(p, low, rows) - diag[p, pl.ds(low, rows), :] * v[p, pl.ds(low, rows), :]
        return value + off(v, wx, wy, wz, p, low, rows)

    def source_at(p, low, rows):
        return fields[0, p, pl.ds(low, rows), :]

    def rhs2_at(p, low, rows):
        return rhs2[p, pl.ds(low, rows), :]

    def restrict1(q):
        both = residual(source_at, near1, level1, 3 + 2 * q, EDGE, 32) + residual(source_at, near1, level1, 4 + 2 * q, EDGE, 32)
        start1[q, pl.ds(EDGE, 32), :] = both
        rhs2[4 + q, pl.ds(EDGE, 16), :] = coarsen_rows(start1, q, 32)

    loop(0, 2, restrict1)
    send(3, rhs2, geo_rhs2, False)

    def keep1(p):
        iter1[p, pl.ds(EDGE, 32), :] = near1[p, pl.ds(EDGE, 32), :]

    loop(3, 7, keep1)
    send(4, iter1, geo_iter1, False)

    wait(recv_sem, 1, tiles_of(geo_coarse2, 2))
    level2 = (masked2, wx2, wy2, wz2, diag2, inv2)
    prepare(
        level2, (lambda p: coarse2[0, p, pl.ds(8, 32), :], lambda p: coarse2[1, p, pl.ds(8, 32), :]), 32, 4, (2, 16), PLANE_SCALES[1]
    )
    wait_spread(recv_sem, 7, bound_y, ny)
    bound_x[0] = functools.reduce(jnp.maximum, [bound_y[n] for n in range(ny)])
    spread(8, bound_x, over_x)

    wait(recv_sem, 3, tiles_of(geo_rhs2, 1))
    loop(2, 8, first_step(step2, inv2, lambda p: rhs2_at(p, 8, 32), 32))

    def presmooth2(p):
        near2[p, pl.ds(8, 32), :] = smooth(step2, wx2, wy2, wz2, inv2, p, 8, 32)

    loop(3, 7, presmooth2)
    both = residual(rhs2_at, near2, level2, 4, EDGE, 16) + residual(rhs2_at, near2, level2, 5, EDGE, 16)
    start2[0, pl.ds(EDGE, 16), :] = both
    rhs3[7, pl.ds(EDGE, 8), :] = coarsen_rows(start2, 0, 16)
    send(5, rhs3, geo_coarse3, False)
    for p in (4, 5):
        iter2[p, pl.ds(EDGE, 16), :] = near2[p, pl.ds(EDGE, 16), :]
    send(6, iter2, geo_coarse2, False)

    wait(recv_sem, 2, tiles_of(geo_coarse3, 2))
    wait_spread(recv_sem, 8, bound_x, nx)
    scale = 2.0 / functools.reduce(jnp.maximum, [bound_x[n] for n in range(nx)])

    def clean3(p):
        ok = inside(p, 24, 8, 7, 15, 1, 8)
        masked3[p, pl.ds(8, 24), :] = jnp.where(ok, coarse3[1, p, pl.ds(8, 24), :], 0.0)

    loop(0, 15, clean3)
    wx3[0, pl.ds(8, 24), :] = (PLANE_SCALES[2] * scale) * (masked3[0, pl.ds(8, 24), :] + masked3[1, pl.ds(8, 24), :])

    def fill3(p):
        wxp, wyp, wzp, total = weights(masked3, p, 8, 24, PLANE_SCALES[2] * scale, VERTICAL * scale)
        total = total + 2.0 * scale * coarse3[0, p, pl.ds(8, 24), :]
        wx3[p, pl.ds(8, 24), :] = wxp
        wy3[p, pl.ds(8, 24), :] = wyp
        wz3[p, pl.ds(8, 24), :] = wzp
        ok = inside(p, 24, 8, 7, 15, 1, 8)
        own3[p, pl.ds(8, 24), :] = jnp.where(ok, total - 2.0, 0.0)
        inside3[p, pl.ds(8, 24), :] = jnp.where(ok, 1.0, 0.0)

    loop(1, 14, fill3)
    wait(recv_sem, 5, tiles_of(geo_coarse3, 1))

    def begin3(p):
        ok = inside(p, 24, 8, 7, 15, 1, 8)
        basis[0, p, pl.ds(8, 24), :] = jnp.where(ok, rhs3[p, pl.ds(8, 24), :], 0.0)

    loop(0, 15, begin3)

    def doubled(v, p, low, rows):
        value = own3[p, pl.ds(low, rows), :] * v[p, pl.ds(low, rows), :]
        return value - inside3[p, pl.ds(low, rows), :] * off(v, wx3, wy3, wz3, p, low, rows)

    for k in range(ITERS):
        low, rows, reach = (8, 24, 6 - k) if k < ITERS - 1 else (EDGE, 8, 0)

        def advance(p, k=k, low=low, rows=rows):
            value = doubled(basis.at[k], p, low, rows)
            value = 0.5 * value if k == 0 else value - basis[k - 1, p, pl.ds(low, rows), :]
            basis[k + 1, p, pl.ds(low, rows), :] = value

        loop(7 - reach, 8 + reach, advance)

    own = [basis[k, 7, pl.ds(EDGE, 8), :] for k in range(ITERS + 1)]
    parts = [halves(v) for v in own]
    for n, (i, j) in enumerate(PAIRS):
        high, low = two_prod(own[i], own[j], parts[i], parts[j])
        pair_high[pl.ds(8 * n, 8), :] = high
        pair_low[pl.ds(8 * n, 8), :] = low
    for n in range(len(PAIRS), ROWS):
        pair_high[pl.ds(8 * n, 8), :] = jnp.zeros((8, 128), jnp.float32)
        pair_low[pl.ds(8 * n, 8), :] = jnp.zeros((8, 128), jnp.float32)

    def merge(a, b):
        s, t = two_sum(a[0], b[0])
        return s, t + (a[1] + b[1])

    def tree(terms):
        while len(terms) > 1:
            terms = [merge(terms[i], terms[i + 1]) if i + 1 < len(terms) else terms[i] for i in range(0, len(terms), 2)]
        return terms[0]

    sums = tree([(pair_high[pl.ds(s, ROWS, stride=8), :], pair_low[pl.ds(s, ROWS, stride=8), :]) for s in range(8)])
    for d in (64, 32, 16, 8, 4, 2, 1):
        sums = merge(sums, (pltpu.roll(sums[0], d, 1), pltpu.roll(sums[1], d, 1)))
    lane, row = lane_of((ROWS, 128)), lax.broadcasted_iota(jnp.int32, (ROWS, 128), 0)
    line = jnp.where(lane == row, sums[0], jnp.where(lane == row + 64, sums[1], 0.0))
    gram_y[0] = jnp.sum(line, axis=0, keepdims=True)

    def total_of(ref, count):
        zero = jnp.zeros((1, 128), jnp.float32)
        s, t = tree([(ref[n], zero) for n in range(count)])
        return s + jnp.where(lane_of((1, 128)) >= 64, pltpu.roll(t, 64, 1), 0.0)

    spread(9, gram_y, over_y)
    wait_spread(recv_sem, 9, gram_y, ny)
    gram_x[0] = total_of(gram_y, ny)
    spread(10, gram_x, over_x)
    wait(recv_sem, 4, tiles_of(geo_iter1, 1))
    wait(recv_sem, 6, tiles_of(geo_coarse2, 1))
    wait_spread(recv_sem, 10, gram_x, nx)
    entries = jnp.broadcast_to(total_of(gram_x, nx), (2 * ROWS, 128))
    lane, row = lane_of((2 * ROWS, 128)), lax.broadcasted_iota(jnp.int32, (2 * ROWS, 128), 0)
    place = jnp.where(row < ROWS, row, row + (64 - ROWS))
    column = jnp.sum(jnp.where(lane == place, entries, 0.0), axis=1, keepdims=True)
    scalars[...] = jnp.broadcast_to(column, (2 * ROWS, 128))

    def gram(i, j):
        n = SLOT[(min(i, j), max(i, j))]
        return scalars[pl.ds(n, 1), :], scalars[pl.ds(ROWS + n, 1), :]

    answer = [value * scale for value in gradient_coefficients(gram)]

    for n in range(5):
        p = 5 + n
        total = answer[0] * basis[0, p, pl.ds(8, 24), :]
        for k in range(1, ITERS):
            total = total + answer[k] * basis[k, p, pl.ds(8, 24), :]
        sol3[n, pl.ds(8, 24), :] = total

    def prolong2(p):
        value = sol3[p // 2, pl.ds(12, 16), :]
        start2[p, pl.ds(8, 16, stride=2), :] = value
        start2[p, pl.ds(9, 16, stride=2), :] = value
        ok = inside(p, 32, 8, 4, 10, 2, 16)
        start2[p, pl.ds(8, 32), :] = jnp.where(ok, start2[p, pl.ds(8, 32), :] + iter2[p, pl.ds(8, 32), :], 0.0)

    loop(1, 9, prolong2)
    loop(2, 8, first_step(step2, inv2, lambda p: residual(rhs2_at, start2, level2, p, 8, 32), 32))

    def post2(p):
        sum2[p, pl.ds(8, 32), :] = start2[p, pl.ds(8, 32), :] + smooth(step2, wx2, wy2, wz2, inv2, p, 8, 32)

    loop(3, 7, post2)

    def prolong1(p):
        value = sum2[(p + 5) // 2, pl.ds(12, 24), :]
        start1[p, pl.ds(8, 24, stride=2), :] = value
        start1[p, pl.ds(9, 24, stride=2), :] = value
        ok = inside(p, 48, 8, 3, 10, 4, 32)
        start1[p, pl.ds(8, 48), :] = jnp.where(ok, start1[p, pl.ds(8, 48), :] + iter1[p, pl.ds(8, 48), :], 0.0)

    loop(1, 9, prolong1)
    loop(2, 8, first_step(step1, inv1, lambda p: residual(source_at, start1, level1, p, 8, 48), 48))

    def post1(p):
        out[p - 3] = start1[p, pl.ds(EDGE, 32), :] + smooth(step1, wx1, wy1, wz1, inv1, p, EDGE, 32)

    loop(3, 7, post1)

    wait(send_sem, 0, tiles_of(geo_fields, 3))
    wait(send_sem, 1, tiles_of(geo_coarse2, 2))
    wait(send_sem, 2, tiles_of(geo_coarse3, 2))
    wait(send_sem, 3, tiles_of(geo_rhs2, 1))
    wait(send_sem, 4, tiles_of(geo_iter1, 1))
    wait(send_sem, 5, tiles_of(geo_coarse3, 1))
    wait(send_sem, 6, tiles_of(geo_coarse2, 1))
    wait_spread(send_sem, 7, bound_y, ny)
    wait_spread(send_sem, 8, bound_x, nx)
    wait_spread(send_sem, 9, gram_y, ny)
    wait_spread(send_sem, 10, gram_x, nx)


def solution(mesh):
    nx, ny = mesh.shape["gx"], mesh.shape["gy"]

    def vmem(*shape):
        return pltpu.VMEM(shape, jnp.float32)

    one = [vmem(10, 64, 128)] * 10
    two = [vmem(10, 48, 128)] * 11
    three = [vmem(15, 40, 128)] * 6 + [vmem(ITERS + 1, 15, 40, 128), vmem(5, 40, 128)]

    def on_device(source, beta, shift):
        return pl.pallas_call(
            functools.partial(kernel, (nx, ny)),
            out_shape=jax.ShapeDtypeStruct(source.shape, jnp.float32),
            in_specs=[pl.BlockSpec(memory_space=pl.ANY)] * 3,
            out_specs=pl.BlockSpec(memory_space=pltpu.VMEM),
            scratch_shapes=[
                vmem(3, 10, 64, 128), vmem(2, 10, 48, 128), vmem(2, 15, 40, 128), vmem(10, 48, 128), vmem(15, 40, 128),
                *one, *two, *three,
                vmem(8 * ROWS, 128), vmem(8 * ROWS, 128),
                vmem(ny, 1, 128), vmem(nx, 1, 128), vmem(ny, 1, 128), vmem(nx, 1, 128),
                vmem(2 * ROWS, 128), vmem(140, 8, 128),
                pltpu.SemaphoreType.DMA((3,)), pltpu.SemaphoreType.DMA((11,)), pltpu.SemaphoreType.DMA((11,)),
            ],
            compiler_params=pltpu.CompilerParams(collective_id=0, has_side_effects=True, vmem_limit_bytes=40 * 2**20),
        )(*[pltpu.with_memory_space_constraint(x, pltpu.HBM) for x in (source, beta, shift)])

    placed = P("gx", "gy", None)
    return jax.shard_map(on_device, mesh=mesh, in_specs=(placed,) * 3, out_specs=placed, check_vma=False)
```

```python
import functools

import jax
import jax.numpy as jnp
from jax import lax
from jax.experimental import pallas as pl
from jax.experimental.pallas import tpu as pltpu
from jax.sharding import PartitionSpec as P

MESH = pl.DeviceIdType.MESH
ITERS = 6
FIRST = 1.0 / 1.2
CARRY = 2.0 / 7.0
SECOND = 0.75 / 0.7
KEEP = 1.0 + CARRY + SECOND * (1.0 - FIRST) / FIRST
VERTICAL = 1.0 / 16.0
PLANE_SCALES = (1.0, 0.25, 0.0625)
EDGE = 16
SPLIT = 4097.0

PAIRS = [(i, j) for i in range(ITERS) for j in range(i, ITERS)] + [(ITERS - 1, ITERS)]
SLOT = {pair: n for n, pair in enumerate(PAIRS)}
ROWS = 24


def two_sum(a, b):
    s = a + b
    t = s - a
    return s, (a - (s - t)) + (b - t)


def fast_two_sum(a, b):
    s = a + b
    return s, b - (s - a)


def halves(a):
    t = SPLIT * a
    high = t - (t - a)
    return high, a - high


def two_prod(a, b, a_halves=None, b_halves=None):
    ah, al = halves(a) if a_halves is None else a_halves
    bh, bl = halves(b) if b_halves is None else b_halves
    p = a * b
    return p, ((ah * bh - p) + ah * bl + al * bh) + al * bl


def dd_add(a, b):
    s, t = two_sum(a[0], b[0])
    return fast_two_sum(s, t + (a[1] + b[1]))


def dd_mul(a, b):
    p, t = two_prod(a[0], b[0])
    return fast_two_sum(p, t + (a[0] * b[1] + a[1] * b[0]))


def dd_neg(a):
    return -a[0], -a[1]


def dd_half(a):
    return 0.5 * a[0], 0.5 * a[1]


def dd_div(a, b):
    q = a[0] / b[0]
    p, t = two_prod(q, b[0])
    rest = ((a[0] - p) - t) + (a[1] - q * b[1])
    return fast_two_sum(q, rest / b[0])


def dd_dot(us, ws):
    terms = [dd_mul(u, w) for u, w in zip(us, ws)]
    while len(terms) > 1:
        terms = [dd_add(terms[i], terms[i + 1]) if i + 1 < len(terms) else terms[i] for i in range(0, len(terms), 2)]
    return terms[0]


def gradient_coefficients(gram):
    one = (jnp.ones_like(gram(0, 0)[0]), jnp.zeros_like(gram(0, 0)[0]))
    residual, direction, answer = [one], [one], [None] * ITERS
    norm_now = gram(0, 0)
    for turn in range(ITERS):
        image = []
        for k in range(turn + 2):
            terms = [direction[k]] if k <= turn else []
            if k >= 1:
                terms.append(direction[0] if k == 1 else dd_half(direction[k - 1]))
            if k + 1 <= turn:
                terms.append(dd_half(direction[k + 1]))
            total = terms[0]
            for term in terms[1:]:
                total = dd_add(total, term)
            image.append(total)
        along = dd_mul(direction[turn], dd_dot(image, [gram(i, turn) for i in range(turn + 2)]))
        alpha = dd_div(norm_now, along)
        for k in range(turn + 1):
            step = dd_mul(alpha, direction[k])
            answer[k] = step if answer[k] is None else dd_add(answer[k], step)
        if turn + 1 == ITERS:
            break
        less = dd_neg(alpha)
        steps = [dd_mul(less, value) for value in image]
        residual = [dd_add(residual[k], steps[k]) if k <= turn else steps[k] for k in range(turn + 2)]
        norm_next = dd_mul(residual[turn + 1], dd_dot(residual, [gram(i, turn + 1) for i in range(turn + 2)]))
        beta = dd_div(norm_next, norm_now)
        norm_now = norm_next
        direction = [dd_add(residual[k], dd_mul(beta, direction[k])) if k <= turn else residual[k] for k in range(turn + 2)]
    return [value[0] + value[1] for value in answer]


def loop(low, high, body):
    def step(p, carry):
        body(p)
        return carry

    for p in range(low, high):
        body(p)


def lane_of(shape):
    return lax.broadcasted_iota(jnp.int32, shape, len(shape) - 1)


def box(reach, width):
    return [(i, j) for i in range(-reach, reach + 1) for j in range(-width, width + 1) if (i, j) != (0, 0)]


def ring(count, size):
    far = sorted(range(1, count), key=lambda d: -min(d, count - d))
    return [((d, 0) if size else (0, d)) for d in far]


def windows(offsets, count, rows, first, reach):
    out = []
    for dx, dy in sorted(offsets, key=lambda o: -abs(o[0]) - abs(o[1])):
        if dx == 0:
            start, planes, target = 0, count, first
        elif dx > 0:
            start = max(0, dx * count - reach)
            planes, target = count - start, first - dx * count + start
        else:
            start, planes = 0, min(count, reach + (dx + 1) * count)
            target = first - dx * count
        row, high, to = (EDGE, rows, EDGE) if dy == 0 else (EDGE + rows - 8, 8, EDGE - 8) if dy > 0 else (EDGE, 8, EDGE + rows)
        out.append((dx, dy, first + start, target, planes, row, to, high))
    return out


def tiles_of(geometry, fields):
    return sum(fields * w[4] * w[7] // 8 for w in geometry)


def kernel(
    counts, source, beta, shift, out,
    fields, coarse2, coarse3, rhs2, rhs3,
    masked1, wx1, wy1, wz1, diag1, inv1, step1, near1, iter1, start1,
    masked2, wx2, wy2, wz2, diag2, inv2, step2, near2, iter2, start2, sum2,
    masked3, wx3, wy3, wz3, own3, inside3, basis, sol3,
    pair_high, pair_low, bound_y, few, more, last, gram_y, gram_x, scalars, dummy,
    load_sem, send_sem, recv_sem,
):
    nx, ny = counts
    gx, gy = lax.axis_index("gx"), lax.axis_index("gy")

    def device(dx, dy):
        return lax.rem(gx + (dx + nx), nx), lax.rem(gy + (dy + ny), ny)

    near, wide, far = box(1, 1), box(2, 1), box(7, 1)
    over_y, over_x = ring(ny, 0), ring(nx, 1)
    middle = [o for o in far if 3 <= abs(o[0]) <= 4]
    outer = [o for o in far if abs(o[0]) > 4]
    few_x = [(d, 0) for d in (4, -4, 3, -3, 2, -2, 1, -1)]
    more_x, last_x = [(8, 0), (-8, 0)], [(nx // 2, 0)]

    loads = [
        pltpu.make_async_copy(ref, fields.at[n, pl.ds(3, 4), pl.ds(EDGE, 32)], load_sem.at[n])
        for n, ref in enumerate((source, shift, beta))
    ]
    for load in loads:
        load.start()

    partners = sorted({(dx, dy % ny) for dx, dy in wide + over_y}, key=lambda o: abs(o[0]) + min(o[1], ny - o[1]))
    barrier = pltpu.get_barrier_semaphore()
    for dx, dy in partners:
        pl.semaphore_signal(barrier, 1, device_id=device(-dx, -dy), device_id_type=MESH)

    def send(phase, ref, geometry, stacked):
        for dx, dy, plane, target, planes, row, to, high in geometry:
            here, there = (pl.ds(plane, planes), pl.ds(row, high)), (pl.ds(target, planes), pl.ds(to, high))
            if stacked:
                here, there = (slice(None), *here), (slice(None), *there)
            pltpu.make_async_remote_copy(
                src_ref=ref.at[here], dst_ref=ref.at[there], send_sem=send_sem.at[phase], recv_sem=recv_sem.at[phase],
                device_id=device(dx, dy), device_id_type=MESH,
            ).start()

    def wait(sems, phase, tiles):
        part = dummy.at[pl.ds(0, tiles)]
        pltpu.make_async_copy(part, part, sems.at[phase]).wait()

    def spread(phase, ref, offsets, slots=None):
        for n, (dx, dy) in enumerate(offsets):
            pltpu.make_async_remote_copy(
                src_ref=ref.at[0], dst_ref=ref.at[max(dx, dy) if slots is None else 1 + n], send_sem=send_sem.at[phase], recv_sem=recv_sem.at[phase],
                device_id=device(dx, dy), device_id_type=MESH,
            ).start()

    def wait_spread(sems, phase, ref, count):
        part = ref.at[pl.ds(1, count - 1)]
        pltpu.make_async_copy(part, part, sems.at[phase]).wait()

    def inside(p, rows, low, first, count, own_planes, own_rows):
        plane = gx * own_planes + (p - first)
        row = gy * own_rows + (low - EDGE) + lax.broadcasted_iota(jnp.int32, (rows, 128), 0)
        fits = jnp.logical_and(plane >= 0, plane < nx * own_planes).astype(jnp.int32)
        return jnp.where(jnp.logical_and(row >= 0, row < ny * own_rows), fits, 0) > 0

    def off(v, wx, wy, wz, p, low, rows):
        here = v[p, pl.ds(low, rows), :]
        up = wz[p, pl.ds(low, rows), :]
        total = wx[p, pl.ds(low, rows), :] * v[p + 1, pl.ds(low, rows), :]
        total = total + wx[p - 1, pl.ds(low, rows), :] * v[p - 1, pl.ds(low, rows), :]
        total = total + wy[p, pl.ds(low, rows), :] * v[p, pl.ds(low + 1, rows), :]
        total = total + wy[p, pl.ds(low - 1, rows), :] * v[p, pl.ds(low - 1, rows), :]
        total = total + up * pltpu.roll(here, 127, 1)
        return total + pltpu.roll(up * here, 1, 1)

    def weights(b, p, low, rows, plane, upright):
        here = b[p, pl.ds(low, rows), :]
        lane = lane_of((rows, 128))
        wxp = plane * (here + b[p + 1, pl.ds(low, rows), :])
        wxm = plane * (here + b[p - 1, pl.ds(low, rows), :])
        wyp = plane * (here + b[p, pl.ds(low + 1, rows), :])
        wym = plane * (here + b[p, pl.ds(low - 1, rows), :])
        wzp = upright * (here + jnp.where(lane < 127, pltpu.roll(here, 127, 1), 0.0))
        wzm = upright * (here + jnp.where(lane > 0, pltpu.roll(here, 1, 1), 0.0))
        return wxp, wyp, jnp.where(lane < 127, wzp, 0.0), wxp + wxm + wyp + wym + wzp + wzm

    def prepare(refs, pair, rows, first, own, scale):
        masked, wx, wy, wz, diag, inv = refs
        shift_at, beta_at = pair

        def clean(p):
            ok = inside(p, rows, 8, first, 10, own[0], own[1])
            masked[p, pl.ds(8, rows), :] = jnp.where(ok, beta_at(p), 0.0)

        def fill(p):
            wxp, wyp, wzp, total = weights(masked, p, 8, rows, 0.5 * scale, 0.5 * VERTICAL)
            total = total + shift_at(p)
            wx[p, pl.ds(8, rows), :] = wxp
            wy[p, pl.ds(8, rows), :] = wyp
            wz[p, pl.ds(8, rows), :] = wzp
            diag[p, pl.ds(8, rows), :] = total
            ok = inside(p, rows, 8, first, 10, own[0], own[1])
            inv[p, pl.ds(8, rows), :] = jnp.where(ok, 1.0 / total, 0.0)

        loop(0, 10, clean)
        loop(1, 9, fill)

    def coarsen_rows(ref, at, rows):
        even = ref[at, pl.ds(EDGE, rows // 2, stride=2), :]
        return 0.25 * (even + ref[at, pl.ds(EDGE + 1, rows // 2, stride=2), :])

    geo_fields = windows(near, 4, 32, 3, 3)
    geo_coarse2 = windows(wide, 2, 16, 4, 3)
    geo_coarse3, geo_middle3, geo_outer3 = (windows(part, 1, 8, 7, 7) for part in (wide, middle, outer))
    geo_rhs3 = windows(far, 1, 8, 7, 7)
    geo_iter1 = windows(near, 4, 32, 3, 2)
    geo_rhs2 = windows(near, 2, 16, 4, 2)
    for load in loads:
        load.wait()
    pl.semaphore_wait(barrier, len(partners))
    send(0, fields, geo_fields, True)

    for n, level in ((0, 1), (1, 2)):
        for q in range(2):
            both = fields[1 + n, 3 + 2 * q, pl.ds(EDGE, 32), :] + fields[1 + n, 4 + 2 * q, pl.ds(EDGE, 32), :]
            near1[q, pl.ds(EDGE, 32), :] = both
            coarse2[n, 4 + q, pl.ds(EDGE, 16), :] = coarsen_rows(near1, q, 32)
        near2[0, pl.ds(EDGE, 16), :] = coarse2[n, 4, pl.ds(EDGE, 16), :] + coarse2[n, 5, pl.ds(EDGE, 16), :]
        coarse3[n, 7, pl.ds(EDGE, 8), :] = coarsen_rows(near2, 0, 16)
    shift_own, beta_own = coarse3[0, 7, pl.ds(EDGE, 8), :], coarse3[1, 7, pl.ds(EDGE, 8), :]
    around = pltpu.roll(beta_own, 1, 0) + pltpu.roll(beta_own, 7, 0) + pltpu.roll(beta_own, 1, 1) + pltpu.roll(beta_own, 127, 1)
    bound = jnp.max(shift_own + PLANE_SCALES[2] * (6.0 * beta_own + 1.5 * around))
    bound_y[0] = jnp.full((1, 128), bound, jnp.float32)

    spread(7, bound_y, over_y)
    send(1, coarse2, geo_coarse2, True)
    send(2, coarse3, geo_coarse3, True)

    wait(recv_sem, 0, tiles_of(geo_fields, 3))
    wait(recv_sem, 1, tiles_of(geo_coarse2, 2))
    wait_spread(recv_sem, 7, bound_y, ny)
    few[0] = functools.reduce(jnp.maximum, [bound_y[n] for n in range(ny)])
    spread(8, few, few_x, True)
    send(11, coarse3, geo_middle3, True)
    level1 = (masked1, wx1, wy1, wz1, diag1, inv1)
    prepare(
        level1, (lambda p: fields[1, p, pl.ds(8, 48), :], lambda p: fields[2, p, pl.ds(8, 48), :]), 48, 3, (4, 32), PLANE_SCALES[0]
    )

    def first_step(step, inv, value, rows):
        def body(p):
            step[p, pl.ds(8, rows), :] = FIRST * value(p) * inv[p, pl.ds(8, rows), :]

        return body

    def smooth(step, wx, wy, wz, inv, p, low, rows):
        part = off(step, wx, wy, wz, p, low, rows)
        return KEEP * step[p, pl.ds(low, rows), :] + SECOND * inv[p, pl.ds(low, rows), :] * part

    loop(1, 9, first_step(step1, inv1, lambda p: fields[0, p, pl.ds(8, 48), :], 48))

    def presmooth1(p):
        near1[p, pl.ds(8, 48), :] = smooth(step1, wx1, wy1, wz1, inv1, p, 8, 48)

    loop(2, 8, presmooth1)

    def residual(f, v, level, p, low, rows):
        _, wx, wy, wz, diag, _ = level
        value = f(p, low, rows) - diag[p, pl.ds(low, rows), :] * v[p, pl.ds(low, rows), :]
        return value + off(v, wx, wy, wz, p, low, rows)

    def source_at(p, low, rows):
        return fields[0, p, pl.ds(low, rows), :]

    def rhs2_at(p, low, rows):
        return rhs2[p, pl.ds(low, rows), :]

    def restrict1(q):
        both = residual(source_at, near1, level1, 3 + 2 * q, EDGE, 32) + residual(source_at, near1, level1, 4 + 2 * q, EDGE, 32)
        start1[q, pl.ds(EDGE, 32), :] = both
        rhs2[4 + q, pl.ds(EDGE, 16), :] = coarsen_rows(start1, q, 32)

    loop(0, 2, restrict1)
    send(3, rhs2, geo_rhs2, False)

    def keep1(p):
        iter1[p, pl.ds(EDGE, 32), :] = near1[p, pl.ds(EDGE, 32), :]

    loop(3, 7, keep1)
    send(4, iter1, geo_iter1, False)

    level2 = (masked2, wx2, wy2, wz2, diag2, inv2)
    prepare(
        level2, (lambda p: coarse2[0, p, pl.ds(8, 32), :], lambda p: coarse2[1, p, pl.ds(8, 32), :]), 32, 4, (2, 16), PLANE_SCALES[1]
    )
    wait_spread(recv_sem, 8, few, 9)
    more[0] = functools.reduce(jnp.maximum, [few[n] for n in range(9)])
    spread(12, more, more_x, True)
    send(13, coarse3, geo_outer3, True)
    wait(recv_sem, 3, tiles_of(geo_rhs2, 1))
    loop(2, 8, first_step(step2, inv2, lambda p: rhs2_at(p, 8, 32), 32))

    def presmooth2(p):
        near2[p, pl.ds(8, 32), :] = smooth(step2, wx2, wy2, wz2, inv2, p, 8, 32)

    loop(3, 7, presmooth2)
    both = residual(rhs2_at, near2, level2, 4, EDGE, 16) + residual(rhs2_at, near2, level2, 5, EDGE, 16)
    start2[0, pl.ds(EDGE, 16), :] = both
    rhs3[7, pl.ds(EDGE, 8), :] = coarsen_rows(start2, 0, 16)
    send(5, rhs3, geo_rhs3, False)
    for p in (4, 5):
        iter2[p, pl.ds(EDGE, 16), :] = near2[p, pl.ds(EDGE, 16), :]
    send(6, iter2, geo_coarse2, False)

    wait_spread(recv_sem, 12, more, 3)
    last[0] = functools.reduce(jnp.maximum, [more[n] for n in range(3)])
    spread(14, last, last_x, True)
    wait(recv_sem, 2, tiles_of(geo_coarse3, 2))
    wait(recv_sem, 11, tiles_of(geo_middle3, 2))
    wait(recv_sem, 13, tiles_of(geo_outer3, 2))
    wait_spread(recv_sem, 14, last, 2)
    scale = 2.0 / jnp.maximum(last[0], last[1])

    def clean3(p):
        ok = inside(p, 24, 8, 7, 15, 1, 8)
        masked3[p, pl.ds(8, 24), :] = jnp.where(ok, coarse3[1, p, pl.ds(8, 24), :], 0.0)

    loop(0, 15, clean3)
    wx3[0, pl.ds(8, 24), :] = (PLANE_SCALES[2] * scale) * (masked3[0, pl.ds(8, 24), :] + masked3[1, pl.ds(8, 24), :])

    def fill3(p):
        wxp, wyp, wzp, total = weights(masked3, p, 8, 24, PLANE_SCALES[2] * scale, VERTICAL * scale)
        total = total + 2.0 * scale * coarse3[0, p, pl.ds(8, 24), :]
        wx3[p, pl.ds(8, 24), :] = wxp
        wy3[p, pl.ds(8, 24), :] = wyp
        wz3[p, pl.ds(8, 24), :] = wzp
        ok = inside(p, 24, 8, 7, 15, 1, 8)
        own3[p, pl.ds(8, 24), :] = jnp.where(ok, total - 2.0, 0.0)
        inside3[p, pl.ds(8, 24), :] = jnp.where(ok, 1.0, 0.0)

    loop(1, 14, fill3)
    wait(recv_sem, 5, tiles_of(geo_rhs3, 1))

    def begin3(p):
        ok = inside(p, 24, 8, 7, 15, 1, 8)
        basis[0, p, pl.ds(8, 24), :] = jnp.where(ok, rhs3[p, pl.ds(8, 24), :], 0.0)

    loop(0, 15, begin3)

    def doubled(v, p, low, rows):
        value = own3[p, pl.ds(low, rows), :] * v[p, pl.ds(low, rows), :]
        return value - inside3[p, pl.ds(low, rows), :] * off(v, wx3, wy3, wz3, p, low, rows)

    for k in range(ITERS):
        low, rows, reach = (8, 24, 6 - k) if k < ITERS - 1 else (EDGE, 8, 0)

        def advance(p, k=k, low=low, rows=rows):
            value = doubled(basis.at[k], p, low, rows)
            value = 0.5 * value if k == 0 else value - basis[k - 1, p, pl.ds(low, rows), :]
            basis[k + 1, p, pl.ds(low, rows), :] = value

        loop(7 - reach, 8 + reach, advance)

    own = [basis[k, 7, pl.ds(EDGE, 8), :] for k in range(ITERS + 1)]
    parts = [halves(v) for v in own]
    for n, (i, j) in enumerate(PAIRS):
        high, low = two_prod(own[i], own[j], parts[i], parts[j])
        pair_high[pl.ds(8 * n, 8), :] = high
        pair_low[pl.ds(8 * n, 8), :] = low
    for n in range(len(PAIRS), ROWS):
        pair_high[pl.ds(8 * n, 8), :] = jnp.zeros((8, 128), jnp.float32)
        pair_low[pl.ds(8 * n, 8), :] = jnp.zeros((8, 128), jnp.float32)

    def merge(a, b):
        s, t = two_sum(a[0], b[0])
        return s, t + (a[1] + b[1])

    def tree(terms):
        while len(terms) > 1:
            terms = [merge(terms[i], terms[i + 1]) if i + 1 < len(terms) else terms[i] for i in range(0, len(terms), 2)]
        return terms[0]

    sums = tree([(pair_high[pl.ds(s, ROWS, stride=8), :], pair_low[pl.ds(s, ROWS, stride=8), :]) for s in range(8)])
    for d in (64, 32, 16, 8, 4, 2, 1):
        sums = merge(sums, (pltpu.roll(sums[0], d, 1), pltpu.roll(sums[1], d, 1)))
    lane, row = lane_of((ROWS, 128)), lax.broadcasted_iota(jnp.int32, (ROWS, 128), 0)
    line = jnp.where(lane == row, sums[0], jnp.where(lane == row + 64, sums[1], 0.0))
    gram_y[0] = jnp.sum(line, axis=0, keepdims=True)

    def total_of(ref, count):
        zero = jnp.zeros((1, 128), jnp.float32)
        s, t = tree([(ref[n], zero) for n in range(count)])
        return s + jnp.where(lane_of((1, 128)) >= 64, pltpu.roll(t, 64, 1), 0.0)

    spread(9, gram_y, over_y)
    wait_spread(recv_sem, 9, gram_y, ny)
    gram_x[0] = total_of(gram_y, ny)
    spread(10, gram_x, over_x)
    wait(recv_sem, 4, tiles_of(geo_iter1, 1))
    wait(recv_sem, 6, tiles_of(geo_coarse2, 1))
    wait_spread(recv_sem, 10, gram_x, nx)
    entries = jnp.broadcast_to(total_of(gram_x, nx), (2 * ROWS, 128))
    lane, row = lane_of((2 * ROWS, 128)), lax.broadcasted_iota(jnp.int32, (2 * ROWS, 128), 0)
    place = jnp.where(row < ROWS, row, row + (64 - ROWS))
    column = jnp.sum(jnp.where(lane == place, entries, 0.0), axis=1, keepdims=True)
    scalars[...] = jnp.broadcast_to(column, (2 * ROWS, 128))

    def gram(i, j):
        n = SLOT[(min(i, j), max(i, j))]
        return scalars[pl.ds(n, 1), :], scalars[pl.ds(ROWS + n, 1), :]

    answer = [value * scale for value in gradient_coefficients(gram)]

    for n in range(5):
        p = 5 + n
        total = answer[0] * basis[0, p, pl.ds(8, 24), :]
        for k in range(1, ITERS):
            total = total + answer[k] * basis[k, p, pl.ds(8, 24), :]
        sol3[n, pl.ds(8, 24), :] = total

    def prolong2(p):
        value = sol3[p // 2, pl.ds(12, 16), :]
        start2[p, pl.ds(8, 16, stride=2), :] = value
        start2[p, pl.ds(9, 16, stride=2), :] = value
        ok = inside(p, 32, 8, 4, 10, 2, 16)
        start2[p, pl.ds(8, 32), :] = jnp.where(ok, start2[p, pl.ds(8, 32), :] + iter2[p, pl.ds(8, 32), :], 0.0)

    loop(1, 9, prolong2)
    loop(2, 8, first_step(step2, inv2, lambda p: residual(rhs2_at, start2, level2, p, 8, 32), 32))

    def post2(p):
        sum2[p, pl.ds(8, 32), :] = start2[p, pl.ds(8, 32), :] + smooth(step2, wx2, wy2, wz2, inv2, p, 8, 32)

    loop(3, 7, post2)

    def prolong1(p):
        value = sum2[(p + 5) // 2, pl.ds(12, 24), :]
        start1[p, pl.ds(8, 24, stride=2), :] = value
        start1[p, pl.ds(9, 24, stride=2), :] = value
        ok = inside(p, 48, 8, 3, 10, 4, 32)
        start1[p, pl.ds(8, 48), :] = jnp.where(ok, start1[p, pl.ds(8, 48), :] + iter1[p, pl.ds(8, 48), :], 0.0)

    loop(1, 9, prolong1)
    loop(2, 8, first_step(step1, inv1, lambda p: residual(source_at, start1, level1, p, 8, 48), 48))

    def post1(p):
        out[p - 3] = start1[p, pl.ds(EDGE, 32), :] + smooth(step1, wx1, wy1, wz1, inv1, p, EDGE, 32)

    loop(3, 7, post1)

    wait(send_sem, 0, tiles_of(geo_fields, 3))
    wait(send_sem, 1, tiles_of(geo_coarse2, 2))
    wait(send_sem, 2, tiles_of(geo_coarse3, 2))
    wait(send_sem, 11, tiles_of(geo_middle3, 2))
    wait(send_sem, 13, tiles_of(geo_outer3, 2))
    wait(send_sem, 3, tiles_of(geo_rhs2, 1))
    wait(send_sem, 4, tiles_of(geo_iter1, 1))
    wait(send_sem, 5, tiles_of(geo_rhs3, 1))
    wait(send_sem, 6, tiles_of(geo_coarse2, 1))
    wait_spread(send_sem, 7, bound_y, ny)
    wait_spread(send_sem, 8, few, 9)
    wait_spread(send_sem, 12, more, 3)
    wait_spread(send_sem, 14, last, 2)
    wait_spread(send_sem, 9, gram_y, ny)
    wait_spread(send_sem, 10, gram_x, nx)


def solution(mesh):
    nx, ny = mesh.shape["gx"], mesh.shape["gy"]

    def vmem(*shape):
        return pltpu.VMEM(shape, jnp.float32)

    one = [vmem(10, 64, 128)] * 10
    two = [vmem(10, 48, 128)] * 11
    three = [vmem(15, 40, 128)] * 6 + [vmem(ITERS + 1, 15, 40, 128), vmem(5, 40, 128)]

    def on_device(source, beta, shift):
        return pl.pallas_call(
            functools.partial(kernel, (nx, ny)),
            out_shape=jax.ShapeDtypeStruct(source.shape, jnp.float32),
            in_specs=[pl.BlockSpec(memory_space=pl.ANY)] * 3,
            out_specs=pl.BlockSpec(memory_space=pltpu.VMEM),
            scratch_shapes=[
                vmem(3, 10, 64, 128), vmem(2, 10, 48, 128), vmem(2, 15, 40, 128), vmem(10, 48, 128), vmem(15, 40, 128),
                *one, *two, *three,
                vmem(8 * ROWS, 128), vmem(8 * ROWS, 128),
                vmem(ny, 1, 128), vmem(9, 1, 128), vmem(3, 1, 128), vmem(2, 1, 128), vmem(ny, 1, 128), vmem(nx, 1, 128),
                vmem(2 * ROWS, 128), vmem(140, 8, 128),
                pltpu.SemaphoreType.DMA((3,)), pltpu.SemaphoreType.DMA((15,)), pltpu.SemaphoreType.DMA((15,)),
            ],
            compiler_params=pltpu.CompilerParams(collective_id=0, has_side_effects=True, vmem_limit_bytes=40 * 2**20),
        )(*[pltpu.with_memory_space_constraint(x, pltpu.HBM) for x in (source, beta, shift)])

    placed = P("gx", "gy", None)
    return jax.shard_map(on_device, mesh=mesh, in_specs=(placed,) * 3, out_specs=placed, check_vma=False)
```

```python
import functools

import jax
import jax.numpy as jnp
from jax import lax
from jax.experimental import pallas as pl
from jax.experimental.pallas import tpu as pltpu
from jax.sharding import PartitionSpec as P

MESH = pl.DeviceIdType.MESH
ITERS = 6
FIRST = 1.0 / 1.2
CARRY = 2.0 / 7.0
SECOND = 0.75 / 0.7
KEEP = 1.0 + CARRY + SECOND * (1.0 - FIRST) / FIRST
VERTICAL = 1.0 / 16.0
PLANE_SCALES = (1.0, 0.25, 0.0625)
EDGE = 16
SPLIT = 4097.0

PAIRS = [(i, j) for i in range(ITERS) for j in range(i, ITERS)] + [(ITERS - 1, ITERS)]
SLOT = {pair: n for n, pair in enumerate(PAIRS)}
ROWS = 24


def two_sum(a, b):
    s = a + b
    t = s - a
    return s, (a - (s - t)) + (b - t)


def fast_two_sum(a, b):
    s = a + b
    return s, b - (s - a)


def halves(a):
    t = SPLIT * a
    high = t - (t - a)
    return high, a - high


def two_prod(a, b, a_halves=None, b_halves=None):
    ah, al = halves(a) if a_halves is None else a_halves
    bh, bl = halves(b) if b_halves is None else b_halves
    p = a * b
    return p, ((ah * bh - p) + ah * bl + al * bh) + al * bl


def dd_add(a, b):
    s, t = two_sum(a[0], b[0])
    return fast_two_sum(s, t + (a[1] + b[1]))


def dd_mul(a, b):
    p, t = two_prod(a[0], b[0])
    return fast_two_sum(p, t + (a[0] * b[1] + a[1] * b[0]))


def dd_neg(a):
    return -a[0], -a[1]


def dd_half(a):
    return 0.5 * a[0], 0.5 * a[1]


def dd_div(a, b):
    q = a[0] / b[0]
    p, t = two_prod(q, b[0])
    rest = ((a[0] - p) - t) + (a[1] - q * b[1])
    return fast_two_sum(q, rest / b[0])


def dd_dot(us, ws):
    terms = [dd_mul(u, w) for u, w in zip(us, ws)]
    while len(terms) > 1:
        terms = [dd_add(terms[i], terms[i + 1]) if i + 1 < len(terms) else terms[i] for i in range(0, len(terms), 2)]
    return terms[0]


def gradient_coefficients(gram):
    one = (jnp.ones_like(gram(0, 0)[0]), jnp.zeros_like(gram(0, 0)[0]))
    residual, direction, answer = [one], [one], [None] * ITERS
    norm_now = gram(0, 0)
    for turn in range(ITERS):
        image = []
        for k in range(turn + 2):
            terms = [direction[k]] if k <= turn else []
            if k >= 1:
                terms.append(direction[0] if k == 1 else dd_half(direction[k - 1]))
            if k + 1 <= turn:
                terms.append(dd_half(direction[k + 1]))
            total = terms[0]
            for term in terms[1:]:
                total = dd_add(total, term)
            image.append(total)
        along = dd_mul(direction[turn], dd_dot(image, [gram(i, turn) for i in range(turn + 2)]))
        alpha = dd_div(norm_now, along)
        for k in range(turn + 1):
            step = dd_mul(alpha, direction[k])
            answer[k] = step if answer[k] is None else dd_add(answer[k], step)
        if turn + 1 == ITERS:
            break
        less = dd_neg(alpha)
        steps = [dd_mul(less, value) for value in image]
        residual = [dd_add(residual[k], steps[k]) if k <= turn else steps[k] for k in range(turn + 2)]
        norm_next = dd_mul(residual[turn + 1], dd_dot(residual, [gram(i, turn + 1) for i in range(turn + 2)]))
        beta = dd_div(norm_next, norm_now)
        norm_now = norm_next
        direction = [dd_add(residual[k], dd_mul(beta, direction[k])) if k <= turn else residual[k] for k in range(turn + 2)]
    return [value[0] + value[1] for value in answer]


def loop(low, high, body):
    def step(p, carry):
        body(p)
        return carry

    for p in range(low, high):
        body(p)


def lane_of(shape):
    return lax.broadcasted_iota(jnp.int32, shape, len(shape) - 1)


def box(reach, width):
    return [(i, j) for i in range(-reach, reach + 1) for j in range(-width, width + 1) if (i, j) != (0, 0)]


def ring(count, size):
    far = sorted(range(1, count), key=lambda d: -min(d, count - d))
    return [((d, 0) if size else (0, d)) for d in far]


def windows(offsets, count, rows, first, reach):
    out = []
    for dx, dy in sorted(offsets, key=lambda o: -abs(o[0]) - abs(o[1])):
        if dx == 0:
            start, planes, target = 0, count, first
        elif dx > 0:
            start = max(0, dx * count - reach)
            planes, target = count - start, first - dx * count + start
        else:
            start, planes = 0, min(count, reach + (dx + 1) * count)
            target = first - dx * count
        edge = 4 if count == 1 and abs(dx) > 3 else 8
        row, high, to = (EDGE, rows, EDGE) if dy == 0 else (EDGE + rows - edge, edge, EDGE - edge) if dy > 0 else (EDGE, edge, EDGE + rows)
        out.append((dx, dy, first + start, target, planes, row, to, high))
    return out


def tiles_of(geometry, fields):
    return fields * sum(w[4] * w[7] for w in geometry) // 8


def kernel(
    counts, source, beta, shift, out,
    fields, coarse2, coarse3, rhs2, rhs3,
    masked1, wx1, wy1, wz1, diag1, inv1, step1, near1, iter1, start1,
    masked2, wx2, wy2, wz2, diag2, inv2, step2, near2, iter2, start2, sum2,
    masked3, wx3, wy3, wz3, own3, inside3, basis, sol3,
    pair_high, pair_low, bound_y, bound_x, gram_y, gram_x, scalars, dummy,
    load_sem, send_sem, recv_sem,
):
    nx, ny = counts
    gx, gy = lax.axis_index("gx"), lax.axis_index("gy")

    def device(dx, dy):
        return lax.rem(gx + (dx + nx), nx), lax.rem(gy + (dy + ny), ny)

    near, wide, far = box(1, 1), box(2, 1), box(7, 1)
    over_y, over_x = ring(ny, 0), ring(nx, 1)
    middle = [o for o in far if 3 <= abs(o[0]) <= 4]
    outer = [o for o in far if abs(o[0]) > 4]

    loads = [
        pltpu.make_async_copy(ref, fields.at[n, pl.ds(3, 4), pl.ds(EDGE, 32)], load_sem.at[n])
        for n, ref in enumerate((source, shift, beta))
    ]
    for load in loads:
        load.start()

    partners = sorted({(dx % nx, dy % ny) for dx, dy in far + over_y + over_x}, key=lambda o: min(o[0], nx - o[0]) + min(o[1], ny - o[1]))
    barrier = pltpu.get_barrier_semaphore()
    for dx, dy in partners:
        pl.semaphore_signal(barrier, 1, device_id=device(-dx, -dy), device_id_type=MESH)

    def send(phase, ref, geometry, stacked):
        for dx, dy, plane, target, planes, row, to, high in geometry:
            here, there = (pl.ds(plane, planes), pl.ds(row, high)), (pl.ds(target, planes), pl.ds(to, high))
            if stacked:
                here, there = (slice(None), *here), (slice(None), *there)
            pltpu.make_async_remote_copy(
                src_ref=ref.at[here], dst_ref=ref.at[there], send_sem=send_sem.at[phase], recv_sem=recv_sem.at[phase],
                device_id=device(dx, dy), device_id_type=MESH,
            ).start()

    def wait(sems, phase, tiles):
        part = dummy.at[pl.ds(0, tiles)]
        pltpu.make_async_copy(part, part, sems.at[phase]).wait()

    def spread(phase, ref, offsets):
        for dx, dy in offsets:
            pltpu.make_async_remote_copy(
                src_ref=ref.at[0], dst_ref=ref.at[max(dx, dy)], send_sem=send_sem.at[phase], recv_sem=recv_sem.at[phase],
                device_id=device(dx, dy), device_id_type=MESH,
            ).start()

    def wait_spread(sems, phase, ref, count):
        part = ref.at[pl.ds(1, count - 1)]
        pltpu.make_async_copy(part, part, sems.at[phase]).wait()

    def inside(p, rows, low, first, count, own_planes, own_rows):
        plane = gx * own_planes + (p - first)
        row = gy * own_rows + (low - EDGE) + lax.broadcasted_iota(jnp.int32, (rows, 128), 0)
        fits = jnp.logical_and(plane >= 0, plane < nx * own_planes).astype(jnp.int32)
        return jnp.where(jnp.logical_and(row >= 0, row < ny * own_rows), fits, 0) > 0

    def off(v, wx, wy, wz, p, low, rows):
        here = v[p, pl.ds(low, rows), :]
        up = wz[p, pl.ds(low, rows), :]
        total = wx[p, pl.ds(low, rows), :] * v[p + 1, pl.ds(low, rows), :]
        total = total + wx[p - 1, pl.ds(low, rows), :] * v[p - 1, pl.ds(low, rows), :]
        total = total + wy[p, pl.ds(low, rows), :] * v[p, pl.ds(low + 1, rows), :]
        total = total + wy[p, pl.ds(low - 1, rows), :] * v[p, pl.ds(low - 1, rows), :]
        total = total + up * pltpu.roll(here, 127, 1)
        return total + pltpu.roll(up * here, 1, 1)

    def weights(b, p, low, rows, plane, upright):
        here = b[p, pl.ds(low, rows), :]
        lane = lane_of((rows, 128))
        wxp = plane * (here + b[p + 1, pl.ds(low, rows), :])
        wxm = plane * (here + b[p - 1, pl.ds(low, rows), :])
        wyp = plane * (here + b[p, pl.ds(low + 1, rows), :])
        wym = plane * (here + b[p, pl.ds(low - 1, rows), :])
        wzp = upright * (here + jnp.where(lane < 127, pltpu.roll(here, 127, 1), 0.0))
        wzm = upright * (here + jnp.where(lane > 0, pltpu.roll(here, 1, 1), 0.0))
        return wxp, wyp, jnp.where(lane < 127, wzp, 0.0), wxp + wxm + wyp + wym + wzp + wzm

    def prepare(refs, pair, rows, first, own, scale):
        masked, wx, wy, wz, diag, inv = refs
        shift_at, beta_at = pair

        def clean(p):
            ok = inside(p, rows, 8, first, 10, own[0], own[1])
            masked[p, pl.ds(8, rows), :] = jnp.where(ok, beta_at(p), 0.0)

        def fill(p):
            wxp, wyp, wzp, total = weights(masked, p, 8, rows, 0.5 * scale, 0.5 * VERTICAL)
            total = total + shift_at(p)
            wx[p, pl.ds(8, rows), :] = wxp
            wy[p, pl.ds(8, rows), :] = wyp
            wz[p, pl.ds(8, rows), :] = wzp
            diag[p, pl.ds(8, rows), :] = total
            ok = inside(p, rows, 8, first, 10, own[0], own[1])
            inv[p, pl.ds(8, rows), :] = jnp.where(ok, 1.0 / total, 0.0)

        loop(0, 10, clean)
        loop(1, 9, fill)

    def coarsen_rows(ref, at, rows):
        even = ref[at, pl.ds(EDGE, rows // 2, stride=2), :]
        return 0.25 * (even + ref[at, pl.ds(EDGE + 1, rows // 2, stride=2), :])

    geo_fields = windows(near, 4, 32, 3, 3)
    geo_coarse2 = windows(wide, 2, 16, 4, 3)
    geo_coarse3, geo_middle3, geo_outer3 = (windows(part, 1, 8, 7, 7) for part in (wide, middle, outer))
    geo_rhs3 = windows(far, 1, 8, 7, 7)
    geo_iter1 = windows(near, 4, 32, 3, 2)
    geo_rhs2 = windows(near, 2, 16, 4, 2)
    for load in loads:
        load.wait()
    pl.semaphore_wait(barrier, len(partners))
    send(0, fields, geo_fields, True)

    for n, level in ((0, 1), (1, 2)):
        for q in range(2):
            both = fields[1 + n, 3 + 2 * q, pl.ds(EDGE, 32), :] + fields[1 + n, 4 + 2 * q, pl.ds(EDGE, 32), :]
            near1[q, pl.ds(EDGE, 32), :] = both
            coarse2[n, 4 + q, pl.ds(EDGE, 16), :] = coarsen_rows(near1, q, 32)
        near2[0, pl.ds(EDGE, 16), :] = coarse2[n, 4, pl.ds(EDGE, 16), :] + coarse2[n, 5, pl.ds(EDGE, 16), :]
        coarse3[n, 7, pl.ds(EDGE, 8), :] = coarsen_rows(near2, 0, 16)
    shift_own, beta_own = coarse3[0, 7, pl.ds(EDGE, 8), :], coarse3[1, 7, pl.ds(EDGE, 8), :]
    around = pltpu.roll(beta_own, 1, 0) + pltpu.roll(beta_own, 7, 0) + pltpu.roll(beta_own, 1, 1) + pltpu.roll(beta_own, 127, 1)
    bound = jnp.max(shift_own + PLANE_SCALES[2] * (6.0 * beta_own + 1.5 * around))
    bound_y[0] = jnp.full((1, 128), bound, jnp.float32)

    spread(7, bound_y, over_y)
    send(1, coarse2, geo_coarse2, True)
    send(2, coarse3, geo_coarse3, True)

    wait(recv_sem, 0, tiles_of(geo_fields, 3))
    send(11, coarse3, geo_middle3, True)
    level1 = (masked1, wx1, wy1, wz1, diag1, inv1)
    prepare(
        level1, (lambda p: fields[1, p, pl.ds(8, 48), :], lambda p: fields[2, p, pl.ds(8, 48), :]), 48, 3, (4, 32), PLANE_SCALES[0]
    )

    def first_step(step, inv, value, rows):
        def body(p):
            step[p, pl.ds(8, rows), :] = FIRST * value(p) * inv[p, pl.ds(8, rows), :]

        return body

    def smooth(step, wx, wy, wz, inv, p, low, rows):
        part = off(step, wx, wy, wz, p, low, rows)
        return KEEP * step[p, pl.ds(low, rows), :] + SECOND * inv[p, pl.ds(low, rows), :] * part

    loop(1, 9, first_step(step1, inv1, lambda p: fields[0, p, pl.ds(8, 48), :], 48))

    def presmooth1(p):
        near1[p, pl.ds(8, 48), :] = smooth(step1, wx1, wy1, wz1, inv1, p, 8, 48)

    loop(2, 8, presmooth1)

    def residual(f, v, level, p, low, rows):
        _, wx, wy, wz, diag, _ = level
        value = f(p, low, rows) - diag[p, pl.ds(low, rows), :] * v[p, pl.ds(low, rows), :]
        return value + off(v, wx, wy, wz, p, low, rows)

    def source_at(p, low, rows):
        return fields[0, p, pl.ds(low, rows), :]

    def rhs2_at(p, low, rows):
        return rhs2[p, pl.ds(low, rows), :]

    def restrict1(q):
        both = residual(source_at, near1, level1, 3 + 2 * q, EDGE, 32) + residual(source_at, near1, level1, 4 + 2 * q, EDGE, 32)
        start1[q, pl.ds(EDGE, 32), :] = both
        rhs2[4 + q, pl.ds(EDGE, 16), :] = coarsen_rows(start1, q, 32)

    loop(0, 2, restrict1)
    send(3, rhs2, geo_rhs2, False)

    def keep1(p):
        iter1[p, pl.ds(EDGE, 32), :] = near1[p, pl.ds(EDGE, 32), :]

    loop(3, 7, keep1)
    send(4, iter1, geo_iter1, False)

    send(13, coarse3, geo_outer3, True)
    wait_spread(recv_sem, 7, bound_y, ny)
    bound_x[0] = functools.reduce(jnp.maximum, [bound_y[n] for n in range(ny)])
    spread(8, bound_x, over_x)
    wait(recv_sem, 1, tiles_of(geo_coarse2, 2))
    level2 = (masked2, wx2, wy2, wz2, diag2, inv2)
    prepare(
        level2, (lambda p: coarse2[0, p, pl.ds(8, 32), :], lambda p: coarse2[1, p, pl.ds(8, 32), :]), 32, 4, (2, 16), PLANE_SCALES[1]
    )
    wait(recv_sem, 3, tiles_of(geo_rhs2, 1))
    loop(2, 8, first_step(step2, inv2, lambda p: rhs2_at(p, 8, 32), 32))

    def presmooth2(p):
        near2[p, pl.ds(8, 32), :] = smooth(step2, wx2, wy2, wz2, inv2, p, 8, 32)

    loop(3, 7, presmooth2)
    both = residual(rhs2_at, near2, level2, 4, EDGE, 16) + residual(rhs2_at, near2, level2, 5, EDGE, 16)
    start2[0, pl.ds(EDGE, 16), :] = both
    rhs3[7, pl.ds(EDGE, 8), :] = coarsen_rows(start2, 0, 16)
    send(5, rhs3, geo_rhs3, False)
    for p in (4, 5):
        iter2[p, pl.ds(EDGE, 16), :] = near2[p, pl.ds(EDGE, 16), :]
    send(6, iter2, geo_coarse2, False)

    wait(recv_sem, 2, tiles_of(geo_coarse3, 2))
    wait(recv_sem, 11, tiles_of(geo_middle3, 2))
    wait(recv_sem, 13, tiles_of(geo_outer3, 2))
    wait_spread(recv_sem, 8, bound_x, nx)
    scale = 2.0 / functools.reduce(jnp.maximum, [bound_x[n] for n in range(nx)])

    def clean3(p):
        ok = inside(p, 24, 8, 7, 15, 1, 8)
        masked3[p, pl.ds(8, 24), :] = jnp.where(ok, coarse3[1, p, pl.ds(8, 24), :], 0.0)

    loop(0, 15, clean3)
    wx3[0, pl.ds(8, 24), :] = (PLANE_SCALES[2] * scale) * (masked3[0, pl.ds(8, 24), :] + masked3[1, pl.ds(8, 24), :])

    def fill3(p):
        wxp, wyp, wzp, total = weights(masked3, p, 8, 24, PLANE_SCALES[2] * scale, VERTICAL * scale)
        total = total + 2.0 * scale * coarse3[0, p, pl.ds(8, 24), :]
        wx3[p, pl.ds(8, 24), :] = wxp
        wy3[p, pl.ds(8, 24), :] = wyp
        wz3[p, pl.ds(8, 24), :] = wzp
        ok = inside(p, 24, 8, 7, 15, 1, 8)
        own3[p, pl.ds(8, 24), :] = jnp.where(ok, total - 2.0, 0.0)
        inside3[p, pl.ds(8, 24), :] = jnp.where(ok, 1.0, 0.0)

    loop(1, 14, fill3)
    wait(recv_sem, 5, tiles_of(geo_rhs3, 1))

    def begin3(p):
        ok = inside(p, 24, 8, 7, 15, 1, 8)
        basis[0, p, pl.ds(8, 24), :] = jnp.where(ok, rhs3[p, pl.ds(8, 24), :], 0.0)

    loop(0, 15, begin3)

    def doubled(v, p, low, rows):
        value = own3[p, pl.ds(low, rows), :] * v[p, pl.ds(low, rows), :]
        return value - inside3[p, pl.ds(low, rows), :] * off(v, wx3, wy3, wz3, p, low, rows)

    for k in range(ITERS):
        low, rows, reach = (8, 24, 6 - k) if k < ITERS - 1 else (EDGE, 8, 0)

        def advance(p, k=k, low=low, rows=rows):
            value = doubled(basis.at[k], p, low, rows)
            value = 0.5 * value if k == 0 else value - basis[k - 1, p, pl.ds(low, rows), :]
            basis[k + 1, p, pl.ds(low, rows), :] = value

        loop(7 - reach, 8 + reach, advance)

    own = [basis[k, 7, pl.ds(EDGE, 8), :] for k in range(ITERS + 1)]
    parts = [halves(v) for v in own]
    for n, (i, j) in enumerate(PAIRS):
        high, low = two_prod(own[i], own[j], parts[i], parts[j])
        pair_high[pl.ds(8 * n, 8), :] = high
        pair_low[pl.ds(8 * n, 8), :] = low
    for n in range(len(PAIRS), ROWS):
        pair_high[pl.ds(8 * n, 8), :] = jnp.zeros((8, 128), jnp.float32)
        pair_low[pl.ds(8 * n, 8), :] = jnp.zeros((8, 128), jnp.float32)

    def merge(a, b):
        s, t = two_sum(a[0], b[0])
        return s, t + (a[1] + b[1])

    def tree(terms):
        while len(terms) > 1:
            terms = [merge(terms[i], terms[i + 1]) if i + 1 < len(terms) else terms[i] for i in range(0, len(terms), 2)]
        return terms[0]

    sums = tree([(pair_high[pl.ds(s, ROWS, stride=8), :], pair_low[pl.ds(s, ROWS, stride=8), :]) for s in range(8)])
    for d in (64, 32, 16, 8, 4, 2, 1):
        sums = merge(sums, (pltpu.roll(sums[0], d, 1), pltpu.roll(sums[1], d, 1)))
    lane, row = lane_of((ROWS, 128)), lax.broadcasted_iota(jnp.int32, (ROWS, 128), 0)
    line = jnp.where(lane == row, sums[0], jnp.where(lane == row + 64, sums[1], 0.0))
    gram_y[0] = jnp.sum(line, axis=0, keepdims=True)

    def total_of(ref, count):
        zero = jnp.zeros((1, 128), jnp.float32)
        s, t = tree([(ref[n], zero) for n in range(count)])
        return s + jnp.where(lane_of((1, 128)) >= 64, pltpu.roll(t, 64, 1), 0.0)

    spread(9, gram_y, over_y)
    wait_spread(recv_sem, 9, gram_y, ny)
    gram_x[0] = total_of(gram_y, ny)
    spread(10, gram_x, over_x)
    wait(recv_sem, 4, tiles_of(geo_iter1, 1))
    wait(recv_sem, 6, tiles_of(geo_coarse2, 1))
    wait_spread(recv_sem, 10, gram_x, nx)
    entries = jnp.broadcast_to(total_of(gram_x, nx), (2 * ROWS, 128))
    lane, row = lane_of((2 * ROWS, 128)), lax.broadcasted_iota(jnp.int32, (2 * ROWS, 128), 0)
    place = jnp.where(row < ROWS, row, row + (64 - ROWS))
    column = jnp.sum(jnp.where(lane == place, entries, 0.0), axis=1, keepdims=True)
    scalars[...] = jnp.broadcast_to(column, (2 * ROWS, 128))

    def gram(i, j):
        n = SLOT[(min(i, j), max(i, j))]
        return scalars[pl.ds(n, 1), :], scalars[pl.ds(ROWS + n, 1), :]

    answer = [value * scale for value in gradient_coefficients(gram)]

    for n in range(5):
        p = 5 + n
        total = answer[0] * basis[0, p, pl.ds(8, 24), :]
        for k in range(1, ITERS):
            total = total + answer[k] * basis[k, p, pl.ds(8, 24), :]
        sol3[n, pl.ds(8, 24), :] = total

    def prolong2(p):
        value = sol3[p // 2, pl.ds(12, 16), :]
        start2[p, pl.ds(8, 16, stride=2), :] = value
        start2[p, pl.ds(9, 16, stride=2), :] = value
        ok = inside(p, 32, 8, 4, 10, 2, 16)
        start2[p, pl.ds(8, 32), :] = jnp.where(ok, start2[p, pl.ds(8, 32), :] + iter2[p, pl.ds(8, 32), :], 0.0)

    loop(1, 9, prolong2)
    loop(2, 8, first_step(step2, inv2, lambda p: residual(rhs2_at, start2, level2, p, 8, 32), 32))

    def post2(p):
        sum2[p, pl.ds(8, 32), :] = start2[p, pl.ds(8, 32), :] + smooth(step2, wx2, wy2, wz2, inv2, p, 8, 32)

    loop(3, 7, post2)

    def prolong1(p):
        value = sum2[(p + 5) // 2, pl.ds(12, 24), :]
        start1[p, pl.ds(8, 24, stride=2), :] = value
        start1[p, pl.ds(9, 24, stride=2), :] = value
        ok = inside(p, 48, 8, 3, 10, 4, 32)
        start1[p, pl.ds(8, 48), :] = jnp.where(ok, start1[p, pl.ds(8, 48), :] + iter1[p, pl.ds(8, 48), :], 0.0)

    loop(1, 9, prolong1)
    loop(2, 8, first_step(step1, inv1, lambda p: residual(source_at, start1, level1, p, 8, 48), 48))

    def post1(p):
        out[p - 3] = start1[p, pl.ds(EDGE, 32), :] + smooth(step1, wx1, wy1, wz1, inv1, p, EDGE, 32)

    loop(3, 7, post1)

    wait(send_sem, 0, tiles_of(geo_fields, 3))
    wait(send_sem, 1, tiles_of(geo_coarse2, 2))
    wait(send_sem, 2, tiles_of(geo_coarse3, 2))
    wait(send_sem, 11, tiles_of(geo_middle3, 2))
    wait(send_sem, 13, tiles_of(geo_outer3, 2))
    wait(send_sem, 3, tiles_of(geo_rhs2, 1))
    wait(send_sem, 4, tiles_of(geo_iter1, 1))
    wait(send_sem, 5, tiles_of(geo_rhs3, 1))
    wait(send_sem, 6, tiles_of(geo_coarse2, 1))
    wait_spread(send_sem, 7, bound_y, ny)
    wait_spread(send_sem, 8, bound_x, nx)
    wait_spread(send_sem, 9, gram_y, ny)
    wait_spread(send_sem, 10, gram_x, nx)


def solution(mesh):
    nx, ny = mesh.shape["gx"], mesh.shape["gy"]

    def vmem(*shape):
        return pltpu.VMEM(shape, jnp.float32)

    one = [vmem(10, 64, 128)] * 10
    two = [vmem(10, 48, 128)] * 11
    three = [vmem(15, 40, 128)] * 6 + [vmem(ITERS + 1, 15, 40, 128), vmem(5, 40, 128)]

    def on_device(source, beta, shift):
        return pl.pallas_call(
            functools.partial(kernel, (nx, ny)),
            out_shape=jax.ShapeDtypeStruct(source.shape, jnp.float32),
            in_specs=[pl.BlockSpec(memory_space=pl.ANY)] * 3,
            out_specs=pl.BlockSpec(memory_space=pltpu.VMEM),
            scratch_shapes=[
                vmem(3, 10, 64, 128), vmem(2, 10, 48, 128), vmem(2, 15, 40, 128), vmem(10, 48, 128), vmem(15, 40, 128),
                *one, *two, *three,
                vmem(8 * ROWS, 128), vmem(8 * ROWS, 128),
                vmem(ny, 1, 128), vmem(nx, 1, 128), vmem(ny, 1, 128), vmem(nx, 1, 128),
                vmem(2 * ROWS, 128), vmem(140, 8, 128),
                pltpu.SemaphoreType.DMA((3,)), pltpu.SemaphoreType.DMA((15,)), pltpu.SemaphoreType.DMA((15,)),
            ],
            compiler_params=pltpu.CompilerParams(collective_id=0, has_side_effects=True, vmem_limit_bytes=40 * 2**20),
        )(*[pltpu.with_memory_space_constraint(x, pltpu.HBM) for x in (source, beta, shift)])

    placed = P("gx", "gy", None)
    return jax.shard_map(on_device, mesh=mesh, in_specs=(placed,) * 3, out_specs=placed, check_vma=False)
```

```python
import functools

import jax
import jax.numpy as jnp
from jax import lax
from jax.experimental import pallas as pl
from jax.experimental.pallas import tpu as pltpu
from jax.sharding import PartitionSpec as P

MESH = pl.DeviceIdType.MESH
ITERS = 6
FIRST = 1.0 / 1.2
CARRY = 2.0 / 7.0
SECOND = 0.75 / 0.7
KEEP = 1.0 + CARRY + SECOND * (1.0 - FIRST) / FIRST
VERTICAL = 1.0 / 16.0
PLANE_SCALES = (1.0, 0.25, 0.0625)
EDGE = 16
SPLIT = 4097.0

PAIRS = [(i, j) for i in range(ITERS) for j in range(i, ITERS)] + [(ITERS - 1, ITERS)]
SLOT = {pair: n for n, pair in enumerate(PAIRS)}
ROWS = 24


def two_sum(a, b):
    s = a + b
    t = s - a
    return s, (a - (s - t)) + (b - t)


def fast_two_sum(a, b):
    s = a + b
    return s, b - (s - a)


def halves(a):
    t = SPLIT * a
    high = t - (t - a)
    return high, a - high


def two_prod(a, b, a_halves=None, b_halves=None):
    ah, al = halves(a) if a_halves is None else a_halves
    bh, bl = halves(b) if b_halves is None else b_halves
    p = a * b
    return p, ((ah * bh - p) + ah * bl + al * bh) + al * bl


def dd_add(a, b):
    s, t = two_sum(a[0], b[0])
    return fast_two_sum(s, t + (a[1] + b[1]))


def dd_mul(a, b):
    p, t = two_prod(a[0], b[0])
    return fast_two_sum(p, t + (a[0] * b[1] + a[1] * b[0]))


def dd_neg(a):
    return -a[0], -a[1]


def dd_half(a):
    return 0.5 * a[0], 0.5 * a[1]


def dd_div(a, b):
    q = a[0] / b[0]
    p, t = two_prod(q, b[0])
    rest = ((a[0] - p) - t) + (a[1] - q * b[1])
    return fast_two_sum(q, rest / b[0])


def dd_dot(us, ws):
    terms = [dd_mul(u, w) for u, w in zip(us, ws)]
    while len(terms) > 1:
        terms = [dd_add(terms[i], terms[i + 1]) if i + 1 < len(terms) else terms[i] for i in range(0, len(terms), 2)]
    return terms[0]


def gradient_coefficients(gram):
    one = (jnp.ones_like(gram(0, 0)[0]), jnp.zeros_like(gram(0, 0)[0]))
    residual, direction, answer = [one], [one], [None] * ITERS
    norm_now = gram(0, 0)
    for turn in range(ITERS):
        image = []
        for k in range(turn + 2):
            terms = [direction[k]] if k <= turn else []
            if k >= 1:
                terms.append(direction[0] if k == 1 else dd_half(direction[k - 1]))
            if k + 1 <= turn:
                terms.append(dd_half(direction[k + 1]))
            total = terms[0]
            for term in terms[1:]:
                total = dd_add(total, term)
            image.append(total)
        along = dd_mul(direction[turn], dd_dot(image, [gram(i, turn) for i in range(turn + 2)]))
        alpha = dd_div(norm_now, along)
        for k in range(turn + 1):
            step = dd_mul(alpha, direction[k])
            answer[k] = step if answer[k] is None else dd_add(answer[k], step)
        if turn + 1 == ITERS:
            break
        less = dd_neg(alpha)
        steps = [dd_mul(less, value) for value in image]
        residual = [dd_add(residual[k], steps[k]) if k <= turn else steps[k] for k in range(turn + 2)]
        norm_next = dd_mul(residual[turn + 1], dd_dot(residual, [gram(i, turn + 1) for i in range(turn + 2)]))
        beta = dd_div(norm_next, norm_now)
        norm_now = norm_next
        direction = [dd_add(residual[k], dd_mul(beta, direction[k])) if k <= turn else residual[k] for k in range(turn + 2)]
    return [value[0] + value[1] for value in answer]


def loop(low, high, body):
    def step(p, carry):
        body(p)
        return carry

    for p in range(low, high):
        body(p)


def lane_of(shape):
    return lax.broadcasted_iota(jnp.int32, shape, len(shape) - 1)


def box(reach, width):
    return [(i, j) for i in range(-reach, reach + 1) for j in range(-width, width + 1) if (i, j) != (0, 0)]


def ring(count, size):
    far = sorted(range(1, count), key=lambda d: -min(d, count - d))
    return [((d, 0) if size else (0, d)) for d in far]


def windows(offsets, count, rows, first, reach):
    out = []
    for dx, dy in sorted(offsets, key=lambda o: -abs(o[0]) - abs(o[1])):
        if dx == 0:
            start, planes, target = 0, count, first
        elif dx > 0:
            start = max(0, dx * count - reach)
            planes, target = count - start, first - dx * count + start
        else:
            start, planes = 0, min(count, reach + (dx + 1) * count)
            target = first - dx * count
        edge = 4 if count == 1 and abs(dx) > 3 else 8
        row, high, to = (EDGE, rows, EDGE) if dy == 0 else (EDGE + rows - edge, edge, EDGE - edge) if dy > 0 else (EDGE, edge, EDGE + rows)
        out.append((dx, dy, first + start, target, planes, row, to, high))
    return out


def tiles_of(geometry, fields):
    return fields * sum(w[4] * w[7] for w in geometry) // 8


def kernel(
    counts, source, beta, shift, out,
    fields, coarse2, coarse3, rhs2, rhs3,
    masked1, wx1, wy1, wz1, diag1, inv1, step1, near1, iter1, start1,
    masked2, wx2, wy2, wz2, diag2, inv2, step2, near2, iter2, start2, sum2,
    masked3, wx3, wy3, wz3, own3, inside3, basis, sol3,
    pair_high, pair_low, bound_y, few, more, gram_y, gram_x, scalars, dummy,
    load_sem, send_sem, recv_sem,
):
    nx, ny = counts
    gx, gy = lax.axis_index("gx"), lax.axis_index("gy")

    def device(dx, dy):
        return lax.rem(gx + (dx + nx), nx), lax.rem(gy + (dy + ny), ny)

    near, wide, far = box(1, 1), box(2, 1), box(7, 1)
    over_y = ring(ny, 0)
    over_z = [(2 * n, 0) for n, _ in ring(nx // 2, 1)]
    along_x = [(d, 0) for d in range(-8, 9) if d]
    few_x = [(d, 0) for n in range(6, 0, -1) for d in (n, -n)]
    more_x = [(13, 0), (-13, 0)]
    middle = [o for o in far if 3 <= abs(o[0]) <= 4]
    outer = [o for o in far if abs(o[0]) > 4]

    loads = [
        pltpu.make_async_copy(ref, fields.at[n, pl.ds(3, 4), pl.ds(EDGE, 32)], load_sem.at[n])
        for n, ref in enumerate((source, shift, beta))
    ]
    for load in loads:
        load.start()

    partners = sorted({(dx % nx, dy % ny) for dx, dy in wide + over_y + along_x}, key=lambda o: min(o[0], nx - o[0]) + min(o[1], ny - o[1]))
    barrier = pltpu.get_barrier_semaphore()
    for dx, dy in partners:
        pl.semaphore_signal(barrier, 1, device_id=device(-dx, -dy), device_id_type=MESH)

    def send(phase, ref, geometry, stacked):
        for dx, dy, plane, target, planes, row, to, high in geometry:
            here, there = (pl.ds(plane, planes), pl.ds(row, high)), (pl.ds(target, planes), pl.ds(to, high))
            if stacked:
                here, there = (slice(None), *here), (slice(None), *there)
            pltpu.make_async_remote_copy(
                src_ref=ref.at[here], dst_ref=ref.at[there], send_sem=send_sem.at[phase], recv_sem=recv_sem.at[phase],
                device_id=device(dx, dy), device_id_type=MESH,
            ).start()

    def wait(sems, phase, tiles):
        part = dummy.at[pl.ds(0, tiles)]
        pltpu.make_async_copy(part, part, sems.at[phase]).wait()

    def spread(phase, ref, offsets, slots=None):
        for n, (dx, dy) in enumerate(offsets):
            pltpu.make_async_remote_copy(
                src_ref=ref.at[0], dst_ref=ref.at[max(dx, dy) if slots is None else slots[n]], send_sem=send_sem.at[phase], recv_sem=recv_sem.at[phase],
                device_id=device(dx, dy), device_id_type=MESH,
            ).start()

    def wait_spread(sems, phase, ref, count):
        part = ref.at[pl.ds(1, count - 1)]
        pltpu.make_async_copy(part, part, sems.at[phase]).wait()

    def inside(p, rows, low, first, count, own_planes, own_rows):
        plane = gx * own_planes + (p - first)
        row = gy * own_rows + (low - EDGE) + lax.broadcasted_iota(jnp.int32, (rows, 128), 0)
        fits = jnp.logical_and(plane >= 0, plane < nx * own_planes).astype(jnp.int32)
        return jnp.where(jnp.logical_and(row >= 0, row < ny * own_rows), fits, 0) > 0

    def off(v, wx, wy, wz, p, low, rows):
        here = v[p, pl.ds(low, rows), :]
        up = wz[p, pl.ds(low, rows), :]
        total = wx[p, pl.ds(low, rows), :] * v[p + 1, pl.ds(low, rows), :]
        total = total + wx[p - 1, pl.ds(low, rows), :] * v[p - 1, pl.ds(low, rows), :]
        total = total + wy[p, pl.ds(low, rows), :] * v[p, pl.ds(low + 1, rows), :]
        total = total + wy[p, pl.ds(low - 1, rows), :] * v[p, pl.ds(low - 1, rows), :]
        total = total + up * pltpu.roll(here, 127, 1)
        return total + pltpu.roll(up * here, 1, 1)

    def weights(b, p, low, rows, plane, upright):
        here = b[p, pl.ds(low, rows), :]
        lane = lane_of((rows, 128))
        wxp = plane * (here + b[p + 1, pl.ds(low, rows), :])
        wxm = plane * (here + b[p - 1, pl.ds(low, rows), :])
        wyp = plane * (here + b[p, pl.ds(low + 1, rows), :])
        wym = plane * (here + b[p, pl.ds(low - 1, rows), :])
        wzp = upright * (here + jnp.where(lane < 127, pltpu.roll(here, 127, 1), 0.0))
        wzm = upright * (here + jnp.where(lane > 0, pltpu.roll(here, 1, 1), 0.0))
        return wxp, wyp, jnp.where(lane < 127, wzp, 0.0), wxp + wxm + wyp + wym + wzp + wzm

    def prepare(refs, pair, rows, first, own, scale):
        masked, wx, wy, wz, diag, inv = refs
        shift_at, beta_at = pair

        def clean(p):
            ok = inside(p, rows, 8, first, 10, own[0], own[1])
            masked[p, pl.ds(8, rows), :] = jnp.where(ok, beta_at(p), 0.0)

        def fill(p):
            wxp, wyp, wzp, total = weights(masked, p, 8, rows, 0.5 * scale, 0.5 * VERTICAL)
            total = total + shift_at(p)
            wx[p, pl.ds(8, rows), :] = wxp
            wy[p, pl.ds(8, rows), :] = wyp
            wz[p, pl.ds(8, rows), :] = wzp
            diag[p, pl.ds(8, rows), :] = total
            ok = inside(p, rows, 8, first, 10, own[0], own[1])
            inv[p, pl.ds(8, rows), :] = jnp.where(ok, 1.0 / total, 0.0)

        loop(0, 10, clean)
        loop(1, 9, fill)

    def coarsen_rows(ref, at, rows):
        even = ref[at, pl.ds(EDGE, rows // 2, stride=2), :]
        return 0.25 * (even + ref[at, pl.ds(EDGE + 1, rows // 2, stride=2), :])

    geo_fields = windows(near, 4, 32, 3, 3)
    geo_coarse2 = windows(wide, 2, 16, 4, 3)
    geo_coarse3, geo_middle3, geo_outer3 = (windows(part, 1, 8, 7, 7) for part in (wide, middle, outer))
    geo_rhs3 = windows(far, 1, 8, 7, 7)
    geo_iter1 = windows(near, 4, 32, 3, 2)
    geo_rhs2 = windows(near, 2, 16, 4, 2)
    for load in loads:
        load.wait()
    pl.semaphore_wait(barrier, len(partners))
    send(0, fields, geo_fields, True)

    for n, level in ((0, 1), (1, 2)):
        for q in range(2):
            both = fields[1 + n, 3 + 2 * q, pl.ds(EDGE, 32), :] + fields[1 + n, 4 + 2 * q, pl.ds(EDGE, 32), :]
            near1[q, pl.ds(EDGE, 32), :] = both
            coarse2[n, 4 + q, pl.ds(EDGE, 16), :] = coarsen_rows(near1, q, 32)
        near2[0, pl.ds(EDGE, 16), :] = coarse2[n, 4, pl.ds(EDGE, 16), :] + coarse2[n, 5, pl.ds(EDGE, 16), :]
        coarse3[n, 7, pl.ds(EDGE, 8), :] = coarsen_rows(near2, 0, 16)
    shift_own, beta_own = coarse3[0, 7, pl.ds(EDGE, 8), :], coarse3[1, 7, pl.ds(EDGE, 8), :]
    around = pltpu.roll(beta_own, 1, 0) + pltpu.roll(beta_own, 7, 0) + pltpu.roll(beta_own, 1, 1) + pltpu.roll(beta_own, 127, 1)
    bound = jnp.max(shift_own + PLANE_SCALES[2] * (6.0 * beta_own + 1.5 * around))
    bound_y[0] = jnp.full((1, 128), bound, jnp.float32)

    spread(7, bound_y, over_y)
    send(1, coarse2, geo_coarse2, True)
    send(2, coarse3, geo_coarse3, True)

    wait(recv_sem, 0, tiles_of(geo_fields, 3))
    wait_spread(recv_sem, 7, bound_y, ny)
    few[0] = functools.reduce(jnp.maximum, [bound_y[n] for n in range(ny)])
    spread(8, few, few_x, range(1, 13))
    send(11, coarse3, geo_middle3, True)
    level1 = (masked1, wx1, wy1, wz1, diag1, inv1)
    prepare(
        level1, (lambda p: fields[1, p, pl.ds(8, 48), :], lambda p: fields[2, p, pl.ds(8, 48), :]), 48, 3, (4, 32), PLANE_SCALES[0]
    )

    def first_step(step, inv, value, rows):
        def body(p):
            step[p, pl.ds(8, rows), :] = FIRST * value(p) * inv[p, pl.ds(8, rows), :]

        return body

    def smooth(step, wx, wy, wz, inv, p, low, rows):
        part = off(step, wx, wy, wz, p, low, rows)
        return KEEP * step[p, pl.ds(low, rows), :] + SECOND * inv[p, pl.ds(low, rows), :] * part

    loop(1, 9, first_step(step1, inv1, lambda p: fields[0, p, pl.ds(8, 48), :], 48))

    def presmooth1(p):
        near1[p, pl.ds(8, 48), :] = smooth(step1, wx1, wy1, wz1, inv1, p, 8, 48)

    loop(2, 8, presmooth1)

    def residual(f, v, level, p, low, rows):
        _, wx, wy, wz, diag, _ = level
        value = f(p, low, rows) - diag[p, pl.ds(low, rows), :] * v[p, pl.ds(low, rows), :]
        return value + off(v, wx, wy, wz, p, low, rows)

    def source_at(p, low, rows):
        return fields[0, p, pl.ds(low, rows), :]

    def rhs2_at(p, low, rows):
        return rhs2[p, pl.ds(low, rows), :]

    def restrict1(q):
        both = residual(source_at, near1, level1, 3 + 2 * q, EDGE, 32) + residual(source_at, near1, level1, 4 + 2 * q, EDGE, 32)
        start1[q, pl.ds(EDGE, 32), :] = both
        rhs2[4 + q, pl.ds(EDGE, 16), :] = coarsen_rows(start1, q, 32)

    loop(0, 2, restrict1)
    send(3, rhs2, geo_rhs2, False)

    def keep1(p):
        iter1[p, pl.ds(EDGE, 32), :] = near1[p, pl.ds(EDGE, 32), :]

    loop(3, 7, keep1)
    send(4, iter1, geo_iter1, False)

    send(13, coarse3, geo_outer3, True)
    wait(recv_sem, 1, tiles_of(geo_coarse2, 2))
    level2 = (masked2, wx2, wy2, wz2, diag2, inv2)
    prepare(
        level2, (lambda p: coarse2[0, p, pl.ds(8, 32), :], lambda p: coarse2[1, p, pl.ds(8, 32), :]), 32, 4, (2, 16), PLANE_SCALES[1]
    )
    wait(recv_sem, 3, tiles_of(geo_rhs2, 1))
    loop(2, 8, first_step(step2, inv2, lambda p: rhs2_at(p, 8, 32), 32))

    def presmooth2(p):
        near2[p, pl.ds(8, 32), :] = smooth(step2, wx2, wy2, wz2, inv2, p, 8, 32)

    loop(3, 7, presmooth2)
    both = residual(rhs2_at, near2, level2, 4, EDGE, 16) + residual(rhs2_at, near2, level2, 5, EDGE, 16)
    start2[0, pl.ds(EDGE, 16), :] = both
    rhs3[7, pl.ds(EDGE, 8), :] = coarsen_rows(start2, 0, 16)
    send(5, rhs3, geo_rhs3, False)
    for p in (4, 5):
        iter2[p, pl.ds(EDGE, 16), :] = near2[p, pl.ds(EDGE, 16), :]
    send(6, iter2, geo_coarse2, False)

    wait_spread(recv_sem, 8, few, 13)
    more[0] = functools.reduce(jnp.maximum, [few[n] for n in range(13)])
    spread(12, more, more_x, range(1, 3))
    wait(recv_sem, 2, tiles_of(geo_coarse3, 2))
    wait(recv_sem, 11, tiles_of(geo_middle3, 2))
    wait(recv_sem, 13, tiles_of(geo_outer3, 2))
    wait_spread(recv_sem, 12, more, 3)
    scale = 2.0 / functools.reduce(jnp.maximum, [more[n] for n in range(3)])

    def clean3(p):
        ok = inside(p, 24, 8, 7, 15, 1, 8)
        masked3[p, pl.ds(8, 24), :] = jnp.where(ok, coarse3[1, p, pl.ds(8, 24), :], 0.0)

    loop(0, 15, clean3)
    wx3[0, pl.ds(8, 24), :] = (PLANE_SCALES[2] * scale) * (masked3[0, pl.ds(8, 24), :] + masked3[1, pl.ds(8, 24), :])

    def fill3(p):
        wxp, wyp, wzp, total = weights(masked3, p, 8, 24, PLANE_SCALES[2] * scale, VERTICAL * scale)
        total = total + 2.0 * scale * coarse3[0, p, pl.ds(8, 24), :]
        wx3[p, pl.ds(8, 24), :] = wxp
        wy3[p, pl.ds(8, 24), :] = wyp
        wz3[p, pl.ds(8, 24), :] = wzp
        ok = inside(p, 24, 8, 7, 15, 1, 8)
        own3[p, pl.ds(8, 24), :] = jnp.where(ok, total - 2.0, 0.0)
        inside3[p, pl.ds(8, 24), :] = jnp.where(ok, 1.0, 0.0)

    loop(1, 14, fill3)
    wait(recv_sem, 5, tiles_of(geo_rhs3, 1))

    def begin3(p):
        ok = inside(p, 24, 8, 7, 15, 1, 8)
        basis[0, p, pl.ds(8, 24), :] = jnp.where(ok, rhs3[p, pl.ds(8, 24), :], 0.0)

    loop(0, 15, begin3)

    def doubled(v, p, low, rows):
        value = own3[p, pl.ds(low, rows), :] * v[p, pl.ds(low, rows), :]
        return value - inside3[p, pl.ds(low, rows), :] * off(v, wx3, wy3, wz3, p, low, rows)

    for k in range(ITERS):
        low, rows, reach = (8, 24, 6 - k) if k < ITERS - 1 else (EDGE, 8, 0)

        def advance(p, k=k, low=low, rows=rows):
            value = doubled(basis.at[k], p, low, rows)
            value = 0.5 * value if k == 0 else value - basis[k - 1, p, pl.ds(low, rows), :]
            basis[k + 1, p, pl.ds(low, rows), :] = value

        loop(7 - reach, 8 + reach, advance)

    own = [basis[k, 7, pl.ds(EDGE, 8), :] for k in range(ITERS + 1)]
    parts = [halves(v) for v in own]
    for n, (i, j) in enumerate(PAIRS):
        high, low = two_prod(own[i], own[j], parts[i], parts[j])
        pair_high[pl.ds(8 * n, 8), :] = high
        pair_low[pl.ds(8 * n, 8), :] = low
    for n in range(len(PAIRS), ROWS):
        pair_high[pl.ds(8 * n, 8), :] = jnp.zeros((8, 128), jnp.float32)
        pair_low[pl.ds(8 * n, 8), :] = jnp.zeros((8, 128), jnp.float32)

    def merge(a, b):
        s, t = two_sum(a[0], b[0])
        return s, t + (a[1] + b[1])

    def tree(terms):
        while len(terms) > 1:
            terms = [merge(terms[i], terms[i + 1]) if i + 1 < len(terms) else terms[i] for i in range(0, len(terms), 2)]
        return terms[0]

    sums = tree([(pair_high[pl.ds(s, ROWS, stride=8), :], pair_low[pl.ds(s, ROWS, stride=8), :]) for s in range(8)])
    for d in (64, 32, 16, 8, 4, 2, 1):
        sums = merge(sums, (pltpu.roll(sums[0], d, 1), pltpu.roll(sums[1], d, 1)))
    lane, row = lane_of((ROWS, 128)), lax.broadcasted_iota(jnp.int32, (ROWS, 128), 0)
    line = jnp.where(lane == row, sums[0], jnp.where(lane == row + 64, sums[1], 0.0))
    gram_y[0] = jnp.sum(line, axis=0, keepdims=True)

    def total_of(ref, count):
        zero = jnp.zeros((1, 128), jnp.float32)
        s, t = tree([(ref[n], zero) for n in range(count)])
        return s + jnp.where(lane_of((1, 128)) >= 64, pltpu.roll(t, 64, 1), 0.0)

    sibling = gx + 1 - 2 * lax.rem(gx, 2)
    for column, y in [(n, dy) for _, dy in over_y + [(0, 0)] for n in (1, 0)]:
        if column or y:
            pltpu.make_async_remote_copy(
                src_ref=gram_y.at[0], dst_ref=gram_y.at[column * ny + y], send_sem=send_sem.at[9], recv_sem=recv_sem.at[9],
                device_id=(sibling if column else gx, device(0, y)[1]), device_id_type=MESH,
            ).start()
    wait_spread(recv_sem, 9, gram_y, 2 * ny)
    gram_x[0] = total_of(gram_y, 2 * ny)
    spread(10, gram_x, over_z, [n // 2 for n, _ in over_z])
    wait(recv_sem, 4, tiles_of(geo_iter1, 1))
    wait(recv_sem, 6, tiles_of(geo_coarse2, 1))
    wait_spread(recv_sem, 10, gram_x, nx // 2)
    entries = jnp.broadcast_to(total_of(gram_x, nx // 2), (2 * ROWS, 128))
    lane, row = lane_of((2 * ROWS, 128)), lax.broadcasted_iota(jnp.int32, (2 * ROWS, 128), 0)
    place = jnp.where(row < ROWS, row, row + (64 - ROWS))
    column = jnp.sum(jnp.where(lane == place, entries, 0.0), axis=1, keepdims=True)
    scalars[...] = jnp.broadcast_to(column, (2 * ROWS, 128))

    def gram(i, j):
        n = SLOT[(min(i, j), max(i, j))]
        return scalars[pl.ds(n, 1), :], scalars[pl.ds(ROWS + n, 1), :]

    answer = [value * scale for value in gradient_coefficients(gram)]

    for n in range(5):
        p = 5 + n
        total = answer[0] * basis[0, p, pl.ds(8, 24), :]
        for k in range(1, ITERS):
            total = total + answer[k] * basis[k, p, pl.ds(8, 24), :]
        sol3[n, pl.ds(8, 24), :] = total

    def prolong2(p):
        value = sol3[p // 2, pl.ds(12, 16), :]
        start2[p, pl.ds(8, 16, stride=2), :] = value
        start2[p, pl.ds(9, 16, stride=2), :] = value
        ok = inside(p, 32, 8, 4, 10, 2, 16)
        start2[p, pl.ds(8, 32), :] = jnp.where(ok, start2[p, pl.ds(8, 32), :] + iter2[p, pl.ds(8, 32), :], 0.0)

    loop(1, 9, prolong2)
    loop(2, 8, first_step(step2, inv2, lambda p: residual(rhs2_at, start2, level2, p, 8, 32), 32))

    def post2(p):
        sum2[p, pl.ds(8, 32), :] = start2[p, pl.ds(8, 32), :] + smooth(step2, wx2, wy2, wz2, inv2, p, 8, 32)

    loop(3, 7, post2)

    def prolong1(p):
        value = sum2[(p + 5) // 2, pl.ds(12, 24), :]
        start1[p, pl.ds(8, 24, stride=2), :] = value
        start1[p, pl.ds(9, 24, stride=2), :] = value
        ok = inside(p, 48, 8, 3, 10, 4, 32)
        start1[p, pl.ds(8, 48), :] = jnp.where(ok, start1[p, pl.ds(8, 48), :] + iter1[p, pl.ds(8, 48), :], 0.0)

    loop(1, 9, prolong1)
    loop(2, 8, first_step(step1, inv1, lambda p: residual(source_at, start1, level1, p, 8, 48), 48))

    def post1(p):
        out[p - 3] = start1[p, pl.ds(EDGE, 32), :] + smooth(step1, wx1, wy1, wz1, inv1, p, EDGE, 32)

    loop(3, 7, post1)

    wait(send_sem, 0, tiles_of(geo_fields, 3))
    wait(send_sem, 1, tiles_of(geo_coarse2, 2))
    wait(send_sem, 2, tiles_of(geo_coarse3, 2))
    wait(send_sem, 11, tiles_of(geo_middle3, 2))
    wait(send_sem, 13, tiles_of(geo_outer3, 2))
    wait(send_sem, 3, tiles_of(geo_rhs2, 1))
    wait(send_sem, 4, tiles_of(geo_iter1, 1))
    wait(send_sem, 5, tiles_of(geo_rhs3, 1))
    wait(send_sem, 6, tiles_of(geo_coarse2, 1))
    wait_spread(send_sem, 7, bound_y, ny)
    wait_spread(send_sem, 8, few, 13)
    wait_spread(send_sem, 12, more, 3)
    wait_spread(send_sem, 9, gram_y, 2 * ny)
    wait_spread(send_sem, 10, gram_x, nx // 2)


def solution(mesh):
    nx, ny = mesh.shape["gx"], mesh.shape["gy"]

    def vmem(*shape):
        return pltpu.VMEM(shape, jnp.float32)

    one = [vmem(10, 64, 128)] * 10
    two = [vmem(10, 48, 128)] * 11
    three = [vmem(15, 40, 128)] * 6 + [vmem(ITERS + 1, 15, 40, 128), vmem(5, 40, 128)]

    def on_device(source, beta, shift):
        return pl.pallas_call(
            functools.partial(kernel, (nx, ny)),
            out_shape=jax.ShapeDtypeStruct(source.shape, jnp.float32),
            in_specs=[pl.BlockSpec(memory_space=pl.ANY)] * 3,
            out_specs=pl.BlockSpec(memory_space=pltpu.VMEM),
            scratch_shapes=[
                vmem(3, 10, 64, 128), vmem(2, 10, 48, 128), vmem(2, 15, 40, 128), vmem(10, 48, 128), vmem(15, 40, 128),
                *one, *two, *three,
                vmem(8 * ROWS, 128), vmem(8 * ROWS, 128),
                vmem(ny, 1, 128), vmem(13, 1, 128), vmem(3, 1, 128), vmem(2 * ny, 1, 128), vmem(nx // 2, 1, 128),
                vmem(2 * ROWS, 128), vmem(140, 8, 128),
                pltpu.SemaphoreType.DMA((3,)), pltpu.SemaphoreType.DMA((15,)), pltpu.SemaphoreType.DMA((15,)),
            ],
            compiler_params=pltpu.CompilerParams(collective_id=0, has_side_effects=True, vmem_limit_bytes=40 * 2**20),
        )(*[pltpu.with_memory_space_constraint(x, pltpu.HBM) for x in (source, beta, shift)])

    placed = P("gx", "gy", None)
    return jax.shard_map(on_device, mesh=mesh, in_specs=(placed,) * 3, out_specs=placed, check_vma=False)
```

```python
import functools

import jax
import jax.numpy as jnp
from jax import lax
from jax.experimental import pallas as pl
from jax.experimental.pallas import tpu as pltpu
from jax.sharding import PartitionSpec as P

MESH = pl.DeviceIdType.MESH
ITERS = 6
FIRST = 1.0 / 1.2
CARRY = 2.0 / 7.0
SECOND = 0.75 / 0.7
KEEP = 1.0 + CARRY + SECOND * (1.0 - FIRST) / FIRST
VERTICAL = 1.0 / 16.0
PLANE_SCALES = (1.0, 0.25, 0.0625)
EDGE = 16
SPLIT = 4097.0
SOON = 2

PAIRS = [(i, j) for i in range(ITERS) for j in range(i, ITERS)] + [(ITERS - 1, ITERS)]
SLOT = {pair: n for n, pair in enumerate(PAIRS)}
ROWS = 24


def two_sum(a, b):
    s = a + b
    t = s - a
    return s, (a - (s - t)) + (b - t)


def fast_two_sum(a, b):
    s = a + b
    return s, b - (s - a)


def halves(a):
    t = SPLIT * a
    high = t - (t - a)
    return high, a - high


def two_prod(a, b, a_halves=None, b_halves=None):
    ah, al = halves(a) if a_halves is None else a_halves
    bh, bl = halves(b) if b_halves is None else b_halves
    p = a * b
    return p, ((ah * bh - p) + ah * bl + al * bh) + al * bl


def dd_add(a, b):
    s, t = two_sum(a[0], b[0])
    return fast_two_sum(s, t + (a[1] + b[1]))


def dd_mul(a, b):
    p, t = two_prod(a[0], b[0])
    return fast_two_sum(p, t + (a[0] * b[1] + a[1] * b[0]))


def dd_neg(a):
    return -a[0], -a[1]


def dd_half(a):
    return 0.5 * a[0], 0.5 * a[1]


def dd_div(a, b):
    q = a[0] / b[0]
    p, t = two_prod(q, b[0])
    rest = ((a[0] - p) - t) + (a[1] - q * b[1])
    return fast_two_sum(q, rest / b[0])


def dd_dot(us, ws):
    terms = [dd_mul(u, w) for u, w in zip(us, ws)]
    while len(terms) > 1:
        terms = [dd_add(terms[i], terms[i + 1]) if i + 1 < len(terms) else terms[i] for i in range(0, len(terms), 2)]
    return terms[0]


def gradient_coefficients(gram):
    one = (jnp.ones_like(gram(0, 0)[0]), jnp.zeros_like(gram(0, 0)[0]))
    residual, direction, answer = [one], [one], [None] * ITERS
    norm_now = gram(0, 0)
    for turn in range(ITERS):
        image = []
        for k in range(turn + 2):
            terms = [direction[k]] if k <= turn else []
            if k >= 1:
                terms.append(direction[0] if k == 1 else dd_half(direction[k - 1]))
            if k + 1 <= turn:
                terms.append(dd_half(direction[k + 1]))
            total = terms[0]
            for term in terms[1:]:
                total = dd_add(total, term)
            image.append(total)
        along = dd_mul(direction[turn], dd_dot(image, [gram(i, turn) for i in range(turn + 2)]))
        alpha = dd_div(norm_now, along)
        for k in range(turn + 1):
            step = dd_mul(alpha, direction[k])
            answer[k] = step if answer[k] is None else dd_add(answer[k], step)
        if turn + 1 == ITERS:
            break
        less = dd_neg(alpha)
        steps = [dd_mul(less, value) for value in image]
        residual = [dd_add(residual[k], steps[k]) if k <= turn else steps[k] for k in range(turn + 2)]
        norm_next = dd_mul(residual[turn + 1], dd_dot(residual, [gram(i, turn + 1) for i in range(turn + 2)]))
        beta = dd_div(norm_next, norm_now)
        norm_now = norm_next
        direction = [dd_add(residual[k], dd_mul(beta, direction[k])) if k <= turn else residual[k] for k in range(turn + 2)]
    return [value[0] + value[1] for value in answer]


def loop(low, high, body):
    def step(p, carry):
        body(p)
        return carry

    for p in range(low, high):
        body(p)


def lane_of(shape):
    return lax.broadcasted_iota(jnp.int32, shape, len(shape) - 1)


def box(reach, width):
    return [(i, j) for i in range(-reach, reach + 1) for j in range(-width, width + 1) if (i, j) != (0, 0)]


def ring(count, size):
    far = sorted(range(1, count), key=lambda d: -min(d, count - d))
    return [((d, 0) if size else (0, d)) for d in far]


def windows(offsets, count, rows, first, reach):
    out = []
    for dx, dy in sorted(offsets, key=lambda o: -abs(o[0]) - abs(o[1])):
        if dx == 0:
            start, planes, target = 0, count, first
        elif dx > 0:
            start = max(0, dx * count - reach)
            planes, target = count - start, first - dx * count + start
        else:
            start, planes = 0, min(count, reach + (dx + 1) * count)
            target = first - dx * count
        edge = 4 if count == 1 and abs(dx) > 3 else 8
        row, high, to = (EDGE, rows, EDGE) if dy == 0 else (EDGE + rows - edge, edge, EDGE - edge) if dy > 0 else (EDGE, edge, EDGE + rows)
        out.append((dx, dy, first + start, target, planes, row, to, high))
    return out


def tiles_of(geometry, fields):
    return fields * sum(w[4] * w[7] for w in geometry) // 8


def kernel(
    counts, source, beta, shift, out,
    fields, coarse2, coarse3, rhs2, rhs3,
    masked1, wx1, wy1, wz1, diag1, inv1, step1, near1, iter1, start1,
    masked2, wx2, wy2, wz2, diag2, inv2, step2, near2, iter2, start2, sum2,
    masked3, wx3, wy3, wz3, own3, inside3, basis, lifted,
    pair_high, pair_low, bound_y, few, more, gram_y, gram_x, scalars, dummy,
    load_sem, send_sem, recv_sem,
):
    nx, ny = counts
    gx, gy = lax.axis_index("gx"), lax.axis_index("gy")

    def device(dx, dy):
        return lax.rem(gx + (dx + nx), nx), lax.rem(gy + (dy + ny), ny)

    near, wide, far = box(1, 1), box(2, 1), box(7, 1)
    over_y = ring(ny, 0)
    over_z = [(2 * n, 0) for n, _ in ring(nx // 2, 1)]
    along_x = [(d, 0) for d in range(-8, 9) if d]
    few_x = [(d, 0) for n in range(6, 0, -1) for d in (n, -n)]
    more_x = [(13, 0), (-13, 0)]
    middle = [o for o in far if 3 <= abs(o[0]) <= 4]
    outer = [o for o in far if abs(o[0]) > 4]

    loads = [
        pltpu.make_async_copy(ref, fields.at[n, pl.ds(3, 4), pl.ds(EDGE, 32)], load_sem.at[n])
        for n, ref in enumerate((source, shift, beta))
    ]
    for load in loads:
        load.start()

    partners = sorted({(dx % nx, dy % ny) for dx, dy in wide + over_y + along_x}, key=lambda o: min(o[0], nx - o[0]) + min(o[1], ny - o[1]))
    barrier = pltpu.get_barrier_semaphore()
    for dx, dy in partners:
        pl.semaphore_signal(barrier, 1, device_id=device(-dx, -dy), device_id_type=MESH)

    def send(phase, ref, geometry, stacked):
        for dx, dy, plane, target, planes, row, to, high in geometry:
            here, there = (pl.ds(plane, planes), pl.ds(row, high)), (pl.ds(target, planes), pl.ds(to, high))
            if stacked:
                here, there = (slice(None), *here), (slice(None), *there)
            pltpu.make_async_remote_copy(
                src_ref=ref.at[here], dst_ref=ref.at[there], send_sem=send_sem.at[phase], recv_sem=recv_sem.at[phase],
                device_id=device(dx, dy), device_id_type=MESH,
            ).start()

    def wait(sems, phase, tiles):
        part = dummy.at[pl.ds(0, tiles)]
        pltpu.make_async_copy(part, part, sems.at[phase]).wait()

    def spread(phase, ref, offsets, slots=None):
        for n, (dx, dy) in enumerate(offsets):
            pltpu.make_async_remote_copy(
                src_ref=ref.at[0], dst_ref=ref.at[max(dx, dy) if slots is None else slots[n]], send_sem=send_sem.at[phase], recv_sem=recv_sem.at[phase],
                device_id=device(dx, dy), device_id_type=MESH,
            ).start()

    def wait_spread(sems, phase, ref, count):
        part = ref.at[pl.ds(1, count - 1)]
        pltpu.make_async_copy(part, part, sems.at[phase]).wait()

    def inside(p, rows, low, first, count, own_planes, own_rows):
        plane = gx * own_planes + (p - first)
        row = gy * own_rows + (low - EDGE) + lax.broadcasted_iota(jnp.int32, (rows, 128), 0)
        fits = jnp.logical_and(plane >= 0, plane < nx * own_planes).astype(jnp.int32)
        return jnp.where(jnp.logical_and(row >= 0, row < ny * own_rows), fits, 0) > 0

    def off(v, wx, wy, wz, p, low, rows):
        here = v[p, pl.ds(low, rows), :]
        up = wz[p, pl.ds(low, rows), :]
        total = wx[p, pl.ds(low, rows), :] * v[p + 1, pl.ds(low, rows), :]
        total = total + wx[p - 1, pl.ds(low, rows), :] * v[p - 1, pl.ds(low, rows), :]
        total = total + wy[p, pl.ds(low, rows), :] * v[p, pl.ds(low + 1, rows), :]
        total = total + wy[p, pl.ds(low - 1, rows), :] * v[p, pl.ds(low - 1, rows), :]
        total = total + up * pltpu.roll(here, 127, 1)
        return total + pltpu.roll(up * here, 1, 1)

    def weights(b, p, low, rows, plane, upright):
        here = b[p, pl.ds(low, rows), :]
        lane = lane_of((rows, 128))
        wxp = plane * (here + b[p + 1, pl.ds(low, rows), :])
        wxm = plane * (here + b[p - 1, pl.ds(low, rows), :])
        wyp = plane * (here + b[p, pl.ds(low + 1, rows), :])
        wym = plane * (here + b[p, pl.ds(low - 1, rows), :])
        wzp = upright * (here + jnp.where(lane < 127, pltpu.roll(here, 127, 1), 0.0))
        wzm = upright * (here + jnp.where(lane > 0, pltpu.roll(here, 1, 1), 0.0))
        return wxp, wyp, jnp.where(lane < 127, wzp, 0.0), wxp + wxm + wyp + wym + wzp + wzm

    def prepare(refs, pair, rows, first, own, scale):
        masked, wx, wy, wz, diag, inv = refs
        shift_at, beta_at = pair

        def clean(p):
            ok = inside(p, rows, 8, first, 10, own[0], own[1])
            masked[p, pl.ds(8, rows), :] = jnp.where(ok, beta_at(p), 0.0)

        def fill(p):
            wxp, wyp, wzp, total = weights(masked, p, 12, rows - 8, 0.5 * scale, 0.5 * VERTICAL)
            total = total + shift_at(p)
            wx[p, pl.ds(12, rows - 8), :] = wxp
            wy[p, pl.ds(12, rows - 8), :] = wyp
            wz[p, pl.ds(12, rows - 8), :] = wzp
            diag[p, pl.ds(12, rows - 8), :] = total
            ok = inside(p, rows - 8, 12, first, 10, own[0], own[1])
            inv[p, pl.ds(12, rows - 8), :] = jnp.where(ok, 1.0 / total, 0.0)

        loop(0, 10, clean)
        loop(1, 9, fill)

    def coarsen_rows(ref, at, rows):
        even = ref[at, pl.ds(EDGE, rows // 2, stride=2), :]
        return 0.25 * (even + ref[at, pl.ds(EDGE + 1, rows // 2, stride=2), :])

    geo_fields = windows(near, 4, 32, 3, 3)
    geo_coarse2 = windows(wide, 2, 16, 4, 3)
    geo_coarse3, geo_middle3, geo_outer3 = (windows(part, 1, 8, 7, 7) for part in (wide, middle, outer))
    geo_rhs3 = windows(far, 1, 8, 7, 7)
    geo_iter1 = windows(near, 4, 32, 3, 2)
    geo_rhs2 = windows(near, 2, 16, 4, 2)
    for load in loads:
        load.wait()
    pl.semaphore_wait(barrier, len(partners))
    send(0, fields, geo_fields, True)

    for n, level in ((0, 1), (1, 2)):
        for q in range(2):
            both = fields[1 + n, 3 + 2 * q, pl.ds(EDGE, 32), :] + fields[1 + n, 4 + 2 * q, pl.ds(EDGE, 32), :]
            near1[q, pl.ds(EDGE, 32), :] = both
            coarse2[n, 4 + q, pl.ds(EDGE, 16), :] = coarsen_rows(near1, q, 32)
        near2[0, pl.ds(EDGE, 16), :] = coarse2[n, 4, pl.ds(EDGE, 16), :] + coarse2[n, 5, pl.ds(EDGE, 16), :]
        coarse3[n, 7, pl.ds(EDGE, 8), :] = coarsen_rows(near2, 0, 16)
    shift_own, beta_own = coarse3[0, 7, pl.ds(EDGE, 8), :], coarse3[1, 7, pl.ds(EDGE, 8), :]
    around = pltpu.roll(beta_own, 1, 0) + pltpu.roll(beta_own, 7, 0) + pltpu.roll(beta_own, 1, 1) + pltpu.roll(beta_own, 127, 1)
    bound = jnp.max(shift_own + PLANE_SCALES[2] * (6.0 * beta_own + 1.5 * around))
    bound_y[0] = jnp.full((1, 128), bound, jnp.float32)

    spread(7, bound_y, over_y)
    send(1, coarse2, geo_coarse2, True)
    send(2, coarse3, geo_coarse3, True)

    wait(recv_sem, 0, tiles_of(geo_fields, 3))
    level1 = (masked1, wx1, wy1, wz1, diag1, inv1)
    prepare(
        level1, (lambda p: fields[1, p, pl.ds(12, 40), :], lambda p: fields[2, p, pl.ds(8, 48), :]), 48, 3, (4, 32), PLANE_SCALES[0]
    )

    def first_step(step, inv, value, rows):
        def body(p):
            step[p, pl.ds(12, rows), :] = FIRST * value(p) * inv[p, pl.ds(12, rows), :]

        return body

    def smooth(step, wx, wy, wz, inv, p, low, rows):
        part = off(step, wx, wy, wz, p, low, rows)
        return KEEP * step[p, pl.ds(low, rows), :] + SECOND * inv[p, pl.ds(low, rows), :] * part

    loop(1, 9, first_step(step1, inv1, lambda p: fields[0, p, pl.ds(12, 40), :], 40))

    def presmooth1(p):
        near1[p, pl.ds(12, 40), :] = smooth(step1, wx1, wy1, wz1, inv1, p, 12, 40)

    loop(2, 8, presmooth1)

    def residual(f, v, level, p, low, rows):
        _, wx, wy, wz, diag, _ = level
        value = f(p, low, rows) - diag[p, pl.ds(low, rows), :] * v[p, pl.ds(low, rows), :]
        return value + off(v, wx, wy, wz, p, low, rows)

    def source_at(p, low, rows):
        return fields[0, p, pl.ds(low, rows), :]

    def rhs2_at(p, low, rows):
        return rhs2[p, pl.ds(low, rows), :]

    def restrict1(q):
        both = residual(source_at, near1, level1, 3 + 2 * q, EDGE, 32) + residual(source_at, near1, level1, 4 + 2 * q, EDGE, 32)
        start1[q, pl.ds(EDGE, 32), :] = both
        rhs2[4 + q, pl.ds(EDGE, 16), :] = coarsen_rows(start1, q, 32)

    loop(0, 2, restrict1)
    send(3, rhs2, geo_rhs2, False)

    def keep1(p):
        iter1[p, pl.ds(EDGE, 32), :] = near1[p, pl.ds(EDGE, 32), :]

    loop(3, 7, keep1)
    send(4, iter1, geo_iter1, False)

    wait_spread(recv_sem, 7, bound_y, ny)
    few[0] = functools.reduce(jnp.maximum, [bound_y[n] for n in range(ny)])
    spread(8, few, few_x, range(1, 13))
    send(11, coarse3, geo_middle3, True)
    send(13, coarse3, geo_outer3, True)
    wait(recv_sem, 1, tiles_of(geo_coarse2, 2))
    level2 = (masked2, wx2, wy2, wz2, diag2, inv2)
    prepare(
        level2, (lambda p: coarse2[0, p, pl.ds(12, 24), :], lambda p: coarse2[1, p, pl.ds(8, 32), :]), 32, 4, (2, 16), PLANE_SCALES[1]
    )
    wait(recv_sem, 3, tiles_of(geo_rhs2, 1))
    loop(2, 8, first_step(step2, inv2, lambda p: rhs2_at(p, 12, 24), 24))

    def presmooth2(p):
        near2[p, pl.ds(12, 24), :] = smooth(step2, wx2, wy2, wz2, inv2, p, 12, 24)

    loop(3, 7, presmooth2)
    both = residual(rhs2_at, near2, level2, 4, EDGE, 16) + residual(rhs2_at, near2, level2, 5, EDGE, 16)
    start2[0, pl.ds(EDGE, 16), :] = both
    rhs3[7, pl.ds(EDGE, 8), :] = coarsen_rows(start2, 0, 16)
    send(5, rhs3, geo_rhs3, False)
    for p in (4, 5):
        iter2[p, pl.ds(EDGE, 16), :] = near2[p, pl.ds(EDGE, 16), :]
    send(6, iter2, geo_coarse2, False)

    wait_spread(recv_sem, 8, few, 13)
    more[0] = functools.reduce(jnp.maximum, [few[n] for n in range(13)])
    spread(12, more, more_x, range(1, 3))
    wait(recv_sem, 2, tiles_of(geo_coarse3, 2))
    wait(recv_sem, 11, tiles_of(geo_middle3, 2))
    wait(recv_sem, 13, tiles_of(geo_outer3, 2))
    wait_spread(recv_sem, 12, more, 3)
    scale = 2.0 / functools.reduce(jnp.maximum, [more[n] for n in range(3)])

    def clean3(p):
        ok = inside(p, 24, 8, 7, 15, 1, 8)
        masked3[p, pl.ds(8, 24), :] = jnp.where(ok, coarse3[1, p, pl.ds(8, 24), :], 0.0)

    loop(0, 15, clean3)
    wx3[0, pl.ds(8, 24), :] = (PLANE_SCALES[2] * scale) * (masked3[0, pl.ds(8, 24), :] + masked3[1, pl.ds(8, 24), :])

    def fill3(p):
        wxp, wyp, wzp, total = weights(masked3, p, 8, 24, PLANE_SCALES[2] * scale, VERTICAL * scale)
        total = total + 2.0 * scale * coarse3[0, p, pl.ds(8, 24), :]
        wx3[p, pl.ds(8, 24), :] = wxp
        wy3[p, pl.ds(8, 24), :] = wyp
        wz3[p, pl.ds(8, 24), :] = wzp
        ok = inside(p, 24, 8, 7, 15, 1, 8)
        own3[p, pl.ds(8, 24), :] = jnp.where(ok, total - 2.0, 0.0)
        inside3[p, pl.ds(8, 24), :] = jnp.where(ok, 1.0, 0.0)

    loop(1, 14, fill3)
    wait(recv_sem, 5, tiles_of(geo_rhs3, 1))

    def begin3(p):
        ok = inside(p, 24, 8, 7, 15, 1, 8)
        basis[0, p, pl.ds(8, 24), :] = jnp.where(ok, rhs3[p, pl.ds(8, 24), :], 0.0)

    loop(0, 15, begin3)

    def doubled(v, p, low, rows):
        value = own3[p, pl.ds(low, rows), :] * v[p, pl.ds(low, rows), :]
        return value - inside3[p, pl.ds(low, rows), :] * off(v, wx3, wy3, wz3, p, low, rows)

    for k in range(ITERS):
        low, rows, reach = (8, 24, 6 - k) if k < ITERS - 1 else (EDGE, 8, 0)

        def advance(p, k=k, low=low, rows=rows):
            value = doubled(basis.at[k], p, low, rows)
            value = 0.5 * value if k == 0 else value - basis[k - 1, p, pl.ds(low, rows), :]
            basis[k + 1, p, pl.ds(low, rows), :] = value

        loop(7 - reach, 8 + reach, advance)

    own = [basis[k, 7, pl.ds(EDGE, 8), :] for k in range(ITERS + 1)]
    parts = [halves(v) for v in own]
    for n, (i, j) in enumerate(PAIRS):
        high, low = two_prod(own[i], own[j], parts[i], parts[j])
        pair_high[pl.ds(8 * n, 8), :] = high
        pair_low[pl.ds(8 * n, 8), :] = low
    for n in range(len(PAIRS), ROWS):
        pair_high[pl.ds(8 * n, 8), :] = jnp.zeros((8, 128), jnp.float32)
        pair_low[pl.ds(8 * n, 8), :] = jnp.zeros((8, 128), jnp.float32)

    def merge(a, b):
        s, t = two_sum(a[0], b[0])
        return s, t + (a[1] + b[1])

    def tree(terms):
        while len(terms) > 1:
            terms = [merge(terms[i], terms[i + 1]) if i + 1 < len(terms) else terms[i] for i in range(0, len(terms), 2)]
        return terms[0]

    sums = tree([(pair_high[pl.ds(s, ROWS, stride=8), :], pair_low[pl.ds(s, ROWS, stride=8), :]) for s in range(8)])
    for d in (64, 32, 16, 8, 4, 2, 1):
        sums = merge(sums, (pltpu.roll(sums[0], d, 1), pltpu.roll(sums[1], d, 1)))
    lane, row = lane_of((ROWS, 128)), lax.broadcasted_iota(jnp.int32, (ROWS, 128), 0)
    line = jnp.where(lane == row, sums[0], jnp.where(lane == row + 64, sums[1], 0.0))
    gram_y[0] = jnp.sum(line, axis=0, keepdims=True)

    def total_of(ref, count):
        zero = jnp.zeros((1, 128), jnp.float32)
        s, t = tree([(ref[n], zero) for n in range(count)])
        return s + jnp.where(lane_of((1, 128)) >= 64, pltpu.roll(t, 64, 1), 0.0)

    sibling = gx + 1 - 2 * lax.rem(gx, 2)
    for column, y in [(n, dy) for _, dy in over_y + [(0, 0)] for n in (1, 0)]:
        if column or y:
            pltpu.make_async_remote_copy(
                src_ref=gram_y.at[0], dst_ref=gram_y.at[column * ny + y], send_sem=send_sem.at[9], recv_sem=recv_sem.at[9],
                device_id=(sibling if column else gx, device(0, y)[1]), device_id_type=MESH,
            ).start()
    def lift(k):
        start = isinstance(k, int)

        def prolong2(p):
            if start:
                value = iter2[p, pl.ds(12, 24), :]
            else:
                coarse = basis[k, 5 + p // 2, pl.ds(14, 12), :]
                start2[p, pl.ds(12, 12, stride=2), :] = coarse
                start2[p, pl.ds(13, 12, stride=2), :] = coarse
                value = start2[p, pl.ds(12, 24), :]
            start2[p, pl.ds(12, 24), :] = jnp.where(inside(p, 24, 12, 4, 10, 2, 16), value, 0.0)

        def zero(p, low, rows):
            return jnp.zeros((rows, 128), jnp.float32)

        loop(1, 9, prolong2)
        rhs = rhs2_at if start else zero
        loop(2, 8, first_step(step2, inv2, lambda p: residual(rhs, start2, level2, p, 12, 24), 24))

        def post2(p):
            sum2[p, pl.ds(12, 24), :] = start2[p, pl.ds(12, 24), :] + smooth(step2, wx2, wy2, wz2, inv2, p, 12, 24)

        loop(3, 7, post2)

        def prolong1(p):
            coarse = sum2[(p + 5) // 2, pl.ds(14, 20), :]
            start1[p, pl.ds(12, 20, stride=2), :] = coarse
            start1[p, pl.ds(13, 20, stride=2), :] = coarse
            value = start1[p, pl.ds(12, 40), :]
            if start:
                value = value + iter1[p, pl.ds(12, 40), :]
            start1[p, pl.ds(12, 40), :] = jnp.where(inside(p, 40, 12, 3, 10, 4, 32), value, 0.0)

        loop(1, 9, prolong1)
        side = source_at if start else zero
        loop(2, 8, first_step(step1, inv1, lambda p: residual(side, start1, level1, p, 12, 40), 40))

        def post1(p):
            lifted[k, p - 3] = start1[p, pl.ds(EDGE, 32), :] + smooth(step1, wx1, wy1, wz1, inv1, p, EDGE, 32)

        loop(3, 7, post1)

    def lift_some(low, high):
        def step(k, carry):
            lift(k)
            return carry

        lax.fori_loop(low, high, step, 0)

    wait(recv_sem, 4, tiles_of(geo_iter1, 1))
    wait(recv_sem, 6, tiles_of(geo_coarse2, 1))
    lift(ITERS)
    lift_some(0, SOON)
    wait_spread(recv_sem, 9, gram_y, 2 * ny)
    gram_x[0] = total_of(gram_y, 2 * ny)
    spread(10, gram_x, over_z, [n // 2 for n, _ in over_z])
    lift_some(SOON, ITERS)
    wait_spread(recv_sem, 10, gram_x, nx // 2)
    entries = jnp.broadcast_to(total_of(gram_x, nx // 2), (2 * ROWS, 128))
    lane, row = lane_of((2 * ROWS, 128)), lax.broadcasted_iota(jnp.int32, (2 * ROWS, 128), 0)
    place = jnp.where(row < ROWS, row, row + (64 - ROWS))
    column = jnp.sum(jnp.where(lane == place, entries, 0.0), axis=1, keepdims=True)
    scalars[...] = jnp.broadcast_to(column, (2 * ROWS, 128))

    def gram(i, j):
        n = SLOT[(min(i, j), max(i, j))]
        return scalars[pl.ds(n, 1), :], scalars[pl.ds(ROWS + n, 1), :]

    answer = [value * scale for value in gradient_coefficients(gram)]

    for p in range(4):
        total = lifted[ITERS, p]
        for k in range(ITERS):
            total = total + answer[k] * lifted[k, p]
        out[p] = total

    wait(send_sem, 0, tiles_of(geo_fields, 3))
    wait(send_sem, 1, tiles_of(geo_coarse2, 2))
    wait(send_sem, 2, tiles_of(geo_coarse3, 2))
    wait(send_sem, 11, tiles_of(geo_middle3, 2))
    wait(send_sem, 13, tiles_of(geo_outer3, 2))
    wait(send_sem, 3, tiles_of(geo_rhs2, 1))
    wait(send_sem, 4, tiles_of(geo_iter1, 1))
    wait(send_sem, 5, tiles_of(geo_rhs3, 1))
    wait(send_sem, 6, tiles_of(geo_coarse2, 1))
    wait_spread(send_sem, 7, bound_y, ny)
    wait_spread(send_sem, 8, few, 13)
    wait_spread(send_sem, 12, more, 3)
    wait_spread(send_sem, 9, gram_y, 2 * ny)
    wait_spread(send_sem, 10, gram_x, nx // 2)


def solution(mesh):
    nx, ny = mesh.shape["gx"], mesh.shape["gy"]

    def vmem(*shape):
        return pltpu.VMEM(shape, jnp.float32)

    one = [vmem(10, 64, 128)] * 10
    two = [vmem(10, 48, 128)] * 11
    three = [vmem(15, 40, 128)] * 6 + [vmem(ITERS + 1, 15, 40, 128), vmem(ITERS + 1, 4, 32, 128)]

    def on_device(source, beta, shift):
        return pl.pallas_call(
            functools.partial(kernel, (nx, ny)),
            out_shape=jax.ShapeDtypeStruct(source.shape, jnp.float32),
            in_specs=[pl.BlockSpec(memory_space=pl.ANY)] * 3,
            out_specs=pl.BlockSpec(memory_space=pltpu.VMEM),
            scratch_shapes=[
                vmem(3, 10, 64, 128), vmem(2, 10, 48, 128), vmem(2, 15, 40, 128), vmem(10, 48, 128), vmem(15, 40, 128),
                *one, *two, *three,
                vmem(8 * ROWS, 128), vmem(8 * ROWS, 128),
                vmem(ny, 1, 128), vmem(13, 1, 128), vmem(3, 1, 128), vmem(2 * ny, 1, 128), vmem(nx // 2, 1, 128),
                vmem(2 * ROWS, 128), vmem(140, 8, 128),
                pltpu.SemaphoreType.DMA((3,)), pltpu.SemaphoreType.DMA((15,)), pltpu.SemaphoreType.DMA((15,)),
            ],
            compiler_params=pltpu.CompilerParams(collective_id=0, has_side_effects=True, vmem_limit_bytes=40 * 2**20),
        )(*[pltpu.with_memory_space_constraint(x, pltpu.HBM) for x in (source, beta, shift)])

    placed = P("gx", "gy", None)
    return jax.shard_map(on_device, mesh=mesh, in_specs=(placed,) * 3, out_specs=placed, check_vma=False)
```

```python
import functools

import jax
import jax.numpy as jnp
from jax import lax
from jax.experimental import pallas as pl
from jax.experimental.pallas import tpu as pltpu
from jax.sharding import PartitionSpec as P

MESH = pl.DeviceIdType.MESH
ITERS = 6
FIRST = 1.0 / 1.2
CARRY = 2.0 / 7.0
SECOND = 0.75 / 0.7
KEEP = 1.0 + CARRY + SECOND * (1.0 - FIRST) / FIRST
VERTICAL = 1.0 / 16.0
PLANE_SCALES = (1.0, 0.25, 0.0625)
EDGE = 16
SPLIT = 4097.0
SOON = 2

PAIRS = [(i, j) for i in range(ITERS) for j in range(i, ITERS)] + [(ITERS - 1, ITERS)]
SLOT = {pair: n for n, pair in enumerate(PAIRS)}
ROWS = 24


def two_sum(a, b):
    s = a + b
    t = s - a
    return s, (a - (s - t)) + (b - t)


def fast_two_sum(a, b):
    s = a + b
    return s, b - (s - a)


def halves(a):
    t = SPLIT * a
    high = t - (t - a)
    return high, a - high


def two_prod(a, b, a_halves=None, b_halves=None):
    ah, al = halves(a) if a_halves is None else a_halves
    bh, bl = halves(b) if b_halves is None else b_halves
    p = a * b
    return p, ((ah * bh - p) + ah * bl + al * bh) + al * bl


def dd_add(a, b):
    s, t = two_sum(a[0], b[0])
    return fast_two_sum(s, t + (a[1] + b[1]))


def dd_mul(a, b):
    p, t = two_prod(a[0], b[0])
    return fast_two_sum(p, t + (a[0] * b[1] + a[1] * b[0]))


def dd_neg(a):
    return -a[0], -a[1]


def dd_half(a):
    return 0.5 * a[0], 0.5 * a[1]


def dd_div(a, b):
    q = a[0] / b[0]
    p, t = two_prod(q, b[0])
    rest = ((a[0] - p) - t) + (a[1] - q * b[1])
    return fast_two_sum(q, rest / b[0])


def dd_dot(us, ws):
    terms = [dd_mul(u, w) for u, w in zip(us, ws)]
    while len(terms) > 1:
        terms = [dd_add(terms[i], terms[i + 1]) if i + 1 < len(terms) else terms[i] for i in range(0, len(terms), 2)]
    return terms[0]


def gradient_coefficients(gram):
    one = (jnp.ones_like(gram(0, 0)[0]), jnp.zeros_like(gram(0, 0)[0]))
    residual, direction, answer = [one], [one], [None] * ITERS
    norm_now = gram(0, 0)
    for turn in range(ITERS):
        image = []
        for k in range(turn + 2):
            terms = [direction[k]] if k <= turn else []
            if k >= 1:
                terms.append(direction[0] if k == 1 else dd_half(direction[k - 1]))
            if k + 1 <= turn:
                terms.append(dd_half(direction[k + 1]))
            total = terms[0]
            for term in terms[1:]:
                total = dd_add(total, term)
            image.append(total)
        along = dd_mul(direction[turn], dd_dot(image, [gram(i, turn) for i in range(turn + 2)]))
        alpha = dd_div(norm_now, along)
        for k in range(turn + 1):
            step = dd_mul(alpha, direction[k])
            answer[k] = step if answer[k] is None else dd_add(answer[k], step)
        if turn + 1 == ITERS:
            break
        less = dd_neg(alpha)
        steps = [dd_mul(less, value) for value in image]
        residual = [dd_add(residual[k], steps[k]) if k <= turn else steps[k] for k in range(turn + 2)]
        norm_next = dd_mul(residual[turn + 1], dd_dot(residual, [gram(i, turn + 1) for i in range(turn + 2)]))
        beta = dd_div(norm_next, norm_now)
        norm_now = norm_next
        direction = [dd_add(residual[k], dd_mul(beta, direction[k])) if k <= turn else residual[k] for k in range(turn + 2)]
    return [value[0] + value[1] for value in answer]


def loop(low, high, body):
    def step(p, carry):
        body(p)
        return carry

    for p in range(low, high):
        body(p)


def lane_of(shape):
    return lax.broadcasted_iota(jnp.int32, shape, len(shape) - 1)


def box(reach, width):
    return [(i, j) for i in range(-reach, reach + 1) for j in range(-width, width + 1) if (i, j) != (0, 0)]


def ring(count, size):
    far = sorted(range(1, count), key=lambda d: -min(d, count - d))
    return [((d, 0) if size else (0, d)) for d in far]


def windows(offsets, count, rows, first, reach):
    out = []
    for dx, dy in sorted(offsets, key=lambda o: -abs(o[0]) - abs(o[1])):
        if dx == 0:
            start, planes, target = 0, count, first
        elif dx > 0:
            start = max(0, dx * count - reach)
            planes, target = count - start, first - dx * count + start
        else:
            start, planes = 0, min(count, reach + (dx + 1) * count)
            target = first - dx * count
        edge = 4 if count == 1 and abs(dx) > 3 else 8
        row, high, to = (EDGE, rows, EDGE) if dy == 0 else (EDGE + rows - edge, edge, EDGE - edge) if dy > 0 else (EDGE, edge, EDGE + rows)
        out.append((dx, dy, first + start, target, planes, row, to, high))
    return out


def tiles_of(geometry, fields):
    return fields * sum(w[4] * w[7] for w in geometry) // 8


def kernel(
    counts, source, beta, shift, out,
    fields, coarse2, coarse3, rhs2, rhs3,
    masked1, wx1, wy1, wz1, diag1, inv1, step1, near1, iter1, start1,
    masked2, wx2, wy2, wz2, diag2, inv2, step2, near2, iter2, start2, sum2,
    masked3, wx3, wy3, wz3, own3, inside3, basis, lifted,
    pair_high, pair_low, bound_y, few, more, last, gram_y, gram_x, scalars, dummy,
    load_sem, send_sem, recv_sem,
):
    nx, ny = counts
    gx, gy = lax.axis_index("gx"), lax.axis_index("gy")

    def device(dx, dy):
        return lax.rem(gx + (dx + nx), nx), lax.rem(gy + (dy + ny), ny)

    near, wide, far = box(1, 1), box(2, 1), box(7, 1)
    over_y = ring(ny, 0)
    over_z = [(2 * n, 0) for n, _ in ring(nx // 2, 1)]
    few_x = [(d, 0) for n in range(4, 0, -1) for d in (n, -n)]
    more_x, last_x = [(8, 0), (-8, 0)], [(nx // 2, 0)]
    middle = [o for o in far if 3 <= abs(o[0]) <= 4]
    outer = [o for o in far if abs(o[0]) > 4]

    loads = [
        pltpu.make_async_copy(ref, fields.at[n, pl.ds(3, 4), pl.ds(EDGE, 32)], load_sem.at[n])
        for n, ref in enumerate((source, shift, beta))
    ]

    partners = sorted({(dx % nx, dy % ny) for dx, dy in wide + over_y}, key=lambda o: min(o[0], nx - o[0]) + min(o[1], ny - o[1]))
    barrier = pltpu.get_barrier_semaphore()
    for dx, dy in partners:
        pl.semaphore_signal(barrier, 1, device_id=device(-dx, -dy), device_id_type=MESH)

    for load in loads:
        load.start()

    def send(phase, ref, geometry, stacked):
        for dx, dy, plane, target, planes, row, to, high in geometry:
            here, there = (pl.ds(plane, planes), pl.ds(row, high)), (pl.ds(target, planes), pl.ds(to, high))
            if stacked:
                here, there = (slice(None), *here), (slice(None), *there)
            pltpu.make_async_remote_copy(
                src_ref=ref.at[here], dst_ref=ref.at[there], send_sem=send_sem.at[phase], recv_sem=recv_sem.at[phase],
                device_id=device(dx, dy), device_id_type=MESH,
            ).start()

    def wait(sems, phase, tiles):
        part = dummy.at[pl.ds(0, tiles)]
        pltpu.make_async_copy(part, part, sems.at[phase]).wait()

    def spread(phase, ref, offsets, slots=None):
        for n, (dx, dy) in enumerate(offsets):
            pltpu.make_async_remote_copy(
                src_ref=ref.at[0], dst_ref=ref.at[max(dx, dy) if slots is None else slots[n]], send_sem=send_sem.at[phase], recv_sem=recv_sem.at[phase],
                device_id=device(dx, dy), device_id_type=MESH,
            ).start()

    def wait_spread(sems, phase, ref, count):
        part = ref.at[pl.ds(1, count - 1)]
        pltpu.make_async_copy(part, part, sems.at[phase]).wait()

    def inside(p, rows, low, first, count, own_planes, own_rows):
        plane = gx * own_planes + (p - first)
        row = gy * own_rows + (low - EDGE) + lax.broadcasted_iota(jnp.int32, (rows, 128), 0)
        fits = jnp.logical_and(plane >= 0, plane < nx * own_planes).astype(jnp.int32)
        return jnp.where(jnp.logical_and(row >= 0, row < ny * own_rows), fits, 0) > 0

    def off(v, wx, wy, wz, p, low, rows):
        here = v[p, pl.ds(low, rows), :]
        up = wz[p, pl.ds(low, rows), :]
        total = wx[p, pl.ds(low, rows), :] * v[p + 1, pl.ds(low, rows), :]
        total = total + wx[p - 1, pl.ds(low, rows), :] * v[p - 1, pl.ds(low, rows), :]
        total = total + wy[p, pl.ds(low, rows), :] * v[p, pl.ds(low + 1, rows), :]
        total = total + wy[p, pl.ds(low - 1, rows), :] * v[p, pl.ds(low - 1, rows), :]
        total = total + up * pltpu.roll(here, 127, 1)
        return total + pltpu.roll(up * here, 1, 1)

    def weights(b, p, low, rows, plane, upright):
        here = b[p, pl.ds(low, rows), :]
        lane = lane_of((rows, 128))
        wxp = plane * (here + b[p + 1, pl.ds(low, rows), :])
        wxm = plane * (here + b[p - 1, pl.ds(low, rows), :])
        wyp = plane * (here + b[p, pl.ds(low + 1, rows), :])
        wym = plane * (here + b[p, pl.ds(low - 1, rows), :])
        wzp = upright * (here + jnp.where(lane < 127, pltpu.roll(here, 127, 1), 0.0))
        wzm = upright * (here + jnp.where(lane > 0, pltpu.roll(here, 1, 1), 0.0))
        return wxp, wyp, jnp.where(lane < 127, wzp, 0.0), wxp + wxm + wyp + wym + wzp + wzm

    def prepare(refs, pair, rows, first, own, scale):
        masked, wx, wy, wz, diag, inv = refs
        shift_at, beta_at = pair

        def clean(p):
            ok = inside(p, rows, 8, first, 10, own[0], own[1])
            masked[p, pl.ds(8, rows), :] = jnp.where(ok, beta_at(p), 0.0)

        def fill(p):
            wxp, wyp, wzp, total = weights(masked, p, 12, rows - 8, 0.5 * scale, 0.5 * VERTICAL)
            total = total + shift_at(p)
            wx[p, pl.ds(12, rows - 8), :] = wxp
            wy[p, pl.ds(12, rows - 8), :] = wyp
            wz[p, pl.ds(12, rows - 8), :] = wzp
            diag[p, pl.ds(12, rows - 8), :] = total
            ok = inside(p, rows - 8, 12, first, 10, own[0], own[1])
            inv[p, pl.ds(12, rows - 8), :] = jnp.where(ok, 1.0 / total, 0.0)

        loop(0, 10, clean)
        loop(1, 9, fill)

    def coarsen_rows(ref, at, rows):
        even = ref[at, pl.ds(EDGE, rows // 2, stride=2), :]
        return 0.25 * (even + ref[at, pl.ds(EDGE + 1, rows // 2, stride=2), :])

    geo_fields = windows(near, 4, 32, 3, 3)
    geo_coarse2 = windows(wide, 2, 16, 4, 3)
    geo_coarse3, geo_middle3, geo_outer3 = (windows(part, 1, 8, 7, 7) for part in (wide, middle, outer))
    geo_rhs3 = windows(far, 1, 8, 7, 7)
    geo_iter1 = windows(near, 4, 32, 3, 2)
    geo_rhs2 = windows(near, 2, 16, 4, 2)
    for load in loads:
        load.wait()
    pl.semaphore_wait(barrier, len(partners))
    send(0, fields, geo_fields, True)

    for n, level in ((0, 1), (1, 2)):
        for q in range(2):
            both = fields[1 + n, 3 + 2 * q, pl.ds(EDGE, 32), :] + fields[1 + n, 4 + 2 * q, pl.ds(EDGE, 32), :]
            near1[q, pl.ds(EDGE, 32), :] = both
            coarse2[n, 4 + q, pl.ds(EDGE, 16), :] = coarsen_rows(near1, q, 32)
        near2[0, pl.ds(EDGE, 16), :] = coarse2[n, 4, pl.ds(EDGE, 16), :] + coarse2[n, 5, pl.ds(EDGE, 16), :]
        coarse3[n, 7, pl.ds(EDGE, 8), :] = coarsen_rows(near2, 0, 16)
    shift_own, beta_own = coarse3[0, 7, pl.ds(EDGE, 8), :], coarse3[1, 7, pl.ds(EDGE, 8), :]
    around = pltpu.roll(beta_own, 1, 0) + pltpu.roll(beta_own, 7, 0) + pltpu.roll(beta_own, 1, 1) + pltpu.roll(beta_own, 127, 1)
    bound = jnp.max(shift_own + PLANE_SCALES[2] * (6.0 * beta_own + 1.5 * around))
    bound_y[0] = jnp.full((1, 128), bound, jnp.float32)

    spread(7, bound_y, over_y)
    send(1, coarse2, geo_coarse2, True)
    send(2, coarse3, geo_coarse3, True)

    wait(recv_sem, 0, tiles_of(geo_fields, 3))
    wait(recv_sem, 1, tiles_of(geo_coarse2, 2))
    wait_spread(recv_sem, 7, bound_y, ny)
    few[0] = functools.reduce(jnp.maximum, [bound_y[n] for n in range(ny)])
    spread(8, few, few_x, range(1, 9))
    level1 = (masked1, wx1, wy1, wz1, diag1, inv1)
    prepare(
        level1, (lambda p: fields[1, p, pl.ds(12, 40), :], lambda p: fields[2, p, pl.ds(8, 48), :]), 48, 3, (4, 32), PLANE_SCALES[0]
    )

    def first_step(step, inv, value, rows):
        def body(p):
            step[p, pl.ds(12, rows), :] = FIRST * value(p) * inv[p, pl.ds(12, rows), :]

        return body

    def smooth(step, wx, wy, wz, inv, p, low, rows):
        part = off(step, wx, wy, wz, p, low, rows)
        return KEEP * step[p, pl.ds(low, rows), :] + SECOND * inv[p, pl.ds(low, rows), :] * part

    loop(1, 9, first_step(step1, inv1, lambda p: fields[0, p, pl.ds(12, 40), :], 40))

    def presmooth1(p):
        near1[p, pl.ds(12, 40), :] = smooth(step1, wx1, wy1, wz1, inv1, p, 12, 40)

    loop(2, 8, presmooth1)

    def residual(f, v, level, p, low, rows):
        _, wx, wy, wz, diag, _ = level
        value = f(p, low, rows) - diag[p, pl.ds(low, rows), :] * v[p, pl.ds(low, rows), :]
        return value + off(v, wx, wy, wz, p, low, rows)

    def source_at(p, low, rows):
        return fields[0, p, pl.ds(low, rows), :]

    def rhs2_at(p, low, rows):
        return rhs2[p, pl.ds(low, rows), :]

    def restrict1(q):
        both = residual(source_at, near1, level1, 3 + 2 * q, EDGE, 32) + residual(source_at, near1, level1, 4 + 2 * q, EDGE, 32)
        start1[q, pl.ds(EDGE, 32), :] = both
        rhs2[4 + q, pl.ds(EDGE, 16), :] = coarsen_rows(start1, q, 32)

    loop(0, 2, restrict1)
    send(3, rhs2, geo_rhs2, False)

    def keep1(p):
        iter1[p, pl.ds(EDGE, 32), :] = near1[p, pl.ds(EDGE, 32), :]

    loop(3, 7, keep1)
    send(4, iter1, geo_iter1, False)

    send(11, coarse3, geo_middle3, True)
    level2 = (masked2, wx2, wy2, wz2, diag2, inv2)
    prepare(
        level2, (lambda p: coarse2[0, p, pl.ds(12, 24), :], lambda p: coarse2[1, p, pl.ds(8, 32), :]), 32, 4, (2, 16), PLANE_SCALES[1]
    )
    wait_spread(recv_sem, 8, few, 9)
    more[0] = functools.reduce(jnp.maximum, [few[n] for n in range(9)])
    spread(12, more, more_x, range(1, 3))
    send(13, coarse3, geo_outer3, True)
    wait(recv_sem, 3, tiles_of(geo_rhs2, 1))
    loop(2, 8, first_step(step2, inv2, lambda p: rhs2_at(p, 12, 24), 24))

    def presmooth2(p):
        near2[p, pl.ds(12, 24), :] = smooth(step2, wx2, wy2, wz2, inv2, p, 12, 24)

    loop(3, 7, presmooth2)
    both = residual(rhs2_at, near2, level2, 4, EDGE, 16) + residual(rhs2_at, near2, level2, 5, EDGE, 16)
    start2[0, pl.ds(EDGE, 16), :] = both
    rhs3[7, pl.ds(EDGE, 8), :] = coarsen_rows(start2, 0, 16)
    send(5, rhs3, geo_rhs3, False)
    for p in (4, 5):
        iter2[p, pl.ds(EDGE, 16), :] = near2[p, pl.ds(EDGE, 16), :]
    send(6, iter2, geo_coarse2, False)

    wait_spread(recv_sem, 12, more, 3)
    last[0] = functools.reduce(jnp.maximum, [more[n] for n in range(3)])
    spread(14, last, last_x, range(1, 2))
    wait(recv_sem, 2, tiles_of(geo_coarse3, 2))
    wait(recv_sem, 11, tiles_of(geo_middle3, 2))
    wait(recv_sem, 13, tiles_of(geo_outer3, 2))
    wait_spread(recv_sem, 14, last, 2)
    scale = 2.0 / jnp.maximum(last[0], last[1])

    def clean3(p):
        ok = inside(p, 24, 8, 7, 15, 1, 8)
        masked3[p, pl.ds(8, 24), :] = jnp.where(ok, coarse3[1, p, pl.ds(8, 24), :], 0.0)

    loop(0, 15, clean3)
    wx3[0, pl.ds(8, 24), :] = (PLANE_SCALES[2] * scale) * (masked3[0, pl.ds(8, 24), :] + masked3[1, pl.ds(8, 24), :])

    def fill3(p):
        wxp, wyp, wzp, total = weights(masked3, p, 8, 24, PLANE_SCALES[2] * scale, VERTICAL * scale)
        total = total + 2.0 * scale * coarse3[0, p, pl.ds(8, 24), :]
        wx3[p, pl.ds(8, 24), :] = wxp
        wy3[p, pl.ds(8, 24), :] = wyp
        wz3[p, pl.ds(8, 24), :] = wzp
        ok = inside(p, 24, 8, 7, 15, 1, 8)
        own3[p, pl.ds(8, 24), :] = jnp.where(ok, total - 2.0, 0.0)
        inside3[p, pl.ds(8, 24), :] = jnp.where(ok, 1.0, 0.0)

    loop(1, 14, fill3)
    wait(recv_sem, 5, tiles_of(geo_rhs3, 1))

    def begin3(p):
        ok = inside(p, 24, 8, 7, 15, 1, 8)
        basis[0, p, pl.ds(8, 24), :] = jnp.where(ok, rhs3[p, pl.ds(8, 24), :], 0.0)

    loop(0, 15, begin3)

    def doubled(v, p, low, rows):
        value = own3[p, pl.ds(low, rows), :] * v[p, pl.ds(low, rows), :]
        return value - inside3[p, pl.ds(low, rows), :] * off(v, wx3, wy3, wz3, p, low, rows)

    for k in range(ITERS):
        low, rows, reach = (8, 24, 6 - k) if k < ITERS - 1 else (EDGE, 8, 0)

        def advance(p, k=k, low=low, rows=rows):
            value = doubled(basis.at[k], p, low, rows)
            value = 0.5 * value if k == 0 else value - basis[k - 1, p, pl.ds(low, rows), :]
            basis[k + 1, p, pl.ds(low, rows), :] = value

        loop(7 - reach, 8 + reach, advance)

    own = [basis[k, 7, pl.ds(EDGE, 8), :] for k in range(ITERS + 1)]
    parts = [halves(v) for v in own]
    for n, (i, j) in enumerate(PAIRS):
        high, low = two_prod(own[i], own[j], parts[i], parts[j])
        pair_high[pl.ds(8 * n, 8), :] = high
        pair_low[pl.ds(8 * n, 8), :] = low
    for n in range(len(PAIRS), ROWS):
        pair_high[pl.ds(8 * n, 8), :] = jnp.zeros((8, 128), jnp.float32)
        pair_low[pl.ds(8 * n, 8), :] = jnp.zeros((8, 128), jnp.float32)

    def merge(a, b):
        s, t = two_sum(a[0], b[0])
        return s, t + (a[1] + b[1])

    def tree(terms):
        while len(terms) > 1:
            terms = [merge(terms[i], terms[i + 1]) if i + 1 < len(terms) else terms[i] for i in range(0, len(terms), 2)]
        return terms[0]

    sums = tree([(pair_high[pl.ds(s, ROWS, stride=8), :], pair_low[pl.ds(s, ROWS, stride=8), :]) for s in range(8)])
    for d in (64, 32, 16, 8, 4, 2, 1):
        sums = merge(sums, (pltpu.roll(sums[0], d, 1), pltpu.roll(sums[1], d, 1)))
    lane, row = lane_of((ROWS, 128)), lax.broadcasted_iota(jnp.int32, (ROWS, 128), 0)
    line = jnp.where(lane == row, sums[0], jnp.where(lane == row + 64, sums[1], 0.0))
    gram_y[0] = jnp.sum(line, axis=0, keepdims=True)

    def total_of(ref, count):
        zero = jnp.zeros((1, 128), jnp.float32)
        s, t = tree([(ref[n], zero) for n in range(count)])
        return s + jnp.where(lane_of((1, 128)) >= 64, pltpu.roll(t, 64, 1), 0.0)

    sibling = gx + 1 - 2 * lax.rem(gx, 2)
    for column, y in [(n, dy) for _, dy in over_y + [(0, 0)] for n in (1, 0)]:
        if column or y:
            pltpu.make_async_remote_copy(
                src_ref=gram_y.at[0], dst_ref=gram_y.at[column * ny + y], send_sem=send_sem.at[9], recv_sem=recv_sem.at[9],
                device_id=(sibling if column else gx, device(0, y)[1]), device_id_type=MESH,
            ).start()
    def lift(k):
        start = isinstance(k, int)

        def prolong2(p):
            if start:
                value = iter2[p, pl.ds(12, 24), :]
            else:
                coarse = basis[k, 5 + p // 2, pl.ds(14, 12), :]
                start2[p, pl.ds(12, 12, stride=2), :] = coarse
                start2[p, pl.ds(13, 12, stride=2), :] = coarse
                value = start2[p, pl.ds(12, 24), :]
            start2[p, pl.ds(12, 24), :] = jnp.where(inside(p, 24, 12, 4, 10, 2, 16), value, 0.0)

        def zero(p, low, rows):
            return jnp.zeros((rows, 128), jnp.float32)

        loop(1, 9, prolong2)
        rhs = rhs2_at if start else zero
        loop(2, 8, first_step(step2, inv2, lambda p: residual(rhs, start2, level2, p, 12, 24), 24))

        def post2(p):
            sum2[p, pl.ds(12, 24), :] = start2[p, pl.ds(12, 24), :] + smooth(step2, wx2, wy2, wz2, inv2, p, 12, 24)

        loop(3, 7, post2)

        def prolong1(p):
            coarse = sum2[(p + 5) // 2, pl.ds(14, 20), :]
            start1[p, pl.ds(12, 20, stride=2), :] = coarse
            start1[p, pl.ds(13, 20, stride=2), :] = coarse
            value = start1[p, pl.ds(12, 40), :]
            if start:
                value = value + iter1[p, pl.ds(12, 40), :]
            start1[p, pl.ds(12, 40), :] = jnp.where(inside(p, 40, 12, 3, 10, 4, 32), value, 0.0)

        loop(1, 9, prolong1)
        side = source_at if start else zero
        loop(2, 8, first_step(step1, inv1, lambda p: residual(side, start1, level1, p, 12, 40), 40))

        def post1(p):
            lifted[k, p - 3] = start1[p, pl.ds(EDGE, 32), :] + smooth(step1, wx1, wy1, wz1, inv1, p, EDGE, 32)

        loop(3, 7, post1)

    def lift_some(low, high):
        def step(k, carry):
            lift(k)
            return carry

        lax.fori_loop(low, high, step, 0)

    wait(recv_sem, 4, tiles_of(geo_iter1, 1))
    wait(recv_sem, 6, tiles_of(geo_coarse2, 1))
    lift(ITERS)
    lift_some(0, SOON)
    wait_spread(recv_sem, 9, gram_y, 2 * ny)
    gram_x[0] = total_of(gram_y, 2 * ny)
    spread(10, gram_x, over_z, [n // 2 for n, _ in over_z])
    lift_some(SOON, ITERS)
    wait_spread(recv_sem, 10, gram_x, nx // 2)
    entries = jnp.broadcast_to(total_of(gram_x, nx // 2), (2 * ROWS, 128))
    lane, row = lane_of((2 * ROWS, 128)), lax.broadcasted_iota(jnp.int32, (2 * ROWS, 128), 0)
    place = jnp.where(row < ROWS, row, row + (64 - ROWS))
    column = jnp.sum(jnp.where(lane == place, entries, 0.0), axis=1, keepdims=True)
    scalars[...] = jnp.broadcast_to(column, (2 * ROWS, 128))

    def gram(i, j):
        n = SLOT[(min(i, j), max(i, j))]
        return scalars[pl.ds(n, 1), :], scalars[pl.ds(ROWS + n, 1), :]

    answer = [value * scale for value in gradient_coefficients(gram)]

    for p in range(4):
        total = lifted[ITERS, p]
        for k in range(ITERS):
            total = total + answer[k] * lifted[k, p]
        out[p] = total

    wait(send_sem, 0, tiles_of(geo_fields, 3))
    wait(send_sem, 1, tiles_of(geo_coarse2, 2))
    wait(send_sem, 2, tiles_of(geo_coarse3, 2))
    wait(send_sem, 11, tiles_of(geo_middle3, 2))
    wait(send_sem, 13, tiles_of(geo_outer3, 2))
    wait(send_sem, 3, tiles_of(geo_rhs2, 1))
    wait(send_sem, 4, tiles_of(geo_iter1, 1))
    wait(send_sem, 5, tiles_of(geo_rhs3, 1))
    wait(send_sem, 6, tiles_of(geo_coarse2, 1))
    wait_spread(send_sem, 7, bound_y, ny)
    wait_spread(send_sem, 8, few, 9)
    wait_spread(send_sem, 12, more, 3)
    wait_spread(send_sem, 14, last, 2)
    wait_spread(send_sem, 9, gram_y, 2 * ny)
    wait_spread(send_sem, 10, gram_x, nx // 2)


def solution(mesh):
    nx, ny = mesh.shape["gx"], mesh.shape["gy"]

    def vmem(*shape):
        return pltpu.VMEM(shape, jnp.float32)

    one = [vmem(10, 64, 128)] * 10
    two = [vmem(10, 48, 128)] * 11
    three = [vmem(15, 40, 128)] * 6 + [vmem(ITERS + 1, 15, 40, 128), vmem(ITERS + 1, 4, 32, 128)]

    def on_device(source, beta, shift):
        return pl.pallas_call(
            functools.partial(kernel, (nx, ny)),
            out_shape=jax.ShapeDtypeStruct(source.shape, jnp.float32),
            in_specs=[pl.BlockSpec(memory_space=pl.ANY)] * 3,
            out_specs=pl.BlockSpec(memory_space=pltpu.VMEM),
            scratch_shapes=[
                vmem(3, 10, 64, 128), vmem(2, 10, 48, 128), vmem(2, 15, 40, 128), vmem(10, 48, 128), vmem(15, 40, 128),
                *one, *two, *three,
                vmem(8 * ROWS, 128), vmem(8 * ROWS, 128),
                vmem(ny, 1, 128), vmem(9, 1, 128), vmem(3, 1, 128), vmem(2, 1, 128), vmem(2 * ny, 1, 128), vmem(nx // 2, 1, 128),
                vmem(2 * ROWS, 128), vmem(140, 8, 128),
                pltpu.SemaphoreType.DMA((3,)), pltpu.SemaphoreType.DMA((15,)), pltpu.SemaphoreType.DMA((15,)),
            ],
            compiler_params=pltpu.CompilerParams(collective_id=0, has_side_effects=True, vmem_limit_bytes=40 * 2**20),
        )(*[pltpu.with_memory_space_constraint(x, pltpu.HBM) for x in (source, beta, shift)])

    placed = P("gx", "gy", None)
    return jax.shard_map(on_device, mesh=mesh, in_specs=(placed,) * 3, out_specs=placed, check_vma=False)
```

```python
import functools

import jax
import jax.numpy as jnp
from jax import lax
from jax.experimental import pallas as pl
from jax.experimental.pallas import tpu as pltpu
from jax.sharding import PartitionSpec as P

MESH = pl.DeviceIdType.MESH
ITERS = 6
FIRST = 1.0 / 1.2
CARRY = 2.0 / 7.0
SECOND = 0.75 / 0.7
KEEP = 1.0 + CARRY + SECOND * (1.0 - FIRST) / FIRST
VERTICAL = 1.0 / 16.0
PLANE_SCALES = (1.0, 0.25, 0.0625)
EDGE = 16
SPLIT = 4097.0
SOON = 2

PAIRS = [(i, j) for i in range(ITERS) for j in range(i, ITERS)] + [(ITERS - 1, ITERS)]
SLOT = {pair: n for n, pair in enumerate(PAIRS)}
ROWS = 24


def two_sum(a, b):
    s = a + b
    t = s - a
    return s, (a - (s - t)) + (b - t)


def fast_two_sum(a, b):
    s = a + b
    return s, b - (s - a)


def halves(a):
    t = SPLIT * a
    high = t - (t - a)
    return high, a - high


def two_prod(a, b, a_halves=None, b_halves=None):
    ah, al = halves(a) if a_halves is None else a_halves
    bh, bl = halves(b) if b_halves is None else b_halves
    p = a * b
    return p, ((ah * bh - p) + ah * bl + al * bh) + al * bl


def dd_add(a, b):
    s, t = two_sum(a[0], b[0])
    return fast_two_sum(s, t + (a[1] + b[1]))


def dd_mul(a, b):
    p, t = two_prod(a[0], b[0])
    return fast_two_sum(p, t + (a[0] * b[1] + a[1] * b[0]))


def dd_neg(a):
    return -a[0], -a[1]


def dd_half(a):
    return 0.5 * a[0], 0.5 * a[1]


def dd_div(a, b):
    q = a[0] / b[0]
    p, t = two_prod(q, b[0])
    rest = ((a[0] - p) - t) + (a[1] - q * b[1])
    return fast_two_sum(q, rest / b[0])


def dd_dot(us, ws):
    terms = [dd_mul(u, w) for u, w in zip(us, ws)]
    while len(terms) > 1:
        terms = [dd_add(terms[i], terms[i + 1]) if i + 1 < len(terms) else terms[i] for i in range(0, len(terms), 2)]
    return terms[0]


def gradient_coefficients(gram):
    one = (jnp.ones_like(gram(0, 0)[0]), jnp.zeros_like(gram(0, 0)[0]))
    residual, direction, answer = [one], [one], [None] * ITERS
    norm_now = gram(0, 0)
    for turn in range(ITERS):
        image = []
        for k in range(turn + 2):
            terms = [direction[k]] if k <= turn else []
            if k >= 1:
                terms.append(direction[0] if k == 1 else dd_half(direction[k - 1]))
            if k + 1 <= turn:
                terms.append(dd_half(direction[k + 1]))
            total = terms[0]
            for term in terms[1:]:
                total = dd_add(total, term)
            image.append(total)
        along = dd_mul(direction[turn], dd_dot(image, [gram(i, turn) for i in range(turn + 2)]))
        alpha = dd_div(norm_now, along)
        for k in range(turn + 1):
            step = dd_mul(alpha, direction[k])
            answer[k] = step if answer[k] is None else dd_add(answer[k], step)
        if turn + 1 == ITERS:
            break
        less = dd_neg(alpha)
        steps = [dd_mul(less, value) for value in image]
        residual = [dd_add(residual[k], steps[k]) if k <= turn else steps[k] for k in range(turn + 2)]
        norm_next = dd_mul(residual[turn + 1], dd_dot(residual, [gram(i, turn + 1) for i in range(turn + 2)]))
        beta = dd_div(norm_next, norm_now)
        norm_now = norm_next
        direction = [dd_add(residual[k], dd_mul(beta, direction[k])) if k <= turn else residual[k] for k in range(turn + 2)]
    return [value[0] + value[1] for value in answer]


def loop(low, high, body):
    def step(p, carry):
        body(p)
        return carry

    for p in range(low, high):
        body(p)


def lane_of(shape):
    return lax.broadcasted_iota(jnp.int32, shape, len(shape) - 1)


def box(reach, width):
    return [(i, j) for i in range(-reach, reach + 1) for j in range(-width, width + 1) if (i, j) != (0, 0)]


def ring(count, size):
    far = sorted(range(1, count), key=lambda d: -min(d, count - d))
    return [((d, 0) if size else (0, d)) for d in far]


def windows(offsets, count, rows, first, reach):
    out = []
    for dx, dy in sorted(offsets, key=lambda o: -abs(o[0]) - abs(o[1])):
        if dx == 0:
            start, planes, target = 0, count, first
        elif dx > 0:
            start = max(0, dx * count - reach)
            planes, target = count - start, first - dx * count + start
        else:
            start, planes = 0, min(count, reach + (dx + 1) * count)
            target = first - dx * count
        edge = 8 if count > 1 or abs(dx) < 4 else 4 if abs(dx) < 6 else 2
        row, high, to = (EDGE, rows, EDGE) if dy == 0 else (EDGE + rows - edge, edge, EDGE - edge) if dy > 0 else (EDGE, edge, EDGE + rows)
        out.append((dx, dy, first + start, target, planes, row, to, high))
    return out


def tiles_of(geometry, fields):
    return fields * sum(w[4] * w[7] for w in geometry) // 8


def kernel(
    counts, source, beta, shift, out,
    fields, coarse2, coarse3, rhs2, rhs3,
    masked1, wx1, wy1, wz1, diag1, inv1, step1, near1, iter1, start1,
    masked2, wx2, wy2, wz2, diag2, inv2, step2, near2, iter2, start2, sum2,
    masked3, wx3, wy3, wz3, own3, inside3, basis, lifted,
    pair_high, pair_low, bound_y, few, more, gram_y, gram_x, scalars, dummy,
    load_sem, send_sem, recv_sem,
):
    nx, ny = counts
    gx, gy = lax.axis_index("gx"), lax.axis_index("gy")

    def device(dx, dy):
        return lax.rem(gx + (dx + nx), nx), lax.rem(gy + (dy + ny), ny)

    near, wide, far = box(1, 1), box(2, 1), box(7, 1)
    over_y = ring(ny, 0)
    over_z = [(2 * n, 0) for n, _ in ring(nx // 2, 1)]
    along_x = [(d, 0) for d in range(-8, 9) if d]
    few_x = [(d, 0) for n in range(6, 0, -1) for d in (n, -n)]
    more_x = [(13, 0), (-13, 0)]
    middle = [o for o in far if 3 <= abs(o[0]) <= 4]
    outer = [o for o in far if abs(o[0]) > 4]

    loads = [
        pltpu.make_async_copy(ref, fields.at[n, pl.ds(3, 4), pl.ds(EDGE, 32)], load_sem.at[n])
        for n, ref in enumerate((source, shift, beta))
    ]

    partners = sorted({(dx % nx, dy % ny) for dx, dy in wide + over_y + along_x}, key=lambda o: min(o[0], nx - o[0]) + min(o[1], ny - o[1]))
    barrier = pltpu.get_barrier_semaphore()
    for dx, dy in partners:
        pl.semaphore_signal(barrier, 1, device_id=device(-dx, -dy), device_id_type=MESH)

    for load in loads:
        load.start()

    def send(phase, ref, geometry, stacked):
        for dx, dy, plane, target, planes, row, to, high in geometry:
            here, there = (pl.ds(plane, planes), pl.ds(row, high)), (pl.ds(target, planes), pl.ds(to, high))
            if stacked:
                here, there = (slice(None), *here), (slice(None), *there)
            pltpu.make_async_remote_copy(
                src_ref=ref.at[here], dst_ref=ref.at[there], send_sem=send_sem.at[phase], recv_sem=recv_sem.at[phase],
                device_id=device(dx, dy), device_id_type=MESH,
            ).start()

    def wait(sems, phase, tiles):
        part = dummy.at[pl.ds(0, tiles)]
        pltpu.make_async_copy(part, part, sems.at[phase]).wait()

    def spread(phase, ref, offsets, slots=None):
        for n, (dx, dy) in enumerate(offsets):
            pltpu.make_async_remote_copy(
                src_ref=ref.at[0], dst_ref=ref.at[max(dx, dy) if slots is None else slots[n]], send_sem=send_sem.at[phase], recv_sem=recv_sem.at[phase],
                device_id=device(dx, dy), device_id_type=MESH,
            ).start()

    def wait_spread(sems, phase, ref, count):
        part = ref.at[pl.ds(1, count - 1)]
        pltpu.make_async_copy(part, part, sems.at[phase]).wait()

    def inside(p, rows, low, first, count, own_planes, own_rows):
        plane = gx * own_planes + (p - first)
        row = gy * own_rows + (low - EDGE) + lax.broadcasted_iota(jnp.int32, (rows, 128), 0)
        fits = jnp.logical_and(plane >= 0, plane < nx * own_planes).astype(jnp.int32)
        return jnp.where(jnp.logical_and(row >= 0, row < ny * own_rows), fits, 0) > 0

    def off(v, wx, wy, wz, p, low, rows):
        here = v[p, pl.ds(low, rows), :]
        up = wz[p, pl.ds(low, rows), :]
        total = wx[p, pl.ds(low, rows), :] * v[p + 1, pl.ds(low, rows), :]
        total = total + wx[p - 1, pl.ds(low, rows), :] * v[p - 1, pl.ds(low, rows), :]
        total = total + wy[p, pl.ds(low, rows), :] * v[p, pl.ds(low + 1, rows), :]
        total = total + wy[p, pl.ds(low - 1, rows), :] * v[p, pl.ds(low - 1, rows), :]
        total = total + up * pltpu.roll(here, 127, 1)
        return total + pltpu.roll(up * here, 1, 1)

    def weights(b, p, low, rows, plane, upright):
        here = b[p, pl.ds(low, rows), :]
        lane = lane_of((rows, 128))
        wxp = plane * (here + b[p + 1, pl.ds(low, rows), :])
        wxm = plane * (here + b[p - 1, pl.ds(low, rows), :])
        wyp = plane * (here + b[p, pl.ds(low + 1, rows), :])
        wym = plane * (here + b[p, pl.ds(low - 1, rows), :])
        wzp = upright * (here + jnp.where(lane < 127, pltpu.roll(here, 127, 1), 0.0))
        wzm = upright * (here + jnp.where(lane > 0, pltpu.roll(here, 1, 1), 0.0))
        return wxp, wyp, jnp.where(lane < 127, wzp, 0.0), wxp + wxm + wyp + wym + wzp + wzm

    def prepare(refs, pair, rows, first, own, scale):
        masked, wx, wy, wz, diag, inv = refs
        shift_at, beta_at = pair

        def clean(p):
            ok = inside(p, rows, 8, first, 10, own[0], own[1])
            masked[p, pl.ds(8, rows), :] = jnp.where(ok, beta_at(p), 0.0)

        def fill(p):
            wxp, wyp, wzp, total = weights(masked, p, 12, rows - 8, 0.5 * scale, 0.5 * VERTICAL)
            total = total + shift_at(p)
            wx[p, pl.ds(12, rows - 8), :] = wxp
            wy[p, pl.ds(12, rows - 8), :] = wyp
            wz[p, pl.ds(12, rows - 8), :] = wzp
            diag[p, pl.ds(12, rows - 8), :] = total
            ok = inside(p, rows - 8, 12, first, 10, own[0], own[1])
            inv[p, pl.ds(12, rows - 8), :] = jnp.where(ok, 1.0 / total, 0.0)

        loop(0, 10, clean)
        loop(1, 9, fill)

    def coarsen_rows(ref, at, rows):
        even = ref[at, pl.ds(EDGE, rows // 2, stride=2), :]
        return 0.25 * (even + ref[at, pl.ds(EDGE + 1, rows // 2, stride=2), :])

    geo_fields = windows(near, 4, 32, 3, 3)
    geo_coarse2 = windows(wide, 2, 16, 4, 3)
    geo_coarse3, geo_middle3, geo_outer3 = (windows(part, 1, 8, 7, 7) for part in (wide, middle, outer))
    geo_rhs3 = windows(far, 1, 8, 7, 7)
    geo_iter1 = windows(near, 4, 32, 3, 2)
    geo_rhs2 = windows(near, 2, 16, 4, 2)
    for load in loads:
        load.wait()
    pl.semaphore_wait(barrier, len(partners))
    send(0, fields, geo_fields, True)

    for n, level in ((0, 1), (1, 2)):
        for q in range(2):
            both = fields[1 + n, 3 + 2 * q, pl.ds(EDGE, 32), :] + fields[1 + n, 4 + 2 * q, pl.ds(EDGE, 32), :]
            near1[q, pl.ds(EDGE, 32), :] = both
            coarse2[n, 4 + q, pl.ds(EDGE, 16), :] = coarsen_rows(near1, q, 32)
        near2[0, pl.ds(EDGE, 16), :] = coarse2[n, 4, pl.ds(EDGE, 16), :] + coarse2[n, 5, pl.ds(EDGE, 16), :]
        coarse3[n, 7, pl.ds(EDGE, 8), :] = coarsen_rows(near2, 0, 16)
    shift_own, beta_own = coarse3[0, 7, pl.ds(EDGE, 8), :], coarse3[1, 7, pl.ds(EDGE, 8), :]
    around = pltpu.roll(beta_own, 1, 0) + pltpu.roll(beta_own, 7, 0) + pltpu.roll(beta_own, 1, 1) + pltpu.roll(beta_own, 127, 1)
    bound = jnp.max(shift_own + PLANE_SCALES[2] * (6.0 * beta_own + 1.5 * around))
    bound_y[0] = jnp.full((1, 128), bound, jnp.float32)

    spread(7, bound_y, over_y)
    send(1, coarse2, geo_coarse2, True)
    send(2, coarse3, geo_coarse3, True)

    wait(recv_sem, 0, tiles_of(geo_fields, 3))
    level1 = (masked1, wx1, wy1, wz1, diag1, inv1)
    prepare(
        level1, (lambda p: fields[1, p, pl.ds(12, 40), :], lambda p: fields[2, p, pl.ds(8, 48), :]), 48, 3, (4, 32), PLANE_SCALES[0]
    )

    def first_step(step, inv, value, rows):
        def body(p):
            step[p, pl.ds(12, rows), :] = FIRST * value(p) * inv[p, pl.ds(12, rows), :]

        return body

    def smooth(step, wx, wy, wz, inv, p, low, rows):
        part = off(step, wx, wy, wz, p, low, rows)
        return KEEP * step[p, pl.ds(low, rows), :] + SECOND * inv[p, pl.ds(low, rows), :] * part

    loop(1, 9, first_step(step1, inv1, lambda p: fields[0, p, pl.ds(12, 40), :], 40))

    def presmooth1(p):
        near1[p, pl.ds(12, 40), :] = smooth(step1, wx1, wy1, wz1, inv1, p, 12, 40)

    loop(2, 8, presmooth1)

    def residual(f, v, level, p, low, rows):
        _, wx, wy, wz, diag, _ = level
        value = f(p, low, rows) - diag[p, pl.ds(low, rows), :] * v[p, pl.ds(low, rows), :]
        return value + off(v, wx, wy, wz, p, low, rows)

    def source_at(p, low, rows):
        return fields[0, p, pl.ds(low, rows), :]

    def rhs2_at(p, low, rows):
        return rhs2[p, pl.ds(low, rows), :]

    def restrict1(q):
        both = residual(source_at, near1, level1, 3 + 2 * q, EDGE, 32) + residual(source_at, near1, level1, 4 + 2 * q, EDGE, 32)
        start1[q, pl.ds(EDGE, 32), :] = both
        rhs2[4 + q, pl.ds(EDGE, 16), :] = coarsen_rows(start1, q, 32)

    loop(0, 2, restrict1)
    send(3, rhs2, geo_rhs2, False)

    def keep1(p):
        iter1[p, pl.ds(EDGE, 32), :] = near1[p, pl.ds(EDGE, 32), :]

    loop(3, 7, keep1)
    send(4, iter1, geo_iter1, False)

    wait_spread(recv_sem, 7, bound_y, ny)
    few[0] = functools.reduce(jnp.maximum, [bound_y[n] for n in range(ny)])
    spread(8, few, few_x, range(1, 13))
    send(11, coarse3, geo_middle3, True)
    send(13, coarse3, geo_outer3, True)
    wait(recv_sem, 1, tiles_of(geo_coarse2, 2))
    level2 = (masked2, wx2, wy2, wz2, diag2, inv2)
    prepare(
        level2, (lambda p: coarse2[0, p, pl.ds(12, 24), :], lambda p: coarse2[1, p, pl.ds(8, 32), :]), 32, 4, (2, 16), PLANE_SCALES[1]
    )
    wait(recv_sem, 3, tiles_of(geo_rhs2, 1))
    loop(2, 8, first_step(step2, inv2, lambda p: rhs2_at(p, 12, 24), 24))

    def presmooth2(p):
        near2[p, pl.ds(12, 24), :] = smooth(step2, wx2, wy2, wz2, inv2, p, 12, 24)

    loop(3, 7, presmooth2)
    both = residual(rhs2_at, near2, level2, 4, EDGE, 16) + residual(rhs2_at, near2, level2, 5, EDGE, 16)
    start2[0, pl.ds(EDGE, 16), :] = both
    rhs3[7, pl.ds(EDGE, 8), :] = coarsen_rows(start2, 0, 16)
    send(5, rhs3, geo_rhs3, False)
    for p in (4, 5):
        iter2[p, pl.ds(EDGE, 16), :] = near2[p, pl.ds(EDGE, 16), :]
    send(6, iter2, geo_coarse2, False)

    wait_spread(recv_sem, 8, few, 13)
    more[0] = functools.reduce(jnp.maximum, [few[n] for n in range(13)])
    spread(12, more, more_x, range(1, 3))
    wait(recv_sem, 2, tiles_of(geo_coarse3, 2))
    wait(recv_sem, 11, tiles_of(geo_middle3, 2))
    wait(recv_sem, 13, tiles_of(geo_outer3, 2))
    wait_spread(recv_sem, 12, more, 3)
    scale = 2.0 / functools.reduce(jnp.maximum, [more[n] for n in range(3)])

    def clean3(p):
        ok = inside(p, 24, 8, 7, 15, 1, 8)
        masked3[p, pl.ds(8, 24), :] = jnp.where(ok, coarse3[1, p, pl.ds(8, 24), :], 0.0)

    loop(0, 15, clean3)
    wx3[0, pl.ds(8, 24), :] = (PLANE_SCALES[2] * scale) * (masked3[0, pl.ds(8, 24), :] + masked3[1, pl.ds(8, 24), :])

    def fill3(p):
        wxp, wyp, wzp, total = weights(masked3, p, 8, 24, PLANE_SCALES[2] * scale, VERTICAL * scale)
        total = total + 2.0 * scale * coarse3[0, p, pl.ds(8, 24), :]
        wx3[p, pl.ds(8, 24), :] = wxp
        wy3[p, pl.ds(8, 24), :] = wyp
        wz3[p, pl.ds(8, 24), :] = wzp
        ok = inside(p, 24, 8, 7, 15, 1, 8)
        own3[p, pl.ds(8, 24), :] = jnp.where(ok, total - 2.0, 0.0)
        inside3[p, pl.ds(8, 24), :] = jnp.where(ok, 1.0, 0.0)

    loop(1, 14, fill3)
    wait(recv_sem, 5, tiles_of(geo_rhs3, 1))

    def begin3(p):
        ok = inside(p, 24, 8, 7, 15, 1, 8)
        basis[0, p, pl.ds(8, 24), :] = jnp.where(ok, rhs3[p, pl.ds(8, 24), :], 0.0)

    loop(0, 15, begin3)

    def doubled(v, p, low, rows):
        value = own3[p, pl.ds(low, rows), :] * v[p, pl.ds(low, rows), :]
        return value - inside3[p, pl.ds(low, rows), :] * off(v, wx3, wy3, wz3, p, low, rows)

    for k in range(ITERS):
        low, rows, reach = (8, 24, 6 - k) if k < ITERS - 1 else (EDGE, 8, 0)

        def advance(p, k=k, low=low, rows=rows):
            value = doubled(basis.at[k], p, low, rows)
            value = 0.5 * value if k == 0 else value - basis[k - 1, p, pl.ds(low, rows), :]
            basis[k + 1, p, pl.ds(low, rows), :] = value

        loop(7 - reach, 8 + reach, advance)

    own = [basis[k, 7, pl.ds(EDGE, 8), :] for k in range(ITERS + 1)]
    parts = [halves(v) for v in own]
    for n, (i, j) in enumerate(PAIRS):
        high, low = two_prod(own[i], own[j], parts[i], parts[j])
        pair_high[pl.ds(8 * n, 8), :] = high
        pair_low[pl.ds(8 * n, 8), :] = low
    for n in range(len(PAIRS), ROWS):
        pair_high[pl.ds(8 * n, 8), :] = jnp.zeros((8, 128), jnp.float32)
        pair_low[pl.ds(8 * n, 8), :] = jnp.zeros((8, 128), jnp.float32)

    def merge(a, b):
        s, t = two_sum(a[0], b[0])
        return s, t + (a[1] + b[1])

    def tree(terms):
        while len(terms) > 1:
            terms = [merge(terms[i], terms[i + 1]) if i + 1 < len(terms) else terms[i] for i in range(0, len(terms), 2)]
        return terms[0]

    sums = tree([(pair_high[pl.ds(s, ROWS, stride=8), :], pair_low[pl.ds(s, ROWS, stride=8), :]) for s in range(8)])
    for d in (64, 32, 16, 8, 4, 2, 1):
        sums = merge(sums, (pltpu.roll(sums[0], d, 1), pltpu.roll(sums[1], d, 1)))
    lane, row = lane_of((ROWS, 128)), lax.broadcasted_iota(jnp.int32, (ROWS, 128), 0)
    line = jnp.where(lane == row, sums[0], jnp.where(lane == row + 64, sums[1], 0.0))
    gram_y[0] = jnp.sum(line, axis=0, keepdims=True)

    def total_of(ref, count):
        zero = jnp.zeros((1, 128), jnp.float32)
        s, t = tree([(ref[n], zero) for n in range(count)])
        return s + jnp.where(lane_of((1, 128)) >= 64, pltpu.roll(t, 64, 1), 0.0)

    sibling = gx + 1 - 2 * lax.rem(gx, 2)
    for column, y in [(n, dy) for _, dy in over_y + [(0, 0)] for n in (1, 0)]:
        if column or y:
            pltpu.make_async_remote_copy(
                src_ref=gram_y.at[0], dst_ref=gram_y.at[column * ny + y], send_sem=send_sem.at[9], recv_sem=recv_sem.at[9],
                device_id=(sibling if column else gx, device(0, y)[1]), device_id_type=MESH,
            ).start()
    def lift(k):
        start = isinstance(k, int)

        def prolong2(p):
            if start:
                value = iter2[p, pl.ds(12, 24), :]
            else:
                coarse = basis[k, 5 + p // 2, pl.ds(14, 12), :]
                start2[p, pl.ds(12, 12, stride=2), :] = coarse
                start2[p, pl.ds(13, 12, stride=2), :] = coarse
                value = start2[p, pl.ds(12, 24), :]
            start2[p, pl.ds(12, 24), :] = jnp.where(inside(p, 24, 12, 4, 10, 2, 16), value, 0.0)

        def zero(p, low, rows):
            return jnp.zeros((rows, 128), jnp.float32)

        loop(1, 9, prolong2)
        rhs = rhs2_at if start else zero
        loop(2, 8, first_step(step2, inv2, lambda p: residual(rhs, start2, level2, p, 12, 24), 24))

        def post2(p):
            sum2[p, pl.ds(12, 24), :] = start2[p, pl.ds(12, 24), :] + smooth(step2, wx2, wy2, wz2, inv2, p, 12, 24)

        loop(3, 7, post2)

        def prolong1(p):
            coarse = sum2[(p + 5) // 2, pl.ds(14, 20), :]
            start1[p, pl.ds(12, 20, stride=2), :] = coarse
            start1[p, pl.ds(13, 20, stride=2), :] = coarse
            value = start1[p, pl.ds(12, 40), :]
            if start:
                value = value + iter1[p, pl.ds(12, 40), :]
            start1[p, pl.ds(12, 40), :] = jnp.where(inside(p, 40, 12, 3, 10, 4, 32), value, 0.0)

        loop(1, 9, prolong1)
        side = source_at if start else zero
        loop(2, 8, first_step(step1, inv1, lambda p: residual(side, start1, level1, p, 12, 40), 40))

        def post1(p):
            lifted[k, p - 3] = start1[p, pl.ds(EDGE, 32), :] + smooth(step1, wx1, wy1, wz1, inv1, p, EDGE, 32)

        loop(3, 7, post1)

    def lift_some(low, high):
        def step(k, carry):
            lift(k)
            return carry

        lax.fori_loop(low, high, step, 0)

    wait(recv_sem, 4, tiles_of(geo_iter1, 1))
    wait(recv_sem, 6, tiles_of(geo_coarse2, 1))
    lift(ITERS)
    lift_some(0, SOON)
    wait_spread(recv_sem, 9, gram_y, 2 * ny)
    gram_x[0] = total_of(gram_y, 2 * ny)
    spread(10, gram_x, over_z, [n // 2 for n, _ in over_z])
    lift_some(SOON, ITERS)
    wait_spread(recv_sem, 10, gram_x, nx // 2)
    entries = jnp.broadcast_to(total_of(gram_x, nx // 2), (2 * ROWS, 128))
    lane, row = lane_of((2 * ROWS, 128)), lax.broadcasted_iota(jnp.int32, (2 * ROWS, 128), 0)
    place = jnp.where(row < ROWS, row, row + (64 - ROWS))
    column = jnp.sum(jnp.where(lane == place, entries, 0.0), axis=1, keepdims=True)
    scalars[...] = jnp.broadcast_to(column, (2 * ROWS, 128))

    def gram(i, j):
        n = SLOT[(min(i, j), max(i, j))]
        return scalars[pl.ds(n, 1), :], scalars[pl.ds(ROWS + n, 1), :]

    answer = [value * scale for value in gradient_coefficients(gram)]

    for p in range(4):
        total = lifted[ITERS, p]
        for k in range(ITERS):
            total = total + answer[k] * lifted[k, p]
        out[p] = total

    wait(send_sem, 0, tiles_of(geo_fields, 3))
    wait(send_sem, 1, tiles_of(geo_coarse2, 2))
    wait(send_sem, 2, tiles_of(geo_coarse3, 2))
    wait(send_sem, 11, tiles_of(geo_middle3, 2))
    wait(send_sem, 13, tiles_of(geo_outer3, 2))
    wait(send_sem, 3, tiles_of(geo_rhs2, 1))
    wait(send_sem, 4, tiles_of(geo_iter1, 1))
    wait(send_sem, 5, tiles_of(geo_rhs3, 1))
    wait(send_sem, 6, tiles_of(geo_coarse2, 1))
    wait_spread(send_sem, 7, bound_y, ny)
    wait_spread(send_sem, 8, few, 13)
    wait_spread(send_sem, 12, more, 3)
    wait_spread(send_sem, 9, gram_y, 2 * ny)
    wait_spread(send_sem, 10, gram_x, nx // 2)


def solution(mesh):
    nx, ny = mesh.shape["gx"], mesh.shape["gy"]

    def vmem(*shape):
        return pltpu.VMEM(shape, jnp.float32)

    one = [vmem(10, 64, 128)] * 10
    two = [vmem(10, 48, 128)] * 11
    three = [vmem(15, 40, 128)] * 6 + [vmem(ITERS + 1, 15, 40, 128), vmem(ITERS + 1, 4, 32, 128)]

    def on_device(source, beta, shift):
        return pl.pallas_call(
            functools.partial(kernel, (nx, ny)),
            out_shape=jax.ShapeDtypeStruct(source.shape, jnp.float32),
            in_specs=[pl.BlockSpec(memory_space=pl.ANY)] * 3,
            out_specs=pl.BlockSpec(memory_space=pltpu.VMEM),
            scratch_shapes=[
                vmem(3, 10, 64, 128), vmem(2, 10, 48, 128), vmem(2, 15, 40, 128), vmem(10, 48, 128), vmem(15, 40, 128),
                *one, *two, *three,
                vmem(8 * ROWS, 128), vmem(8 * ROWS, 128),
                vmem(ny, 1, 128), vmem(13, 1, 128), vmem(3, 1, 128), vmem(2 * ny, 1, 128), vmem(nx // 2, 1, 128),
                vmem(2 * ROWS, 128), vmem(140, 8, 128),
                pltpu.SemaphoreType.DMA((3,)), pltpu.SemaphoreType.DMA((15,)), pltpu.SemaphoreType.DMA((15,)),
            ],
            compiler_params=pltpu.CompilerParams(collective_id=0, has_side_effects=True, vmem_limit_bytes=40 * 2**20),
        )(*[pltpu.with_memory_space_constraint(x, pltpu.HBM) for x in (source, beta, shift)])

    placed = P("gx", "gy", None)
    return jax.shard_map(on_device, mesh=mesh, in_specs=(placed,) * 3, out_specs=placed, check_vma=False)
```
